32 devices in a mesh: patch: 8 (over z, y), sub: 4 (over x, core).
Axes of the slice: x: 2, y: 2, z: 4, core: 2. Of those that a mesh axis runs over, the one named last changes fastest.
Arguments:
- pieces_image: float32 [4, 256, 8, 256], P('sub', 'patch'), may hold values from -6 to 6
- pieces_variance: float32 [4, 256, 8, 256], P('sub', 'patch'), may hold values from 0.5 to 2
- piece_patch: int32 [4, 256, 1], P('sub', 'patch'), may hold values from 0 to 7; in each aligned block of 32 rows (0 to 31, 32 to 63, ..., all dimensions but the last counted through in order) at most 8 rows name the same one
- piece_cell: int32 [4, 256], P('sub', 'patch'), may hold values from 0 to 31
- stamp_row: int32 [8, 48], P('patch', 'sub'), may hold values from 0 to 63
- stamp_col: int32 [8, 48], P('patch', 'sub'), may hold values from 0 to 255
- stamp_count: int32 [8, 4], P('patch', 'sub'), may hold values from 2 to 12, as said below
- warp_offsets: int32 [4], replicated, may hold values from 0 to 8
Outputs:
- difference: float32 [4, 8, 256, 256], P(None, 'patch', 'sub')
- significance: float32 [4, 8, 256, 256], P(None, 'patch', 'sub')
The draws below stay inside these ranges and needn't reach their ends.
Inputs may be any that keep to these rules, and one draw needn't show every extreme that they name: `piece_patch`: the pieces of one device name the same patch at most 8 times, and in every draw some device names some patch exactly 8 times. `stamp_count`: stamps of a sub-tile whose index is this count or more are unused.
All inputs are finite; a program needn't handle non-finite values.
Results may differ from the reference program's by a relative error of at most 0.0003.
Values sent between devices are 32-bit elements; how exact they have to be, the bound alone decides.
No kernel may reach another device: no remote copies, remote signals or barrier semaphores. Data moves between devices by JAX's collectives and lax.ppermute only.
A program may use at most 64 MiB of HBM per device.

```python
import math
import jax
import jax.numpy as jnp
import numpy as np
from jax import lax

V = 4
NCELL = 8
RT = 64
CW = 256
NS = 12
NB = 40
KR = 10
PR = 10
SH = 15
WARP = 4
CR = 8
NP = 32
CAP = 8
N_PATCH = 8
N_SUB = 4


def draw_stamp_count(key, part):
    position = jnp.arange(N_SUB).astype(jnp.int32)
    lowest = jnp.maximum(position * NS // N_SUB + 1, 2)
    highest = (position + 1) * NS // N_SUB + 1
    return jax.random.randint(key, (N_PATCH, N_SUB), lowest[None, :], highest[None, :]).astype(jnp.int32)


def draw_stamp_row(key, part):
    first_key, second_key, third_key = jax.random.split(key, 3)
    reach = min(SH, RT)
    general = jax.random.randint(first_key, (N_PATCH, N_SUB, NS), 0, RT).astype(jnp.int32)
    near_top = jax.random.randint(second_key, (N_PATCH, N_SUB, 1), 0, reach).astype(jnp.int32)
    near_bottom = jax.random.randint(third_key, (N_PATCH, N_SUB, 1), RT - reach, RT).astype(jnp.int32)
    values = jnp.concatenate([near_top, near_bottom, general[:, :, 2:]], axis=2)
    return values.reshape(N_PATCH, N_SUB * NS)


def draw_warp_offsets(key, part):
    first_key, second_key = jax.random.split(key)
    middle = jax.random.randint(first_key, (V - 2,), 0, 2 * WARP + 1).astype(jnp.int32)
    values = jnp.concatenate([jnp.array([0, 2 * WARP], jnp.int32), middle])
    return values[jax.random.permutation(second_key, V)]


def set_ends(values, stream_key, least, top_value):
    shape = values.shape
    place = [jax.random.randint(jax.random.fold_in(stream_key, axis), (), 0, shape[axis]) for axis in range(len(shape))]
    values = values.at[tuple(place)].set(least)
    longest = shape.index(max(shape))
    place[longest] = (place[longest] + 1) % shape[longest]
    return values.at[tuple(place)].set(top_value)


def level_of(key, shape, shards, least, high):
    factor_of, own = 1.0, jax.random.fold_in(key, 6)
    for dim, shards_of in shards:
        heights = jnp.exp(jax.random.uniform(jax.random.fold_in(own, dim), (shards_of,), jnp.float32, least / len(shards), high / len(shards)))
        factor_of = factor_of * jnp.repeat(heights, shape[dim] // shards_of).reshape([-1 if axis == dim else 1 for axis in range(len(shape))])
    return factor_of


def deal_out(rng, own, number, rows, amount, top, bound, skew):
    order = jax.random.permutation(rng, amount)
    crowded, common = portions_of(amount, rows * top, bound, skew, True), portions_of(amount, rows * top, bound, skew, False)
    places = jnp.arange(amount)

    def named(sizes, rotation):
        used = int((sizes > 0).sum())
        fixed = max(1, used // 4)
        passed = fixed + (places - fixed + rotation * (used - fixed)) % max(1, amount - fixed)
        return jnp.zeros((amount,), jnp.int32).at[order[jnp.where(places < fixed, places, passed)]].set(jnp.asarray(sizes, jnp.int32))

    sizes = jnp.where(number % 4 == 0, named(crowded, number // 4), named(common, number - number // 4 - 1))
    mixed = jax.random.permutation(jax.random.fold_in(own, 3), amount)
    giver, taker = mixed[0:amount // 2 * 2:2], mixed[1:amount // 2 * 2:2]
    room = jnp.minimum(sizes[giver] - 1, bound - sizes[taker]) // 2
    room = jnp.where((giver == order[0]) | (taker == order[0]) | (sizes[taker] == 0), 0, jnp.maximum(room, 0))
    passed = jax.random.randint(jax.random.fold_in(own, 4), (amount // 2,), 0, 1 << 20) % (room + 1)
    sizes = sizes.at[giver].add(-passed).at[taker].add(passed)
    labels = jnp.searchsorted(jnp.cumsum(sizes), jnp.arange(rows * top), side="right").astype(jnp.int32)
    grid = labels.reshape(top, rows).T
    grid = grid[jax.random.permutation(jax.random.fold_in(own, 1), rows)]
    rotation = jax.random.randint(jax.random.fold_in(own, 2), (rows, 1), 0, top)
    return jnp.take_along_axis(grid, (jnp.arange(top)[None, :] + rotation) % top, axis=1)


def portions_of(count, total, limit, skew, full):
    loads = [(1 << 20) // math.isqrt(rank ** skew) + 1 for rank in range(1, count + 1)]
    largest = limit if full else min(limit, max(-(-total // count), total * loads[0] // sum(loads)))
    least = 1 if total - largest >= count - 1 else 0
    given, spare = [largest] + [least] * (count - 1), total - largest - least * (count - 1)
    while spare > 0:
        free = [i for i in range(1, count) if given[i] < largest] or [i for i in range(1, count) if given[i] < limit]
        mass, budget = sum([loads[i] for i in free]), spare
        for i in free:
            extra = min(limit - given[i], max(1, budget * loads[i] // mass), spare)
            given[i] = given[i] + extra
            spare = spare - extra
    return np.array(given)


def centred(rng, extent, deviation, most, cuts=(), kind=jnp.bfloat16):
    values = deviation * jax.random.normal(rng, extent, jnp.float32)
    if cuts:
        values = values * level_of(rng, extent, cuts, -0.22, 0.18)
    return jnp.clip(values, -most, most).astype(kind)


def setup_inputs(seed: int = 0) -> dict:
    seeds = jax.random.split(jax.random.key(seed), 9)
    pieces_image = centred(seeds[0], (N_SUB, NP * N_PATCH, CR, CW), 1.0, 6.0, ((0, 4), (1, 8)), jnp.float32)
    pieces_variance = jnp.clip(jnp.exp(math.log(2.0) - 1.3862944 * jax.random.uniform(seeds[1], (N_SUB, NP * N_PATCH, CR, CW), jnp.float32) ** level_of(seeds[1], (N_SUB, NP * N_PATCH, CR, CW), ((0, 4), (1, 8)), -0.2, 0.2)), 0.5, 2.0)
    piece_patch_keys = jax.random.split(jax.random.fold_in(seeds[2], 1), N_SUB * (NP * N_PATCH) // NP)
    piece_patch_turns = jax.random.permutation(jax.random.fold_in(seeds[2], 3), N_SUB * (NP * N_PATCH) // NP)
    piece_patch = jax.vmap(lambda own, number: deal_out(jax.random.fold_in(seeds[2], 2), own, number, NP, N_PATCH, 1, CAP, 2))(piece_patch_keys, piece_patch_turns).reshape((N_SUB, NP * N_PATCH, 1))
    piece_cell = set_ends(jax.random.randint(seeds[3], (N_SUB, NP * N_PATCH), 0, V * NCELL), jax.random.fold_in(seeds[3], 1), 0, (V * NCELL) - 1).astype(jnp.int32)
    stamp_row = draw_stamp_row(jax.random.fold_in(seeds[8], 71), 0)
    stamp_col = set_ends(jax.random.randint(seeds[5], (N_PATCH, N_SUB * NS), 0, CW), jax.random.fold_in(seeds[5], 1), 0, CW - 1).astype(jnp.int32)
    stamp_count = draw_stamp_count(jax.random.fold_in(seeds[8], 71), 0)
    warp_offsets = draw_warp_offsets(jax.random.fold_in(seeds[8], 71), 0)
    return dict(pieces_image=pieces_image, pieces_variance=pieces_variance, piece_patch=piece_patch, piece_cell=piece_cell, stamp_row=stamp_row, stamp_col=stamp_col, stamp_count=stamp_count, warp_offsets=warp_offsets)


SIGMAS = (0.75, 1.5, 3.0)
DEGREES = (4, 4, 3)
PSF_SIGMA = 2.0
SKY_VAR = 0.1
RIDGE = 0.5
EPS = 1e-05
HIGH = lax.Precision.HIGHEST

def hermite(degree, argument):
    previous = jnp.ones_like(argument)
    if degree == 0:
        return previous
    current = argument
    for term_no in range(1, degree):
        previous, current = (current, argument * current - term_no * previous)
    return current

def shapes_at(offset):
    result = []
    for spread, degree in zip(SIGMAS, DEGREES):
        scaled = offset / spread
        envelope = jnp.exp(-0.5 * scaled * scaled)
        for term_no in range(degree + 1):
            result.append(hermite(term_no, scaled) * envelope)
    return jnp.stack(result)

def basis_taps():
    offset = jnp.arange(-KR, KR + 1).astype(jnp.float32)
    unscaled = shapes_at(offset)
    return unscaled / jnp.sqrt(lax.optimization_barrier(jnp.sum(unscaled * unscaled, axis=1, keepdims=True)))

def psf_value(offset, power):
    support = jnp.arange(-PR, PR + 1).astype(jnp.float32)
    summed = jnp.sum(jnp.exp(-0.5 * (support / PSF_SIGMA) ** 2))
    return (jnp.exp(-0.5 * (offset / PSF_SIGMA) ** 2) / summed) ** power

def group_pairs():
    result = []
    first_tap = 0
    for degree in DEGREES:
        members = []
        for row_tap in range(degree + 1):
            for col_tap in range(degree + 1 - row_tap):
                members.append((first_tap + row_tap, first_tap + col_tap))
        result.append(members)
        first_tap += degree + 1
    return result

def filter_columns(image, filter_taps):
    radius = (filter_taps.shape[1] - 1) // 2
    col_count = image.shape[-1]
    padded = jnp.pad(image, [(0, 0)] * (image.ndim - 1) + [(radius, radius)])
    result = jnp.zeros((filter_taps.shape[0],) + image.shape, jnp.float32)
    expand = (-1,) + (1,) * image.ndim
    for tap_no in range(2 * radius + 1):
        result = result + filter_taps[:, tap_no].reshape(expand) * padded[..., tap_no:tap_no + col_count][None]
    return result

def filter_rows(image, filter_taps):
    radius = (filter_taps.shape[1] - 1) // 2
    row_count = image.shape[-2]
    padded = jnp.pad(image, [(0, 0)] * (image.ndim - 2) + [(radius, radius), (0, 0)])
    result = jnp.zeros((filter_taps.shape[0],) + image.shape, jnp.float32)
    expand = (-1,) + (1,) * image.ndim
    for tap_no in range(2 * radius + 1):
        result = result + filter_taps[:, tap_no].reshape(expand) * padded[..., tap_no:tap_no + row_count, :][None]
    return result

def solve_kernel(gram_matrix, right_side, normalizer):
    gram_matrix = gram_matrix / normalizer
    right_side = right_side / normalizer
    scaling = 1.0 / jnp.sqrt(jnp.diagonal(gram_matrix) + EPS)
    system = gram_matrix * scaling[:, None] * scaling[None, :] + RIDGE * jnp.eye(gram_matrix.shape[0], dtype=jnp.float32)
    factor = jnp.linalg.cholesky(system)
    return jax.scipy.linalg.cho_solve((factor, True), right_side * scaling) * scaling

def reference(pieces_image, pieces_variance, piece_patch, piece_cell, stamp_row, stamp_col, stamp_count, warp_offsets):
    slot_count = V * NCELL
    sub_index = jnp.arange(N_SUB).astype(jnp.int32)[:, None]
    segment = ((sub_index * N_PATCH + piece_patch[:, :, 0]) * slot_count + piece_cell).reshape(-1)
    segment_total = N_SUB * N_PATCH * slot_count
    piece_total = N_SUB * NP * N_PATCH
    image_sum = jax.ops.segment_sum(pieces_image.reshape(piece_total, CR * CW), segment, num_segments=segment_total)
    variance_sum = jax.ops.segment_sum(pieces_variance.reshape(piece_total, CR * CW), segment, num_segments=segment_total)
    row_count = N_SUB * RT

    def arrange(flat_sum):
        sectioned = flat_sum.reshape(N_SUB, N_PATCH, V, RT, CW).transpose(1, 2, 0, 3, 4)
        padded = jnp.pad(sectioned.reshape(N_PATCH, V, row_count, CW), ((0, 0), (0, 0), (0, 0), (WARP, WARP)))
        return jax.vmap(lambda visit_plane, offset: lax.dynamic_slice_in_dim(visit_plane, offset, CW, axis=2), in_axes=(1, 0), out_axes=1)(padded, warp_offsets)
    science_all = arrange(image_sum)
    variance_all = arrange(variance_sum)
    filter_taps = basis_taps()
    pairs = [pair for members in group_pairs() for pair in members]
    support = jnp.arange(-PR, PR + 1).astype(jnp.float32)
    psf_one = psf_value(support, 1)[None]
    psf_two = psf_value(support, 2)[None]
    normalizer = N_SUB * NS * (2 * SH + 1) ** 2

    def one_patch(inputs):
        science, variance, rows_here, cols_here, counts_here = inputs
        template = lax.optimization_barrier(jnp.sum(science, axis=0)) / V
        template_var = lax.optimization_barrier(jnp.sum(variance, axis=0)) / (V * V)
        filtered = filter_columns(template, filter_taps)
        design = jnp.stack([filter_rows(filtered[col_tap], filter_taps[row_tap:row_tap + 1])[0] for row_tap, col_tap in pairs] + [jnp.ones((row_count, CW), jnp.float32)]).reshape(NB + 1, row_count * CW)
        centre_rows = (jnp.arange(N_SUB).astype(jnp.int32)[:, None] * RT + rows_here.reshape(N_SUB, NS)).reshape(-1)
        live = (jnp.arange(NS).astype(jnp.int32)[None, :] < counts_here[:, None]).reshape(-1)
        row_in = ((jnp.abs(jnp.arange(row_count).astype(jnp.int32)[None, :] - centre_rows[:, None]) <= SH) & live[:, None]).astype(jnp.float32)
        col_in = (jnp.abs(jnp.arange(CW).astype(jnp.int32)[None, :] - cols_here[:, None]) <= SH).astype(jnp.float32)
        stamp_mask = jnp.minimum(jnp.dot(row_in.T.astype(jnp.float32), col_in.astype(jnp.float32), precision=HIGH, preferred_element_type=jnp.float32), 1.0)
        diff_list = []
        sig_list = []
        for visit_no in range(V):
            total_var = variance[visit_no] + template_var + SKY_VAR
            weight = (stamp_mask / total_var).reshape(-1)
            weighted = design * weight[None, :]
            gram_matrix = jnp.einsum('kp,lp->kl', weighted, design, precision=HIGH)
            right_side = jnp.einsum('kp,p->k', weighted, science[visit_no].reshape(-1), precision=HIGH)
            coefficients = solve_kernel(gram_matrix, right_side, normalizer)
            model = jnp.einsum('k,kp->p', coefficients, design, precision=HIGH).reshape(row_count, CW)
            difference = science[visit_no] - model
            numerator = filter_rows(filter_columns(difference / total_var, psf_one)[0], psf_one)[0]
            denominator = filter_rows(filter_columns(1.0 / total_var, psf_two)[0], psf_two)[0]
            diff_list.append(difference)
            sig_list.append(numerator / jnp.sqrt(denominator))
        return (jnp.stack(diff_list), jnp.stack(sig_list))
    diffs, sigs = lax.map(one_patch, (science_all, variance_all, stamp_row, stamp_col, stamp_count))
    return (diffs.transpose(1, 0, 2, 3), sigs.transpose(1, 0, 2, 3))
```

```python
import functools

import jax
import jax.numpy as jnp
import ml_dtypes
import numpy as np
from jax import lax
from jax.experimental import pallas as pl
from jax.experimental.pallas import tpu as pltpu
from jax.sharding import PartitionSpec as P

NCELL = 8
KR = 10
PR = 10
SH = 15
WARP = 4

SIGMAS = (0.75, 1.5, 3.0)
DEGREES = (4, 4, 3)
PSF_SIGMA = 2.0
SKY_VAR = 0.1
RIDGE = 0.5
EPS = 1e-05

F32 = jnp.float32
BF16 = jnp.bfloat16
LANES = 128
HALO = 24
EDGE = 16
BLOCK = 32
WINDOW = 64
VMEM_BYTES = 20 * 1024 * 1024

TILES = ((0, (0, 2)), (0, (1, 3, 4)), (1, (0, 2)), (1, (1, 3, 4)), (2, (0, 1, 3)), (2, (2,)))
SLOTS = 8 * len(TILES)
HALF = 64
TAP_FIRST = (0, DEGREES[0] + 1, DEGREES[0] + DEGREES[1] + 2)
TAP_COUNT = sum(DEGREES) + len(DEGREES)


def slot_table():
    result = {}
    for tile, (group, columns) in enumerate(TILES):
        slot = 8 * tile
        for column in columns:
            for row in range(DEGREES[group] + 1 - column):
                result[slot] = (TAP_FIRST[group] + row, TAP_FIRST[group] + column)
                slot += 1
    return result


SLOT_TAPS = slot_table()
ONE_SLOT = 8 * (len(TILES) - 1) + 2
SCI_SLOT = ONE_SLOT + 1
LIVE_SLOTS = sorted(SLOT_TAPS) + [ONE_SLOT]


def basis_taps():
    offset = np.arange(-KR, KR + 1, dtype=np.float64)
    rows = []
    for spread, degree in zip(SIGMAS, DEGREES):
        scaled = offset / spread
        envelope = np.exp(-0.5 * scaled * scaled)
        previous, current = np.zeros_like(scaled), np.ones_like(scaled)
        for term_no in range(degree + 1):
            rows.append(current * envelope)
            previous, current = current, scaled * current - term_no * previous
    taps = np.stack(rows)
    return taps / np.sqrt(np.sum(taps * taps, axis=1, keepdims=True))


def psf_taps():
    offset = np.arange(-PR, PR + 1, dtype=np.float64)
    values = np.exp(-0.5 * (offset / PSF_SIGMA) ** 2)
    return values / values.sum()


def band(taps, rows, columns, shift):
    radius = (taps.shape[-1] - 1) // 2
    offset = np.arange(columns)[None, :] - shift - np.arange(rows)[:, None]
    inside = np.abs(offset) <= radius
    return np.where(inside, taps[..., np.clip(offset + radius, 0, 2 * radius)], 0.0)


def halves(values):
    values = np.asarray(values, np.float32)
    high = values.astype(ml_dtypes.bfloat16)
    low = (values - high.astype(np.float32)).astype(ml_dtypes.bfloat16)
    return high, low


def tile_depth(tile, visits):
    depth = len(TILES[tile][1]) * WINDOW
    return depth + visits * BLOCK + 16 if tile == len(TILES) - 1 else depth


@functools.lru_cache(maxsize=None)
def constants(visits, row_count, col_count):
    taps = basis_taps()
    column_bands = np.stack([band(taps[t], col_count, col_count, 0).T for t in range(TAP_COUNT)])
    toeplitz = np.stack([band(taps[t], BLOCK, WINDOW, EDGE) for t in range(TAP_COUNT)])
    row_parts = []
    for tile, (group, columns) in enumerate(TILES):
        matrix = np.zeros((BLOCK, 8, tile_depth(tile, visits)))
        slot = 0
        for place, column in enumerate(columns):
            for row in range(DEGREES[group] + 1 - column):
                matrix[:, slot, place * WINDOW : (place + 1) * WINDOW] = toeplitz[TAP_FIRST[group] + row]
                slot += 1
        if tile == len(TILES) - 1:
            base = len(columns) * WINDOW
            for visit in range(visits):
                first = base + visit * BLOCK
                matrix[np.arange(BLOCK), slot + 1 + visit, first + np.arange(BLOCK)] = 1.0
            matrix[:, slot, base + visits * BLOCK] = 1.0
        row_parts.append(matrix.reshape(BLOCK * 8, -1))
    depth = col_count
    for tile, part in enumerate(row_parts):
        row_parts[tile] = np.pad(part, ((0, 0), (0, depth - part.shape[1])))
    design = np.stack(halves(np.concatenate([column_bands, np.stack(row_parts)])), axis=1)
    psf = psf_taps()
    filters = np.stack([half for power in (1, 2) for half in halves(band(psf**power, col_count, col_count, 0).T)])
    edges = np.stack(
        [half for power in (1, 2) for half in halves(band(psf**power, row_count, row_count + 2 * EDGE, EDGE))]
    )
    edges = np.pad(edges, ((0, 0), (0, 0), (0, -edges.shape[2] % LANES)))
    doubled = np.concatenate([toeplitz, toeplitz], axis=2).astype(np.float32)
    return design, filters, edges, doubled


def split(values):
    high = values.astype(BF16)
    return high, (values - high.astype(F32)).astype(BF16)


def mul(left, right):
    return jnp.dot(left, right, preferred_element_type=F32)


def mul3(left, right):
    return mul(left[0], right[0]) + mul(left[0], right[1]) + mul(left[1], right[0])


def mul_nt(left, right):
    return lax.dot_general(left, right, (((1,), (1,)), ((), ())), preferred_element_type=F32)


def fill(cfg, outs, source, chosen_ref, table_ref):
    patches, capacity = cfg
    me = lax.axis_index("patch")
    for block in range(patches):
        if len(outs) == 1:
            out, place, away = outs[0], block, block ^ me
        else:
            out, place, away = outs[block], 0, block
        for rank in range(capacity):
            piece = chosen_ref[away * capacity + rank]
            out[place, 2 * rank] = source[0, piece, :, :LANES]
            out[place, 2 * rank + 1] = source[0, piece, :, LANES:]
        if table_ref is not None:
            out[place, 2 * capacity] = jnp.broadcast_to(table_ref[pl.ds(away, 1), :], (8, LANES))


def start_copies(pairs, sems):
    copies = [pltpu.make_async_copy(source, place, sems.at[number]) for number, (source, place) in enumerate(pairs)]
    for copy in copies:
        copy.start()
    return copies


def pack_kernel(cfg, *refs):
    patches, capacity, pieces, blocks, slots = cfg
    sources, refs = refs[:7], refs[7:]
    outs, refs = refs[:blocks], refs[blocks:]
    stamp_out, warp_out, chosen_ref, table_ref, count_ref, *held = refs
    held, sems = held[:-1], held[-1]
    target_ref, cell_ref, row_ref, col_ref, live_ref, image_ref = held
    copies = start_copies(
        zip(sources, (target_ref, cell_ref, row_ref, col_ref, live_ref, image_ref, warp_out)), sems
    )
    me = lax.axis_index("patch")
    for entry in range(patches * capacity):
        chosen_ref[entry] = 0
    for entry in range(patches):
        count_ref[entry] = 0
    line = lax.broadcasted_iota(jnp.int32, table_ref.shape, 0)
    lane = lax.broadcasted_iota(jnp.int32, table_ref.shape, 1)
    copies[0].wait()
    copies[1].wait()
    table = jnp.full(table_ref.shape, -1.0, F32)
    for piece in range(pieces):
        away = target_ref[0, piece] ^ me
        rank = count_ref[away]
        count_ref[away] = rank + 1
        chosen_ref[away * capacity + rank] = piece
        value = cell_ref[0, piece].astype(F32)
        table = jnp.where((line == away) & (lane == rank), value, table)
    table_ref[...] = table
    for copy in copies[2:5]:
        copy.wait()
    live = lax.broadcasted_iota(jnp.int32, (1, slots), 1) < live_ref[0, 0]
    stamp_out[...] = jnp.zeros(stamp_out.shape, F32)
    stamp_out[0:1, :slots] = row_ref[...].astype(F32)
    stamp_out[1:2, :slots] = col_ref[...].astype(F32)
    stamp_out[2:3, :slots] = jnp.where(live, 1.0, 0.0)
    copies[5].wait()
    fill((patches, capacity), outs, image_ref, chosen_ref, table_ref)
    copies[6].wait()


def pack_more_kernel(cfg, chosen_ref, var_hbm, *refs):
    patches, capacity, blocks = cfg
    outs, (var_ref, sems) = refs[:blocks], refs[blocks:]
    (copy,) = start_copies([(var_hbm, var_ref)], sems)
    copy.wait()
    fill((patches, capacity), outs, var_ref, chosen_ref, None)


def assemble(cfg, blocks, cells_ref, total_ref, me):
    patches, capacity = cfg
    total_ref[...] = jnp.zeros(total_ref.shape, F32)
    for block in range(patches):
        if len(blocks) == 1:
            ref, place, away = blocks[0], block, block ^ me
        else:
            ref, place, away = blocks[block], 0, block
        for rank in range(capacity):
            cell = cells_ref[away * capacity + rank]
            total_ref[cell, 0] += ref[place, 2 * rank]
            total_ref[cell, 1] += ref[place, 2 * rank + 1]


def warped(total_ref, visit, warp_ref, row_count, col_count):
    first = visit * NCELL
    left = total_ref[first : first + NCELL, 0].reshape(row_count, LANES)
    right = total_ref[first : first + NCELL, 1].reshape(row_count, LANES)
    plane = jnp.concatenate([left, right], axis=1)
    offset = warp_ref[visit] - WARP
    moved = pltpu.roll(plane, lax.rem(col_count - offset, col_count), 1)
    source = lax.broadcasted_iota(jnp.int32, plane.shape, 1) + offset
    return jnp.where((source >= 0) & (source < col_count), moved, 0.0)


def image_kernel(cfg, warp_ref, stamp_ref, *refs):
    patches, capacity, visits, row_count, col_count, block_count = cfg
    blocks = refs[:block_count]
    sci_ref, up_ref, down_ref, cells_ref, total_ref, near_ref, sems = refs[block_count:]
    me = lax.axis_index("patch")
    copies = []
    for block in range(patches):
        ref, place = (blocks[0], block) if block_count == 1 else (blocks[block], 0)
        copies.append(
            pltpu.make_async_copy(
                ref.at[place, 2 * capacity, pl.ds(0, 1), :], near_ref.at[pl.ds(block, 1), :], sems.at[block]
            )
        )
    for copy in copies:
        copy.start()
    for copy in copies:
        copy.wait()
    for block in range(patches):
        away = block ^ me if block_count == 1 else block
        for rank in range(capacity):
            cell = near_ref[block, rank].astype(jnp.int32)
            cells_ref[away * capacity + rank] = jnp.where(cell < 0, visits * NCELL, cell)
    assemble((patches, capacity), blocks, cells_ref, total_ref, me)
    for visit in range(visits):
        plane = warped(total_ref, visit, warp_ref, row_count, col_count)
        sci_ref[visit] = plane
        up_ref[visit * HALO : (visit + 1) * HALO] = plane[:HALO]
        down_ref[visit * HALO : (visit + 1) * HALO] = plane[row_count - HALO :]
    first = visits * HALO
    for ref in (up_ref, down_ref):
        ref[first : first + 8, :LANES] = stamp_ref[...]
        ref[first : first + 8, LANES:] = jnp.zeros((8, col_count - LANES), F32)


def near_mask(stamps, shift, row_count, col_count):
    row_at = lax.broadcasted_iota(jnp.int32, (row_count, LANES), 0).astype(F32)
    col_at = lax.broadcasted_iota(jnp.int32, (col_count, LANES), 0).astype(F32)
    row_in = (jnp.abs(row_at - (stamps[0:1] + shift)) <= SH) & (stamps[2:3] > 0.5)
    col_in = jnp.abs(col_at - stamps[1:2]) <= SH
    return mul_nt(jnp.where(row_in, 1.0, 0.0).astype(BF16), jnp.where(col_in, 1.0, 0.0).astype(BF16))


def filter_columns(image, tap, held_ref):
    rows = image[0].shape[0]
    both = mul(jnp.concatenate(image, axis=0), held_ref[tap, 0])
    return split(both[:rows] + both[rows:] + mul(image[0], held_ref[tap, 1]))


def own_kernel(cfg, sci_ref, stamp_ref, fixed_ref, held_ref, high_ref, low_ref, hits_ref, sems):
    visits, row_count, col_count = cfg
    copies = start_copies([(fixed_ref.at[n], held_ref.at[n]) for n in range(TAP_COUNT + len(TILES))], sems)
    own = sci_ref[0]
    for visit in range(1, visits):
        own = own + sci_ref[visit]
    template = split(own * (1.0 / visits))
    hits_ref[...] = near_mask(stamp_ref[...], 0.0, row_count, col_count)
    for tap in range(TAP_COUNT):
        copies[tap].wait()
        high_ref[tap], low_ref[tap] = filter_columns(template, tap, held_ref)
    for copy in copies[TAP_COUNT:]:
        copy.wait()


def design_kernel(cfg, sci_ref, above_ref, below_ref, held_ref, own_high, own_low, hits_ref, *refs):
    visits, row_count, col_count = cfg
    design_ref, mask_ref, high_out, low_out, wide_out, high_ref, low_ref, wide_ref, sems = refs
    above = above_ref[0:HALO]
    below = below_ref[0:HALO]
    for visit in range(1, visits):
        above = above + above_ref[visit * HALO : (visit + 1) * HALO]
        below = below + below_ref[visit * HALO : (visit + 1) * HALO]
    rim = jnp.zeros((BLOCK - HALO, col_count), F32)
    template = split(jnp.concatenate([rim, above, below, rim], axis=0) * (1.0 / visits))
    for tap in range(TAP_COUNT):
        for ref, own, part in zip((high_ref, low_ref), (own_high, own_low), filter_columns(template, tap, held_ref)):
            ref[tap, :BLOCK] = part[:BLOCK]
            ref[tap, BLOCK : BLOCK + row_count] = own[tap]
            ref[tap, BLOCK + row_count :] = part[BLOCK:]
    for visit in range(visits):
        first = visit * HALO
        wide_ref[visit, :EDGE] = above_ref[first + HALO - EDGE : first + HALO]
        wide_ref[visit, EDGE : EDGE + row_count] = sci_ref[visit]
        wide_ref[visit, EDGE + row_count :] = below_ref[first : first + EDGE]
    copies = start_copies(((high_ref, high_out), (low_ref, low_out), (wide_ref, wide_out)), sems)
    for block in range(row_count // BLOCK):
        start = EDGE + block * BLOCK
        for tile, (group, columns) in enumerate(TILES):
            depth = tile_depth(tile, visits)
            rows = [held_ref[TAP_COUNT + tile, half, :, :depth] for half in range(2)]
            taps = [TAP_FIRST[group] + column for column in columns]
            high = [high_ref[tap, start : start + WINDOW] for tap in taps]
            low = [low_ref[tap, start : start + WINDOW] for tap in taps]
            if tile == len(TILES) - 1:
                for visit in range(visits):
                    pair = split(sci_ref[visit, block * BLOCK : (block + 1) * BLOCK])
                    high.append(pair[0])
                    low.append(pair[1])
                high.append(jnp.ones((16, col_count), BF16))
                low.append(jnp.zeros((16, col_count), BF16))
            both = mul(jnp.concatenate(rows, axis=0), jnp.concatenate(high, axis=0))
            part = both[: 8 * BLOCK] + both[8 * BLOCK :] + mul(rows[0], jnp.concatenate(low, axis=0))
            design_ref[block * BLOCK : (block + 1) * BLOCK, 8 * tile : 8 * tile + 8] = part.reshape(
                BLOCK, 8, col_count
            )
    first = visits * HALO
    hits = hits_ref[...]
    for ref, shift in ((above_ref, -row_count), (below_ref, row_count)):
        hits = hits + near_mask(ref[first : first + 8, :LANES], float(shift), row_count, col_count)
    mask_ref[...] = jnp.minimum(hits, 1.0)
    for copy in copies:
        copy.wait()


def gram_kernel(cfg, warp_ref, cells_ref, mask_ref, design_ref, *refs):
    patches, capacity, visits, row_count, col_count, block_count, step = cfg
    blocks = refs[:block_count]
    var_ref, down_ref, up_ref, gram_ref, total_ref, weight_ref, sum_ref = refs[block_count:]
    me = lax.axis_index("patch")
    assemble((patches, capacity), blocks, cells_ref, total_ref, me)
    shared = jnp.full((row_count, col_count), SKY_VAR, F32)
    for visit in range(visits):
        plane = warped(total_ref, visit, warp_ref, row_count, col_count)
        var_ref[visit] = plane
        shared = shared + plane * (1.0 / (visits * visits))
    mask = mask_ref[...]
    for visit in range(visits):
        weight_ref[visit] = mask / (var_ref[visit] + shared)
    sum_ref[...] = jnp.zeros(sum_ref.shape, F32)

    def body(number, carry):
        left, right = [], []
        for extra in range(step):
            row = number * step + extra
            design = design_ref[row]
            high, low = split(design)
            blank = jnp.zeros((HALF - SLOTS, col_count), BF16)
            right.append(jnp.concatenate([high, blank, low, blank], axis=0))
            scaled = [design * weight_ref[visit, pl.ds(row, 1), :] for visit in range(visits)]
            left.append(jnp.concatenate(split(jnp.concatenate(scaled, axis=0)), axis=0))
        sum_ref[...] += mul_nt(jnp.concatenate(left, axis=1), jnp.concatenate(right, axis=1))
        return carry

    lax.fori_loop(0, row_count // step, body, 0)
    lane = lax.broadcasted_iota(jnp.int32, (SLOTS, 2 * HALF), 1)
    both = []
    for visit in range(visits):
        first = visit * SLOTS
        second = (visits + visit) * SLOTS
        value = sum_ref[first : first + SLOTS] + sum_ref[second : second + SLOTS]
        both.append(value + pltpu.roll(value, HALF, 1))
    for pair in range(visits // 2):
        value = jnp.where(lane < HALF, both[2 * pair], both[2 * pair + 1])
        for ref in (gram_ref, down_ref, up_ref):
            ref[pair * SLOTS : (pair + 1) * SLOTS] = value
    first = visits // 2 * SLOTS
    for visit in range(visits):
        for part in range(col_count // LANES):
            place = first + (visit * (col_count // LANES) + part) * EDGE
            lanes = slice(part * LANES, (part + 1) * LANES)
            down_ref[place : place + EDGE] = var_ref[visit, row_count - EDGE :, lanes]
            up_ref[place : place + EDGE] = var_ref[visit, :EDGE, lanes]


def solve_kernel(cfg, var_ref, *refs):
    visits, row_count, col_count, subtiles, normalizer, gram_count = cfg
    grams = refs[:gram_count]
    fixed = refs[gram_count : gram_count + 6]
    diff_ref, sig_ref, *held, sems = refs[gram_count + 6 :]
    copies = start_copies(zip(fixed, held), sems)
    filter_ref, edge_ref, doubled_ref, wide_ref, high_ref, low_ref = held
    sub = lax.axis_index("sub")
    high_rows = row_count + 2 * EDGE
    parts = col_count // LANES
    first = visits // 2 * SLOTS

    def halo(ref, visit):
        pieces = [ref[first + (visit * parts + part) * EDGE :][:EDGE] for part in range(parts)]
        return jnp.concatenate(pieces, axis=1)

    from_above, from_below = grams[1], grams[-1]
    row_at = lax.broadcasted_iota(jnp.int32, (high_rows, col_count), 0) + sub * row_count - EDGE
    inside = (row_at >= 0) & (row_at < subtiles * row_count)
    spread = [
        jnp.concatenate([halo(from_above, visit), var_ref[visit], halo(from_below, visit)], axis=0)
        for visit in range(visits)
    ]
    shared = jnp.full((high_rows, col_count), SKY_VAR, F32)
    for visit in range(visits):
        shared = shared + spread[visit] * (1.0 / (visits * visits))
    inverse = [jnp.where(inside, 1.0 / (spread[visit] + shared), 0.0) for visit in range(visits)]

    def detected(images, kind):
        filtered = mul3(split(jnp.concatenate(images, axis=0)), (filter_ref[kind], filter_ref[kind + 1]))
        pair = split(filtered)
        rows = (edge_ref[kind, :, :high_rows], edge_ref[kind + 1, :, :high_rows])
        return [
            mul3(rows, (pair[0][v * high_rows : (v + 1) * high_rows], pair[1][v * high_rows : (v + 1) * high_rows]))
            for v in range(visits)
        ]

    for copy in copies[:3]:
        copy.wait()
    noise = detected(inverse, 2)

    lane = lax.broadcasted_iota(jnp.int32, (SLOTS, 2 * HALF), 1)
    line = lax.broadcasted_iota(jnp.int32, (SLOTS, 2 * HALF), 0)
    systems = []
    for pair in range(visits // 2):
        total = grams[0][pair * SLOTS : (pair + 1) * SLOTS]
        for ref in grams[1:]:
            total = total + ref[pair * SLOTS : (pair + 1) * SLOTS]
        diagonal = (lane == line) | (lane == line + HALF)
        systems.append(total + jnp.where(diagonal, RIDGE * total + RIDGE * EPS * normalizer, 0.0))
    for slot in LIVE_SLOTS:
        place = jnp.where(lane < HALF, slot, HALF + slot)
        for pair in range(visits // 2):
            matrix = systems[pair]
            column = jnp.take_along_axis(matrix, place, axis=1)
            row = matrix[slot : slot + 1] / column[slot : slot + 1]
            systems[pair] = jnp.where(line == slot, row, matrix - column * row)
    for copy in copies[3:]:
        copy.wait()
    left = []
    offsets = []
    half_lane = lax.broadcasted_iota(jnp.int32, (BLOCK, 2 * HALF), 1) < HALF
    for pair in range(visits // 2):
        wanted = SCI_SLOT + 2 * pair
        place = jnp.where(lane < HALF, wanted, HALF + wanted + 1)
        solved = jnp.take_along_axis(systems[pair], place, axis=1)
        mixes = [None] * TAP_COUNT
        for slot, (row_tap, col_tap) in SLOT_TAPS.items():
            term = solved[slot : slot + 1] * doubled_ref[row_tap]
            mixes[col_tap] = term if mixes[col_tap] is None else mixes[col_tap] + term
        own, other = [], []
        for tap in range(0, TAP_COUNT, 2):
            own.append(jnp.where(half_lane, mixes[tap], pltpu.roll(mixes[tap + 1], HALF, 1)))
            other.append(jnp.where(half_lane, pltpu.roll(mixes[tap], HALF, 1), mixes[tap + 1]))
        left += [jnp.concatenate(own, axis=1), jnp.concatenate(other, axis=1)]
        tail = solved[ONE_SLOT // 8 * 8 : ONE_SLOT // 8 * 8 + 8]
        for begin in (0, HALF):
            flat = jnp.take_along_axis(tail, jnp.full((8, LANES), begin, jnp.int32), axis=1)
            flat = flat[ONE_SLOT % 8 : ONE_SLOT % 8 + 1]
            offsets.append(jnp.concatenate([flat] * parts, axis=1))
    left = split(jnp.concatenate(left, axis=0))
    models = []
    for block in range(high_rows // BLOCK):
        start = block * BLOCK
        stack = tuple(
            jnp.concatenate([ref[tap, start : start + WINDOW] for tap in range(TAP_COUNT)], axis=0)
            for ref in (high_ref, low_ref)
        )
        models.append(mul3(left, stack))
    weighted = []
    for visit in range(visits):
        model = jnp.concatenate([part[visit * BLOCK : (visit + 1) * BLOCK] for part in models], axis=0)
        difference = wide_ref[visit] - model - offsets[visit]
        diff_ref[visit, 0] = difference[EDGE : EDGE + row_count]
        weighted.append(difference * inverse[visit])
    signal = detected(weighted, 0)
    for visit in range(visits):
        sig_ref[visit, 0] = signal[visit] * lax.rsqrt(noise[visit])


def vmem():
    return pl.BlockSpec(memory_space=pltpu.VMEM)


def smem():
    return pl.BlockSpec(memory_space=pltpu.SMEM)


def far():
    return pl.BlockSpec(memory_space=pltpu.HBM)


def in_hbm(array):
    return pltpu.with_memory_space_constraint(jnp.asarray(array), pltpu.HBM)


def call(kernel, outs, out_specs, in_specs, scratch):
    return pl.pallas_call(
        kernel,
        out_shape=outs,
        in_specs=in_specs,
        out_specs=out_specs,
        scratch_shapes=scratch,
        compiler_params=pltpu.CompilerParams(vmem_limit_bytes=VMEM_BYTES),
    )


def local(
    pieces_image,
    pieces_variance,
    piece_patch,
    piece_cell,
    stamp_row,
    stamp_col,
    stamp_count,
    warp_offsets,
):
    patches = lax.axis_size("patch")
    subtiles = lax.axis_size("sub")
    _, pieces, cell_rows, col_count = pieces_image.shape
    visits = warp_offsets.shape[0]
    row_count = cell_rows * NCELL
    slots = stamp_row.shape[1]
    capacity = max(2, 2 * pieces // patches)
    direct = patches <= 8
    units = 2 * capacity
    sds = jax.ShapeDtypeStruct
    design_fixed, filters, edges, doubled = constants(visits, row_count, col_count)

    image_blocks = var_blocks = 1

    def sent(blocks, depth):
        return [sds((1 if blocks > 1 else patches, depth, 8, LANES), F32)] * blocks

    *images, stamps, warps, chosen = call(
        functools.partial(pack_kernel, (patches, capacity, pieces, image_blocks, slots)),
        sent(image_blocks, units + 1)
        + [sds((8, LANES), F32), sds((visits,), jnp.int32), sds((patches * capacity,), jnp.int32)],
        [vmem()] * (image_blocks + 1) + [smem()] * 2,
        [far()] * 7,
        [
            pltpu.VMEM((-(-patches // 8) * 8, LANES), F32),
            pltpu.SMEM((patches,), jnp.int32),
            pltpu.SMEM((1, pieces), jnp.int32),
            pltpu.SMEM((1, pieces), jnp.int32),
            pltpu.VMEM((1, slots), jnp.int32),
            pltpu.VMEM((1, slots), jnp.int32),
            pltpu.SMEM((1, 1), jnp.int32),
            pltpu.VMEM(pieces_image.shape, F32),
            pltpu.SemaphoreType.DMA((7,)),
        ],
    )(
        in_hbm(piece_patch[:, :, 0]),
        in_hbm(piece_cell),
        in_hbm(stamp_row),
        in_hbm(stamp_col),
        stamp_count,
        in_hbm(pieces_image),
        in_hbm(warp_offsets),
    )

    def route(blocks, order):
        if len(blocks) == 1:
            return [lax.all_to_all(blocks[0], "patch", split_axis=0, concat_axis=0, tiled=True)]
        result = [blocks[0]] * patches
        for away in order:
            result[away] = lax.ppermute(blocks[away], "patch", [(i, i ^ away) for i in range(patches)])
        return result

    got = route(images, list(range(patches - 1, 0, -1)))
    variances = call(
        functools.partial(pack_more_kernel, (patches, capacity, var_blocks)),
        sent(var_blocks, units),
        [vmem()] * var_blocks,
        [smem(), far()],
        [pltpu.VMEM(pieces_image.shape, F32), pltpu.SemaphoreType.DMA((1,))],
    )(chosen, in_hbm(pieces_variance))
    got_var = route(variances, range(1, patches))

    side = sds((visits * HALO + 8, col_count), F32)
    science, up, down, cells = call(
        functools.partial(image_kernel, (patches, capacity, visits, row_count, col_count, image_blocks)),
        [sds((visits, row_count, col_count), F32), side, side, sds((patches * capacity,), jnp.int32)],
        [vmem(), vmem(), vmem(), smem()],
        [smem()] + [vmem()] * (1 + image_blocks),
        [
            pltpu.VMEM((visits * NCELL + 1, 2, 8, LANES), F32),
            pltpu.SMEM((patches, LANES), F32),
            pltpu.SemaphoreType.DMA((patches,)),
        ],
    )(warps, stamps, *got)
    above = lax.ppermute(down, "sub", [(i, i + 1) for i in range(subtiles - 1)])
    below = lax.ppermute(up, "sub", [(i + 1, i) for i in range(subtiles - 1)])

    field = sds((TAP_COUNT, row_count + 2 * BLOCK, col_count), BF16)
    own_field = sds((TAP_COUNT, row_count, col_count), BF16)
    plane = sds((row_count, col_count), F32)
    wide = sds((visits, row_count + 2 * EDGE, col_count), F32)
    held, own_high, own_low, hits = call(
        functools.partial(own_kernel, (visits, row_count, col_count)),
        [sds(design_fixed.shape, BF16), own_field, own_field, plane],
        [vmem()] * 4,
        [vmem(), vmem(), far()],
        [pltpu.SemaphoreType.DMA((design_fixed.shape[0],))],
    )(science, stamps, in_hbm(design_fixed))
    design, mask, high, low, wide_science = call(
        functools.partial(design_kernel, (visits, row_count, col_count)),
        [sds((row_count, SLOTS, col_count), F32), plane] + [pltpu.HBM(part.shape, part.dtype) for part in (field, field, wide)],
        [vmem()] * 2 + [far()] * 3,
        [vmem()] * 7,
        [pltpu.VMEM(part.shape, part.dtype) for part in (field, field, wide)] + [pltpu.SemaphoreType.DMA((3,))],
    )(science, above, below, held, own_high, own_low, hits)

    gram_rows = visits // 2 * SLOTS
    tail_rows = visits * EDGE * (col_count // LANES)
    step = 32
    variance, to_below, to_above, gram = call(
        functools.partial(gram_kernel, (patches, capacity, visits, row_count, col_count, var_blocks, step)),
        [
            sds((visits, row_count, col_count), F32),
            sds((gram_rows + tail_rows, LANES), F32),
            sds((gram_rows + tail_rows, LANES), F32),
            sds((gram_rows, LANES), F32),
        ],
        [vmem()] * 4,
        [smem(), smem(), vmem(), vmem()] + [vmem()] * var_blocks,
        [
            pltpu.VMEM((visits * NCELL + 1, 2, 8, LANES), F32),
            pltpu.VMEM((visits, row_count, col_count), F32),
            pltpu.VMEM((2 * visits * SLOTS, 2 * HALF), F32),
        ],
    )(warps, cells, mask, design, *got_var)
    grams = [gram]
    for shift in range(1, subtiles):
        sent = to_below if shift == 1 else to_above if shift == subtiles - 1 else gram
        grams.append(lax.ppermute(sent, "sub", [(i, (i + shift) % subtiles) for i in range(subtiles)]))

    normalizer = subtiles * slots * (2 * SH + 1) ** 2
    result = sds((visits, 1, row_count, col_count), F32)
    kept = [filters, edges, doubled, wide_science, high, low]
    return call(
        functools.partial(solve_kernel, (visits, row_count, col_count, subtiles, float(normalizer), len(grams))),
        [result, result],
        [vmem(), vmem()],
        [vmem()] * (1 + len(grams)) + [far()] * len(kept),
        [pltpu.VMEM(part.shape, part.dtype) for part in kept] + [pltpu.SemaphoreType.DMA((len(kept),))],
    )(variance, *grams, *[in_hbm(part) for part in kept])


def solution(mesh):
    in_specs = (
        P("sub", "patch", None, None),
        P("sub", "patch", None, None),
        P("sub", "patch", None),
        P("sub", "patch"),
        P("patch", "sub"),
        P("patch", "sub"),
        P("patch", "sub"),
        P(),
    )
    out_specs = (P(None, "patch", "sub", None), P(None, "patch", "sub", None))
    return jax.shard_map(local, mesh=mesh, in_specs=in_specs, out_specs=out_specs, check_vma=False)
```

```python
import functools

import jax
import jax.numpy as jnp
import ml_dtypes
import numpy as np
from jax import lax
from jax.experimental import pallas as pl
from jax.experimental.pallas import tpu as pltpu
from jax.sharding import PartitionSpec as P

NCELL = 8
KR = 10
PR = 10
SH = 15
WARP = 4

SIGMAS = (0.75, 1.5, 3.0)
DEGREES = (4, 4, 3)
PSF_SIGMA = 2.0
SKY_VAR = 0.1
RIDGE = 0.5
EPS = 1e-05

F32 = jnp.float32
BF16 = jnp.bfloat16
LANES = 128
HALO = 24
EDGE = 16
BLOCK = 32
WINDOW = 64
VMEM_BYTES = 20 * 1024 * 1024

TILES = ((0, (0, 2)), (0, (1, 3, 4)), (1, (0, 2)), (1, (1, 3, 4)), (2, (0, 1, 3)), (2, (2,)))
SLOTS = 8 * len(TILES)
HALF = 64
TAP_FIRST = (0, DEGREES[0] + 1, DEGREES[0] + DEGREES[1] + 2)
TAP_COUNT = sum(DEGREES) + len(DEGREES)


def slot_table():
    result = {}
    for tile, (group, columns) in enumerate(TILES):
        slot = 8 * tile
        for column in columns:
            for row in range(DEGREES[group] + 1 - column):
                result[slot] = (TAP_FIRST[group] + row, TAP_FIRST[group] + column)
                slot += 1
    return result


SLOT_TAPS = slot_table()
ONE_SLOT = 8 * (len(TILES) - 1) + 2
SCI_SLOT = ONE_SLOT + 1
LIVE_SLOTS = sorted(SLOT_TAPS) + [ONE_SLOT]


def basis_taps():
    offset = np.arange(-KR, KR + 1, dtype=np.float64)
    rows = []
    for spread, degree in zip(SIGMAS, DEGREES):
        scaled = offset / spread
        envelope = np.exp(-0.5 * scaled * scaled)
        previous, current = np.zeros_like(scaled), np.ones_like(scaled)
        for term_no in range(degree + 1):
            rows.append(current * envelope)
            previous, current = current, scaled * current - term_no * previous
    taps = np.stack(rows)
    return taps / np.sqrt(np.sum(taps * taps, axis=1, keepdims=True))


def psf_taps():
    offset = np.arange(-PR, PR + 1, dtype=np.float64)
    values = np.exp(-0.5 * (offset / PSF_SIGMA) ** 2)
    return values / values.sum()


def band(taps, rows, columns, shift):
    radius = (taps.shape[-1] - 1) // 2
    offset = np.arange(columns)[None, :] - shift - np.arange(rows)[:, None]
    inside = np.abs(offset) <= radius
    return np.where(inside, taps[..., np.clip(offset + radius, 0, 2 * radius)], 0.0)


def halves(values):
    values = np.asarray(values, np.float32)
    high = values.astype(ml_dtypes.bfloat16)
    low = (values - high.astype(np.float32)).astype(ml_dtypes.bfloat16)
    return high, low


def tile_depth(tile, visits):
    depth = len(TILES[tile][1]) * WINDOW
    return depth + visits * BLOCK + 16 if tile == len(TILES) - 1 else depth


@functools.lru_cache(maxsize=None)
def constants(visits, row_count, col_count):
    taps = basis_taps()
    column_bands = np.stack([band(taps[t], col_count, col_count, 0).T for t in range(TAP_COUNT)])
    toeplitz = np.stack([band(taps[t], BLOCK, WINDOW, EDGE) for t in range(TAP_COUNT)])
    row_parts = []
    for tile, (group, columns) in enumerate(TILES):
        matrix = np.zeros((BLOCK, 8, tile_depth(tile, visits)))
        slot = 0
        for place, column in enumerate(columns):
            for row in range(DEGREES[group] + 1 - column):
                matrix[:, slot, place * WINDOW : (place + 1) * WINDOW] = toeplitz[TAP_FIRST[group] + row]
                slot += 1
        if tile == len(TILES) - 1:
            base = len(columns) * WINDOW
            for visit in range(visits):
                first = base + visit * BLOCK
                matrix[np.arange(BLOCK), slot + 1 + visit, first + np.arange(BLOCK)] = 1.0
            matrix[:, slot, base + visits * BLOCK] = 1.0
        row_parts.append(matrix.reshape(BLOCK * 8, -1))
    depth = col_count
    for tile, part in enumerate(row_parts):
        row_parts[tile] = np.pad(part, ((0, 0), (0, depth - part.shape[1])))
    design = np.stack(halves(np.concatenate([column_bands, np.stack(row_parts)])), axis=1)
    psf = psf_taps()
    filters = np.stack([half for power in (1, 2) for half in halves(band(psf**power, col_count, col_count, 0).T)])
    edges = np.stack(
        [half for power in (1, 2) for half in halves(band(psf**power, row_count, row_count + 2 * EDGE, EDGE))]
    )
    edges = np.pad(edges, ((0, 0), (0, 0), (0, -edges.shape[2] % LANES)))
    doubled = np.concatenate([toeplitz, toeplitz], axis=2).astype(np.float32)
    return design, filters, edges, doubled


def split(values):
    high = values.astype(BF16)
    return high, (values - high.astype(F32)).astype(BF16)


def mul(left, right):
    return jnp.dot(left, right, preferred_element_type=F32)


def mul3(left, right):
    return mul(left[0], right[0]) + mul(left[0], right[1]) + mul(left[1], right[0])


def mul_nt(left, right):
    return lax.dot_general(left, right, (((1,), (1,)), ((), ())), preferred_element_type=F32)


def turn(patches):
    near, far_half = list(range(1, patches // 2)), list(range(patches // 2, patches))
    return [0, *near[:2], *far_half, *near[2:]]


def fill(cfg, outs, source, chosen_ref, table_ref):
    patches, capacity = cfg
    me = lax.axis_index("patch")
    for block in range(patches):
        if len(outs) == 1:
            out, place, away = outs[0], block, block ^ me
        else:
            out, place, away = outs[block], 0, turn(patches)[block]
        for rank in range(capacity):
            piece = chosen_ref[away * capacity + rank]
            out[place, 2 * rank] = source[0, piece, :, :LANES]
            out[place, 2 * rank + 1] = source[0, piece, :, LANES:]
        if table_ref is not None:
            out[place, 2 * capacity] = jnp.broadcast_to(table_ref[pl.ds(away, 1), :], (8, LANES))


def start_copies(pairs, sems):
    copies = [pltpu.make_async_copy(source, place, sems.at[number]) for number, (source, place) in enumerate(pairs)]
    for copy in copies:
        copy.start()
    return copies


def pack_kernel(cfg, *refs):
    patches, capacity, pieces, blocks, slots = cfg
    sources, refs = refs[:7], refs[7:]
    outs, refs = refs[:blocks], refs[blocks:]
    stamp_out, warp_out, chosen_ref, table_ref, count_ref, *held = refs
    held, sems = held[:-1], held[-1]
    target_ref, cell_ref, row_ref, col_ref, live_ref, image_ref = held
    copies = start_copies(
        zip(sources, (target_ref, cell_ref, row_ref, col_ref, live_ref, image_ref, warp_out)), sems
    )
    me = lax.axis_index("patch")
    for entry in range(patches * capacity):
        chosen_ref[entry] = 0
    for entry in range(patches):
        count_ref[entry] = 0
    line = lax.broadcasted_iota(jnp.int32, table_ref.shape, 0)
    lane = lax.broadcasted_iota(jnp.int32, table_ref.shape, 1)
    copies[0].wait()
    copies[1].wait()
    table = jnp.full(table_ref.shape, -1.0, F32)
    for piece in range(pieces):
        away = target_ref[0, piece] ^ me
        rank = count_ref[away]
        count_ref[away] = rank + 1
        chosen_ref[away * capacity + rank] = piece
        value = cell_ref[0, piece].astype(F32)
        table = jnp.where((line == away) & (lane == rank), value, table)
    table_ref[...] = table
    for copy in copies[2:5]:
        copy.wait()
    live = lax.broadcasted_iota(jnp.int32, (1, slots), 1) < live_ref[0, 0]
    stamp_out[...] = jnp.zeros(stamp_out.shape, F32)
    stamp_out[0:1, :slots] = row_ref[...].astype(F32)
    stamp_out[1:2, :slots] = col_ref[...].astype(F32)
    stamp_out[2:3, :slots] = jnp.where(live, 1.0, 0.0)
    copies[5].wait()
    fill((patches, capacity), outs, image_ref, chosen_ref, table_ref)
    copies[6].wait()


def pack_more_kernel(cfg, chosen_ref, var_hbm, *refs):
    patches, capacity, blocks = cfg
    outs, (var_ref, sems) = refs[:blocks], refs[blocks:]
    (copy,) = start_copies([(var_hbm, var_ref)], sems)
    copy.wait()
    fill((patches, capacity), outs, var_ref, chosen_ref, None)


def assemble(cfg, blocks, cells_ref, total_ref, me):
    patches, capacity = cfg
    total_ref[...] = jnp.zeros(total_ref.shape, F32)
    for block in range(patches):
        if len(blocks) == 1:
            ref, place, away = blocks[0], block, block ^ me
        else:
            ref, place, away = blocks[block], 0, turn(patches)[block]
        for rank in range(capacity):
            cell = cells_ref[away * capacity + rank]
            total_ref[cell, 0] += ref[place, 2 * rank]
            total_ref[cell, 1] += ref[place, 2 * rank + 1]


def warped(total_ref, visit, warp_ref, row_count, col_count):
    first = visit * NCELL
    left = total_ref[first : first + NCELL, 0].reshape(row_count, LANES)
    right = total_ref[first : first + NCELL, 1].reshape(row_count, LANES)
    plane = jnp.concatenate([left, right], axis=1)
    offset = warp_ref[visit] - WARP
    moved = pltpu.roll(plane, lax.rem(col_count - offset, col_count), 1)
    source = lax.broadcasted_iota(jnp.int32, plane.shape, 1) + offset
    return jnp.where((source >= 0) & (source < col_count), moved, 0.0)


def image_kernel(cfg, warp_ref, stamp_ref, *refs):
    patches, capacity, visits, row_count, col_count, block_count = cfg
    blocks = refs[:block_count]
    sci_ref, up_ref, down_ref, cells_ref, total_ref, near_ref, sems = refs[block_count:]
    me = lax.axis_index("patch")
    copies = []
    for block in range(patches):
        ref, place = (blocks[0], block) if block_count == 1 else (blocks[block], 0)
        copies.append(
            pltpu.make_async_copy(
                ref.at[place, 2 * capacity, pl.ds(0, 1), :], near_ref.at[pl.ds(block, 1), :], sems.at[block]
            )
        )
    for copy in copies:
        copy.start()
    for copy in copies:
        copy.wait()
    for block in range(patches):
        away = block ^ me if block_count == 1 else turn(patches)[block]
        for rank in range(capacity):
            cell = near_ref[block, rank].astype(jnp.int32)
            cells_ref[away * capacity + rank] = jnp.where(cell < 0, visits * NCELL, cell)
    assemble((patches, capacity), blocks, cells_ref, total_ref, me)
    for visit in range(visits):
        plane = warped(total_ref, visit, warp_ref, row_count, col_count)
        sci_ref[visit] = plane
        up_ref[visit * HALO : (visit + 1) * HALO] = plane[:HALO]
        down_ref[visit * HALO : (visit + 1) * HALO] = plane[row_count - HALO :]
    first = visits * HALO
    for ref in (up_ref, down_ref):
        ref[first : first + 8, :LANES] = stamp_ref[...]
        ref[first : first + 8, LANES:] = jnp.zeros((8, col_count - LANES), F32)


def near_mask(stamps, shift, row_count, col_count):
    row_at = lax.broadcasted_iota(jnp.int32, (row_count, LANES), 0).astype(F32)
    col_at = lax.broadcasted_iota(jnp.int32, (col_count, LANES), 0).astype(F32)
    row_in = (jnp.abs(row_at - (stamps[0:1] + shift)) <= SH) & (stamps[2:3] > 0.5)
    col_in = jnp.abs(col_at - stamps[1:2]) <= SH
    return mul_nt(jnp.where(row_in, 1.0, 0.0).astype(BF16), jnp.where(col_in, 1.0, 0.0).astype(BF16))


def filter_columns(image, tap, held_ref):
    rows = image[0].shape[0]
    both = mul(jnp.concatenate(image, axis=0), held_ref[tap, 0])
    return split(both[:rows] + both[rows:] + mul(image[0], held_ref[tap, 1]))


def own_kernel(cfg, sci_ref, stamp_ref, fixed_ref, held_ref, high_ref, low_ref, hits_ref, sems):
    visits, row_count, col_count = cfg
    copies = start_copies([(fixed_ref.at[n], held_ref.at[n]) for n in range(TAP_COUNT + len(TILES))], sems)
    own = sci_ref[0]
    for visit in range(1, visits):
        own = own + sci_ref[visit]
    template = split(own * (1.0 / visits))
    hits_ref[...] = near_mask(stamp_ref[...], 0.0, row_count, col_count)
    for tap in range(TAP_COUNT):
        copies[tap].wait()
        high_ref[tap], low_ref[tap] = filter_columns(template, tap, held_ref)
    for copy in copies[TAP_COUNT:]:
        copy.wait()


def design_kernel(cfg, sci_ref, above_ref, below_ref, held_ref, own_high, own_low, hits_ref, *refs):
    visits, row_count, col_count = cfg
    design_ref, mask_ref, high_out, low_out, wide_out, high_ref, low_ref, wide_ref, sems = refs
    above = above_ref[0:HALO]
    below = below_ref[0:HALO]
    for visit in range(1, visits):
        above = above + above_ref[visit * HALO : (visit + 1) * HALO]
        below = below + below_ref[visit * HALO : (visit + 1) * HALO]
    rim = jnp.zeros((BLOCK - HALO, col_count), F32)
    template = split(jnp.concatenate([rim, above, below, rim], axis=0) * (1.0 / visits))
    for tap in range(TAP_COUNT):
        for ref, own, part in zip((high_ref, low_ref), (own_high, own_low), filter_columns(template, tap, held_ref)):
            ref[tap, :BLOCK] = part[:BLOCK]
            ref[tap, BLOCK : BLOCK + row_count] = own[tap]
            ref[tap, BLOCK + row_count :] = part[BLOCK:]
    for visit in range(visits):
        first = visit * HALO
        wide_ref[visit, :EDGE] = above_ref[first + HALO - EDGE : first + HALO]
        wide_ref[visit, EDGE : EDGE + row_count] = sci_ref[visit]
        wide_ref[visit, EDGE + row_count :] = below_ref[first : first + EDGE]
    copies = start_copies(((high_ref, high_out), (low_ref, low_out), (wide_ref, wide_out)), sems)
    for block in range(row_count // BLOCK):
        start = EDGE + block * BLOCK
        for tile, (group, columns) in enumerate(TILES):
            depth = tile_depth(tile, visits)
            rows = [held_ref[TAP_COUNT + tile, half, :, :depth] for half in range(2)]
            taps = [TAP_FIRST[group] + column for column in columns]
            high = [high_ref[tap, start : start + WINDOW] for tap in taps]
            low = [low_ref[tap, start : start + WINDOW] for tap in taps]
            if tile == len(TILES) - 1:
                for visit in range(visits):
                    pair = split(sci_ref[visit, block * BLOCK : (block + 1) * BLOCK])
                    high.append(pair[0])
                    low.append(pair[1])
                high.append(jnp.ones((16, col_count), BF16))
                low.append(jnp.zeros((16, col_count), BF16))
            both = mul(jnp.concatenate(rows, axis=0), jnp.concatenate(high, axis=0))
            part = both[: 8 * BLOCK] + both[8 * BLOCK :] + mul(rows[0], jnp.concatenate(low, axis=0))
            design_ref[block * BLOCK : (block + 1) * BLOCK, 8 * tile : 8 * tile + 8] = part.reshape(
                BLOCK, 8, col_count
            )
    first = visits * HALO
    hits = hits_ref[...]
    for ref, shift in ((above_ref, -row_count), (below_ref, row_count)):
        hits = hits + near_mask(ref[first : first + 8, :LANES], float(shift), row_count, col_count)
    mask_ref[...] = jnp.minimum(hits, 1.0)
    for copy in copies:
        copy.wait()


def gram_kernel(cfg, warp_ref, cells_ref, mask_ref, design_ref, *refs):
    patches, capacity, visits, row_count, col_count, block_count, step = cfg
    blocks = refs[:block_count]
    var_ref, down_ref, up_ref, gram_ref, total_ref, weight_ref, sum_ref = refs[block_count:]
    me = lax.axis_index("patch")
    assemble((patches, capacity), blocks, cells_ref, total_ref, me)
    shared = jnp.full((row_count, col_count), SKY_VAR, F32)
    for visit in range(visits):
        plane = warped(total_ref, visit, warp_ref, row_count, col_count)
        var_ref[visit] = plane
        shared = shared + plane * (1.0 / (visits * visits))
    mask = mask_ref[...]
    for visit in range(visits):
        weight_ref[visit] = mask / (var_ref[visit] + shared)
    sum_ref[...] = jnp.zeros(sum_ref.shape, F32)

    def body(number, carry):
        left, right = [], []
        for extra in range(step):
            row = number * step + extra
            design = design_ref[row]
            high, low = split(design)
            blank = jnp.zeros((HALF - SLOTS, col_count), BF16)
            right.append(jnp.concatenate([high, blank, low, blank], axis=0))
            scaled = [design * weight_ref[visit, pl.ds(row, 1), :] for visit in range(visits)]
            left.append(jnp.concatenate(split(jnp.concatenate(scaled, axis=0)), axis=0))
        sum_ref[...] += mul_nt(jnp.concatenate(left, axis=1), jnp.concatenate(right, axis=1))
        return carry

    lax.fori_loop(0, row_count // step, body, 0)
    lane = lax.broadcasted_iota(jnp.int32, (SLOTS, 2 * HALF), 1)
    both = []
    for visit in range(visits):
        first = visit * SLOTS
        second = (visits + visit) * SLOTS
        value = sum_ref[first : first + SLOTS] + sum_ref[second : second + SLOTS]
        both.append(value + pltpu.roll(value, HALF, 1))
    for pair in range(visits // 2):
        value = jnp.where(lane < HALF, both[2 * pair], both[2 * pair + 1])
        for ref in (gram_ref, down_ref, up_ref):
            ref[pair * SLOTS : (pair + 1) * SLOTS] = value
    first = visits // 2 * SLOTS
    for visit in range(visits):
        for part in range(col_count // LANES):
            place = first + (visit * (col_count // LANES) + part) * EDGE
            lanes = slice(part * LANES, (part + 1) * LANES)
            down_ref[place : place + EDGE] = var_ref[visit, row_count - EDGE :, lanes]
            up_ref[place : place + EDGE] = var_ref[visit, :EDGE, lanes]


def solve_kernel(cfg, var_ref, *refs):
    visits, row_count, col_count, subtiles, normalizer, gram_count = cfg
    grams = refs[:gram_count]
    fixed = refs[gram_count : gram_count + 6]
    diff_ref, sig_ref, *held, sems = refs[gram_count + 6 :]
    copies = start_copies(zip(fixed, held), sems)
    filter_ref, edge_ref, doubled_ref, wide_ref, high_ref, low_ref = held
    sub = lax.axis_index("sub")
    high_rows = row_count + 2 * EDGE
    parts = col_count // LANES
    first = visits // 2 * SLOTS

    def halo(ref, visit):
        pieces = [ref[first + (visit * parts + part) * EDGE :][:EDGE] for part in range(parts)]
        return jnp.concatenate(pieces, axis=1)

    from_above, from_below = grams[1], grams[-1]
    row_at = lax.broadcasted_iota(jnp.int32, (high_rows, col_count), 0) + sub * row_count - EDGE
    inside = (row_at >= 0) & (row_at < subtiles * row_count)
    spread = [
        jnp.concatenate([halo(from_above, visit), var_ref[visit], halo(from_below, visit)], axis=0)
        for visit in range(visits)
    ]
    shared = jnp.full((high_rows, col_count), SKY_VAR, F32)
    for visit in range(visits):
        shared = shared + spread[visit] * (1.0 / (visits * visits))
    inverse = [jnp.where(inside, 1.0 / (spread[visit] + shared), 0.0) for visit in range(visits)]

    def detected(images, kind):
        filtered = mul3(split(jnp.concatenate(images, axis=0)), (filter_ref[kind], filter_ref[kind + 1]))
        pair = split(filtered)
        rows = (edge_ref[kind, :, :high_rows], edge_ref[kind + 1, :, :high_rows])
        return [
            mul3(rows, (pair[0][v * high_rows : (v + 1) * high_rows], pair[1][v * high_rows : (v + 1) * high_rows]))
            for v in range(visits)
        ]

    for copy in copies[:3]:
        copy.wait()
    noise = detected(inverse, 2)

    lane = lax.broadcasted_iota(jnp.int32, (SLOTS, 2 * HALF), 1)
    line = lax.broadcasted_iota(jnp.int32, (SLOTS, 2 * HALF), 0)
    systems = []
    for pair in range(visits // 2):
        total = grams[0][pair * SLOTS : (pair + 1) * SLOTS]
        for ref in grams[1:]:
            total = total + ref[pair * SLOTS : (pair + 1) * SLOTS]
        diagonal = (lane == line) | (lane == line + HALF)
        systems.append(total + jnp.where(diagonal, RIDGE * total + RIDGE * EPS * normalizer, 0.0))
    pairs = range(visits // 2)
    tiles = [[matrix[8 * part : 8 * part + 8] for part in range(len(TILES))] for matrix in systems]
    line, lane = line[:8], lane[:8]
    for panel in range(len(TILES)):
        slots = [slot for slot in LIVE_SLOTS if slot // 8 == panel]
        place = {slot: jnp.where(lane < HALF, slot, HALF + slot) for slot in slots}
        columns = [
            {slot: [jnp.take_along_axis(tile, place[slot], axis=1) for tile in tiles[pair]] for slot in slots}
            for pair in pairs
        ]
        for number, slot in enumerate(slots):
            row = slot % 8
            at_row = line == row
            for pair in pairs:
                column = columns[pair][slot]
                scale = 1.0 / column[panel][row : row + 1]

                def eliminate(parts):
                    factor = parts[panel][row : row + 1] * scale
                    done = [part - column[index] * factor for index, part in enumerate(parts)]
                    done[panel] = jnp.where(at_row, factor, done[panel])
                    return done

                for later in slots[number + 1 :]:
                    columns[pair][later] = eliminate(columns[pair][later])
                tiles[pair] = eliminate(tiles[pair])
    for copy in copies[3:]:
        copy.wait()
    left = []
    offsets = []
    half_lane = lax.broadcasted_iota(jnp.int32, (BLOCK, 2 * HALF), 1) < HALF
    for pair in range(visits // 2):
        wanted = SCI_SLOT + 2 * pair
        place = jnp.where(lane < HALF, wanted, HALF + wanted + 1)
        solved = jnp.concatenate([jnp.take_along_axis(tile, place, axis=1) for tile in tiles[pair]], axis=0)
        mixes = [None] * TAP_COUNT
        for slot, (row_tap, col_tap) in SLOT_TAPS.items():
            term = solved[slot : slot + 1] * doubled_ref[row_tap]
            mixes[col_tap] = term if mixes[col_tap] is None else mixes[col_tap] + term
        own, other = [], []
        for tap in range(0, TAP_COUNT, 2):
            own.append(jnp.where(half_lane, mixes[tap], pltpu.roll(mixes[tap + 1], HALF, 1)))
            other.append(jnp.where(half_lane, pltpu.roll(mixes[tap], HALF, 1), mixes[tap + 1]))
        left += [jnp.concatenate(own, axis=1), jnp.concatenate(other, axis=1)]
        tail = solved[ONE_SLOT // 8 * 8 : ONE_SLOT // 8 * 8 + 8]
        for begin in (0, HALF):
            flat = jnp.take_along_axis(tail, jnp.full((8, LANES), begin, jnp.int32), axis=1)
            flat = flat[ONE_SLOT % 8 : ONE_SLOT % 8 + 1]
            offsets.append(jnp.concatenate([flat] * parts, axis=1))
    left = split(jnp.concatenate(left, axis=0))
    models = []
    for block in range(high_rows // BLOCK):
        start = block * BLOCK
        stack = tuple(
            jnp.concatenate([ref[tap, start : start + WINDOW] for tap in range(TAP_COUNT)], axis=0)
            for ref in (high_ref, low_ref)
        )
        models.append(mul3(left, stack))
    weighted = []
    for visit in range(visits):
        model = jnp.concatenate([part[visit * BLOCK : (visit + 1) * BLOCK] for part in models], axis=0)
        difference = wide_ref[visit] - model - offsets[visit]
        diff_ref[visit, 0] = difference[EDGE : EDGE + row_count]
        weighted.append(difference * inverse[visit])
    signal = detected(weighted, 0)
    for visit in range(visits):
        sig_ref[visit, 0] = signal[visit] * lax.rsqrt(noise[visit])


def vmem():
    return pl.BlockSpec(memory_space=pltpu.VMEM)


def smem():
    return pl.BlockSpec(memory_space=pltpu.SMEM)


def far():
    return pl.BlockSpec(memory_space=pltpu.HBM)


def in_hbm(array):
    return pltpu.with_memory_space_constraint(jnp.asarray(array), pltpu.HBM)


def call(kernel, outs, out_specs, in_specs, scratch):
    return pl.pallas_call(
        kernel,
        out_shape=outs,
        in_specs=in_specs,
        out_specs=out_specs,
        scratch_shapes=scratch,
        compiler_params=pltpu.CompilerParams(vmem_limit_bytes=VMEM_BYTES),
    )


def after(array, others):
    return pl.pallas_call(
        lambda *refs: None,
        out_shape=[jax.ShapeDtypeStruct(array.shape, array.dtype)],
        in_specs=[far()] * (1 + len(others)),
        out_specs=[far()],
        input_output_aliases={0: 0},
        compiler_params=pltpu.CompilerParams(vmem_limit_bytes=1024 * 1024),
    )(array, *others)


def local(
    pieces_image,
    pieces_variance,
    piece_patch,
    piece_cell,
    stamp_row,
    stamp_col,
    stamp_count,
    warp_offsets,
):
    patches = lax.axis_size("patch")
    subtiles = lax.axis_size("sub")
    _, pieces, cell_rows, col_count = pieces_image.shape
    visits = warp_offsets.shape[0]
    row_count = cell_rows * NCELL
    slots = stamp_row.shape[1]
    capacity = max(2, 2 * pieces // patches)
    direct = patches <= 8
    units = 2 * capacity
    sds = jax.ShapeDtypeStruct
    design_fixed, filters, edges, doubled = constants(visits, row_count, col_count)

    image_blocks = patches if direct else 1
    var_blocks = 1

    def sent(blocks, depth):
        return [sds((1 if blocks > 1 else patches, depth, 8, LANES), F32)] * blocks

    *images, stamps, warps, chosen = call(
        functools.partial(pack_kernel, (patches, capacity, pieces, image_blocks, slots)),
        sent(image_blocks, units + 1)
        + [sds((8, LANES), F32), sds((visits,), jnp.int32), sds((patches * capacity,), jnp.int32)],
        [vmem()] * (image_blocks + 1) + [smem()] * 2,
        [far()] * 7,
        [
            pltpu.VMEM((-(-patches // 8) * 8, LANES), F32),
            pltpu.SMEM((patches,), jnp.int32),
            pltpu.SMEM((1, pieces), jnp.int32),
            pltpu.SMEM((1, pieces), jnp.int32),
            pltpu.VMEM((1, slots), jnp.int32),
            pltpu.VMEM((1, slots), jnp.int32),
            pltpu.SMEM((1, 1), jnp.int32),
            pltpu.VMEM(pieces_image.shape, F32),
            pltpu.SemaphoreType.DMA((7,)),
        ],
    )(
        in_hbm(piece_patch[:, :, 0]),
        in_hbm(piece_cell),
        in_hbm(stamp_row),
        in_hbm(stamp_col),
        stamp_count,
        in_hbm(pieces_image),
        in_hbm(warp_offsets),
    )

    def route(blocks):
        if len(blocks) == 1:
            return [lax.all_to_all(blocks[0], "patch", split_axis=0, concat_axis=0, tiled=True)]
        result = list(blocks[:1])
        for away, block in zip(turn(patches)[1:], blocks[1:]):
            result.append(lax.ppermute(block, "patch", [(i, i ^ away) for i in range(patches)]))
        return result

    got = route(images)
    variances = call(
        functools.partial(pack_more_kernel, (patches, capacity, var_blocks)),
        sent(var_blocks, units),
        [vmem()] * var_blocks,
        [smem(), far()],
        [pltpu.VMEM(pieces_image.shape, F32), pltpu.SemaphoreType.DMA((1,))],
    )(chosen, in_hbm(pieces_variance))
    if direct:
        variances = after(variances[0], got[1:])
    got_var = route(variances)

    side = sds((visits * HALO + 8, col_count), F32)
    science, up, down, cells = call(
        functools.partial(image_kernel, (patches, capacity, visits, row_count, col_count, image_blocks)),
        [sds((visits, row_count, col_count), F32), side, side, sds((patches * capacity,), jnp.int32)],
        [vmem(), vmem(), vmem(), smem()],
        [smem()] + [vmem()] * (1 + image_blocks),
        [
            pltpu.VMEM((visits * NCELL + 1, 2, 8, LANES), F32),
            pltpu.SMEM((patches, LANES), F32),
            pltpu.SemaphoreType.DMA((patches,)),
        ],
    )(warps, stamps, *got)
    above = lax.ppermute(down, "sub", [(i, i + 1) for i in range(subtiles - 1)])
    below = lax.ppermute(up, "sub", [(i + 1, i) for i in range(subtiles - 1)])

    field = sds((TAP_COUNT, row_count + 2 * BLOCK, col_count), BF16)
    own_field = sds((TAP_COUNT, row_count, col_count), BF16)
    plane = sds((row_count, col_count), F32)
    wide = sds((visits, row_count + 2 * EDGE, col_count), F32)
    held, own_high, own_low, hits = call(
        functools.partial(own_kernel, (visits, row_count, col_count)),
        [sds(design_fixed.shape, BF16), own_field, own_field, plane],
        [vmem()] * 4,
        [vmem(), vmem(), far()],
        [pltpu.SemaphoreType.DMA((design_fixed.shape[0],))],
    )(science, stamps, in_hbm(design_fixed))
    design, mask, high, low, wide_science = call(
        functools.partial(design_kernel, (visits, row_count, col_count)),
        [sds((row_count, SLOTS, col_count), F32), plane] + [pltpu.HBM(part.shape, part.dtype) for part in (field, field, wide)],
        [vmem()] * 2 + [far()] * 3,
        [vmem()] * 7,
        [pltpu.VMEM(part.shape, part.dtype) for part in (field, field, wide)] + [pltpu.SemaphoreType.DMA((3,))],
    )(science, above, below, held, own_high, own_low, hits)

    gram_rows = visits // 2 * SLOTS
    tail_rows = visits * EDGE * (col_count // LANES)
    step = 32
    variance, to_below, to_above, gram = call(
        functools.partial(gram_kernel, (patches, capacity, visits, row_count, col_count, var_blocks, step)),
        [
            sds((visits, row_count, col_count), F32),
            sds((gram_rows + tail_rows, LANES), F32),
            sds((gram_rows + tail_rows, LANES), F32),
            sds((gram_rows, LANES), F32),
        ],
        [vmem()] * 4,
        [smem(), smem(), vmem(), vmem()] + [vmem()] * var_blocks,
        [
            pltpu.VMEM((visits * NCELL + 1, 2, 8, LANES), F32),
            pltpu.VMEM((visits, row_count, col_count), F32),
            pltpu.VMEM((2 * visits * SLOTS, 2 * HALF), F32),
        ],
    )(warps, cells, mask, design, *got_var)
    grams = [gram]
    for shift in range(1, subtiles):
        sent = to_below if shift == 1 else to_above if shift == subtiles - 1 else gram
        grams.append(lax.ppermute(sent, "sub", [(i, (i + shift) % subtiles) for i in range(subtiles)]))

    normalizer = subtiles * slots * (2 * SH + 1) ** 2
    result = sds((visits, 1, row_count, col_count), F32)
    kept = [filters, edges, doubled, wide_science, high, low]
    return call(
        functools.partial(solve_kernel, (visits, row_count, col_count, subtiles, float(normalizer), len(grams))),
        [result, result],
        [vmem(), vmem()],
        [vmem()] * (1 + len(grams)) + [far()] * len(kept),
        [pltpu.VMEM(part.shape, part.dtype) for part in kept] + [pltpu.SemaphoreType.DMA((len(kept),))],
    )(variance, *grams, *[in_hbm(part) for part in kept])


def solution(mesh):
    in_specs = (
        P("sub", "patch", None, None),
        P("sub", "patch", None, None),
        P("sub", "patch", None),
        P("sub", "patch"),
        P("patch", "sub"),
        P("patch", "sub"),
        P("patch", "sub"),
        P(),
    )
    out_specs = (P(None, "patch", "sub", None), P(None, "patch", "sub", None))
    return jax.shard_map(local, mesh=mesh, in_specs=in_specs, out_specs=out_specs, check_vma=False)
```

```python
import functools

import jax
import jax.numpy as jnp
import ml_dtypes
import numpy as np
from jax import lax
from jax.experimental import pallas as pl
from jax.experimental.pallas import tpu as pltpu
from jax.sharding import PartitionSpec as P

NCELL = 8
KR = 10
PR = 10
SH = 15
WARP = 4

SIGMAS = (0.75, 1.5, 3.0)
DEGREES = (4, 4, 3)
PSF_SIGMA = 2.0
SKY_VAR = 0.1
RIDGE = 0.5
EPS = 1e-05

F32 = jnp.float32
BF16 = jnp.bfloat16
LANES = 128
HALO = 24
EDGE = 16
BLOCK = 32
WINDOW = 64
VMEM_BYTES = 20 * 1024 * 1024

TILES = ((0, (0, 2)), (0, (1, 3, 4)), (1, (0, 2)), (1, (1, 3, 4)), (2, (0, 1, 3)), (2, (2,)))
SLOTS = 8 * len(TILES)
HALF = 64
TAP_FIRST = (0, DEGREES[0] + 1, DEGREES[0] + DEGREES[1] + 2)
TAP_COUNT = sum(DEGREES) + len(DEGREES)


def slot_table():
    result = {}
    for tile, (group, columns) in enumerate(TILES):
        slot = 8 * tile
        for column in columns:
            for row in range(DEGREES[group] + 1 - column):
                result[slot] = (TAP_FIRST[group] + row, TAP_FIRST[group] + column)
                slot += 1
    return result


SLOT_TAPS = slot_table()
ONE_SLOT = 8 * (len(TILES) - 1) + 2
SCI_SLOT = ONE_SLOT + 1
LIVE_SLOTS = sorted(SLOT_TAPS) + [ONE_SLOT]


def basis_taps():
    offset = np.arange(-KR, KR + 1, dtype=np.float64)
    rows = []
    for spread, degree in zip(SIGMAS, DEGREES):
        scaled = offset / spread
        envelope = np.exp(-0.5 * scaled * scaled)
        previous, current = np.zeros_like(scaled), np.ones_like(scaled)
        for term_no in range(degree + 1):
            rows.append(current * envelope)
            previous, current = current, scaled * current - term_no * previous
    taps = np.stack(rows)
    return taps / np.sqrt(np.sum(taps * taps, axis=1, keepdims=True))


def psf_taps():
    offset = np.arange(-PR, PR + 1, dtype=np.float64)
    values = np.exp(-0.5 * (offset / PSF_SIGMA) ** 2)
    return values / values.sum()


def band(taps, rows, columns, shift):
    radius = (taps.shape[-1] - 1) // 2
    offset = np.arange(columns)[None, :] - shift - np.arange(rows)[:, None]
    inside = np.abs(offset) <= radius
    return np.where(inside, taps[..., np.clip(offset + radius, 0, 2 * radius)], 0.0)


def halves(values):
    values = np.asarray(values, np.float32)
    high = values.astype(ml_dtypes.bfloat16)
    low = (values - high.astype(np.float32)).astype(ml_dtypes.bfloat16)
    return high, low


def tile_depth(tile, visits):
    depth = len(TILES[tile][1]) * WINDOW
    return depth + visits * BLOCK + 16 if tile == len(TILES) - 1 else depth


@functools.lru_cache(maxsize=None)
def constants(visits, row_count, col_count):
    taps = basis_taps()
    column_bands = np.stack([band(taps[t], col_count, col_count, 0).T for t in range(TAP_COUNT)])
    toeplitz = np.stack([band(taps[t], BLOCK, WINDOW, EDGE) for t in range(TAP_COUNT)])
    row_parts = []
    for tile, (group, columns) in enumerate(TILES):
        matrix = np.zeros((BLOCK, 8, tile_depth(tile, visits)))
        slot = 0
        for place, column in enumerate(columns):
            for row in range(DEGREES[group] + 1 - column):
                matrix[:, slot, place * WINDOW : (place + 1) * WINDOW] = toeplitz[TAP_FIRST[group] + row]
                slot += 1
        if tile == len(TILES) - 1:
            base = len(columns) * WINDOW
            for visit in range(visits):
                first = base + visit * BLOCK
                matrix[np.arange(BLOCK), slot + 1 + visit, first + np.arange(BLOCK)] = 1.0
            matrix[:, slot, base + visits * BLOCK] = 1.0
        row_parts.append(matrix.reshape(BLOCK * 8, -1))
    depth = col_count
    for tile, part in enumerate(row_parts):
        row_parts[tile] = np.pad(part, ((0, 0), (0, depth - part.shape[1])))
    design = np.stack(halves(np.concatenate([column_bands, np.stack(row_parts)])), axis=1)
    psf = psf_taps()
    filters = np.stack([half for power in (1, 2) for half in halves(band(psf**power, col_count, col_count, 0).T)])
    edges = np.stack(
        [half for power in (1, 2) for half in halves(band(psf**power, row_count, row_count + 2 * EDGE, EDGE))]
    )
    edges = np.pad(edges, ((0, 0), (0, 0), (0, -edges.shape[2] % LANES)))
    doubled = np.concatenate([toeplitz, toeplitz], axis=2).astype(np.float32)
    return design, filters, edges, doubled


def split(values):
    high = values.astype(BF16)
    return high, (values - high.astype(F32)).astype(BF16)


def mul(left, right):
    return jnp.dot(left, right, preferred_element_type=F32)


def mul3(left, right):
    return mul(left[0], right[0]) + mul(left[0], right[1]) + mul(left[1], right[0])


def mul_nt(left, right):
    return lax.dot_general(left, right, (((1,), (1,)), ((), ())), preferred_element_type=F32)


def turn(patches):
    near, far_half = list(range(1, patches // 2)), list(range(patches // 2, patches))
    return [0, *near[:2], *far_half, *near[2:]]


def fill(cfg, outs, source, chosen_ref, table_ref):
    patches, capacity = cfg
    me = lax.axis_index("patch")
    for block in range(patches):
        if len(outs) == 1:
            out, place, away = outs[0], block, block ^ me
        else:
            out, place, away = outs[block], 0, turn(patches)[block]
        for rank in range(capacity):
            piece = chosen_ref[away * capacity + rank]
            out[place, 2 * rank] = source[0, piece, :, :LANES]
            out[place, 2 * rank + 1] = source[0, piece, :, LANES:]
        if table_ref is not None:
            out[place, 2 * capacity] = jnp.broadcast_to(table_ref[pl.ds(away, 1), :], (8, LANES))


def start_copies(pairs, sems):
    copies = [pltpu.make_async_copy(source, place, sems.at[number]) for number, (source, place) in enumerate(pairs)]
    for copy in copies:
        copy.start()
    return copies


def pack_kernel(cfg, *refs):
    patches, capacity, pieces, blocks, slots = cfg
    sources, refs = refs[:7], refs[7:]
    outs, refs = refs[:blocks], refs[blocks:]
    stamp_out, warp_out, chosen_ref, table_ref, count_ref, *held = refs
    held, sems = held[:-1], held[-1]
    target_ref, cell_ref, row_ref, col_ref, live_ref, image_ref = held
    copies = start_copies(
        zip(sources, (target_ref, cell_ref, row_ref, col_ref, live_ref, image_ref, warp_out)), sems
    )
    me = lax.axis_index("patch")
    for entry in range(patches * capacity):
        chosen_ref[entry] = 0
    for entry in range(patches):
        count_ref[entry] = 0
    line = lax.broadcasted_iota(jnp.int32, table_ref.shape, 0)
    lane = lax.broadcasted_iota(jnp.int32, table_ref.shape, 1)
    copies[0].wait()
    copies[1].wait()
    table = jnp.full(table_ref.shape, -1.0, F32)
    for piece in range(pieces):
        away = target_ref[0, piece] ^ me
        rank = count_ref[away]
        count_ref[away] = rank + 1
        chosen_ref[away * capacity + rank] = piece
        value = cell_ref[0, piece].astype(F32)
        table = jnp.where((line == away) & (lane == rank), value, table)
    table_ref[...] = table
    for copy in copies[2:5]:
        copy.wait()
    live = lax.broadcasted_iota(jnp.int32, (1, slots), 1) < live_ref[0, 0]
    stamp_out[...] = jnp.zeros(stamp_out.shape, F32)
    stamp_out[0:1, :slots] = row_ref[...].astype(F32)
    stamp_out[1:2, :slots] = col_ref[...].astype(F32)
    stamp_out[2:3, :slots] = jnp.where(live, 1.0, 0.0)
    copies[5].wait()
    fill((patches, capacity), outs, image_ref, chosen_ref, table_ref)
    copies[6].wait()


def pack_more_kernel(cfg, chosen_ref, var_hbm, *refs):
    patches, capacity, blocks = cfg
    outs, (var_ref, sems) = refs[:blocks], refs[blocks:]
    (copy,) = start_copies([(var_hbm, var_ref)], sems)
    copy.wait()
    fill((patches, capacity), outs, var_ref, chosen_ref, None)


def assemble(cfg, blocks, cells_ref, total_ref, me):
    patches, capacity = cfg
    total_ref[...] = jnp.zeros(total_ref.shape, F32)
    for block in range(patches):
        if len(blocks) == 1:
            ref, place, away = blocks[0], block, block ^ me
        else:
            ref, place, away = blocks[block], 0, turn(patches)[block]
        for rank in range(capacity):
            cell = cells_ref[away * capacity + rank]
            total_ref[cell, 0] += ref[place, 2 * rank]
            total_ref[cell, 1] += ref[place, 2 * rank + 1]


def warped(total_ref, visit, warp_ref, row_count, col_count):
    first = visit * NCELL
    left = total_ref[first : first + NCELL, 0].reshape(row_count, LANES)
    right = total_ref[first : first + NCELL, 1].reshape(row_count, LANES)
    plane = jnp.concatenate([left, right], axis=1)
    offset = warp_ref[visit] - WARP
    moved = pltpu.roll(plane, lax.rem(col_count - offset, col_count), 1)
    source = lax.broadcasted_iota(jnp.int32, plane.shape, 1) + offset
    return jnp.where((source >= 0) & (source < col_count), moved, 0.0)


def image_kernel(cfg, warp_ref, stamp_ref, *refs):
    patches, capacity, visits, row_count, col_count, block_count = cfg
    blocks = refs[:block_count]
    sci_ref, near_out, far_out, cells_ref, total_ref, near_ref, sems = refs[block_count:]
    me = lax.axis_index("patch")
    odd = lax.axis_index("sub") % 2 == 1
    copies = []
    for block in range(patches):
        ref, place = (blocks[0], block) if block_count == 1 else (blocks[block], 0)
        copies.append(
            pltpu.make_async_copy(
                ref.at[place, 2 * capacity, pl.ds(0, 1), :], near_ref.at[pl.ds(block, 1), :], sems.at[block]
            )
        )
    for copy in copies:
        copy.start()
    for copy in copies:
        copy.wait()
    for block in range(patches):
        away = block ^ me if block_count == 1 else turn(patches)[block]
        for rank in range(capacity):
            cell = near_ref[block, rank].astype(jnp.int32)
            cells_ref[away * capacity + rank] = jnp.where(cell < 0, visits * NCELL, cell)
    assemble((patches, capacity), blocks, cells_ref, total_ref, me)
    for visit in range(visits):
        plane = warped(total_ref, visit, warp_ref, row_count, col_count)
        sci_ref[visit] = plane
        top, bottom = plane[:HALO], plane[row_count - HALO :]
        near_out[visit * HALO : (visit + 1) * HALO] = jnp.where(odd, top, bottom)
        far_out[visit * HALO : (visit + 1) * HALO] = jnp.where(odd, bottom, top)
    first = visits * HALO
    for ref in (near_out, far_out):
        ref[first : first + 8, :LANES] = stamp_ref[...]
        ref[first : first + 8, LANES:] = jnp.zeros((8, col_count - LANES), F32)


def near_mask(stamps, shift, row_count, col_count):
    row_at = lax.broadcasted_iota(jnp.int32, (row_count, LANES), 0).astype(F32)
    col_at = lax.broadcasted_iota(jnp.int32, (col_count, LANES), 0).astype(F32)
    row_in = (jnp.abs(row_at - (stamps[0:1] + shift)) <= SH) & (stamps[2:3] > 0.5)
    col_in = jnp.abs(col_at - stamps[1:2]) <= SH
    return mul_nt(jnp.where(row_in, 1.0, 0.0).astype(BF16), jnp.where(col_in, 1.0, 0.0).astype(BF16))


def filter_columns(image, tap, held_ref):
    rows = image[0].shape[0]
    both = mul(jnp.concatenate(image, axis=0), held_ref[tap, 0])
    return split(both[:rows] + both[rows:] + mul(image[0], held_ref[tap, 1]))


def own_kernel(cfg, sci_ref, stamp_ref, fixed_ref, held_ref, high_ref, low_ref, hits_ref, sems):
    visits, row_count, col_count = cfg
    copies = start_copies([(fixed_ref.at[n], held_ref.at[n]) for n in range(TAP_COUNT + len(TILES))], sems)
    own = sci_ref[0]
    for visit in range(1, visits):
        own = own + sci_ref[visit]
    template = split(own * (1.0 / visits))
    hits_ref[...] = near_mask(stamp_ref[...], 0.0, row_count, col_count)
    for tap in range(TAP_COUNT):
        copies[tap].wait()
        high_ref[tap], low_ref[tap] = filter_columns(template, tap, held_ref)
    for copy in copies[TAP_COUNT:]:
        copy.wait()


def design_kernel(cfg, sci_ref, far_ref, near_ref, held_ref, own_high, own_low, hits_ref, *refs):
    visits, row_count, col_count = cfg
    design_ref, mask_ref, high_out, low_out, wide_out, high_ref, low_ref, wide_ref, sems = refs
    odd = lax.axis_index("sub") % 2 == 1

    def beside(first, count, lanes=slice(None)):
        near, far = near_ref[first : first + count, lanes], far_ref[first : first + count, lanes]
        return jnp.where(odd, near, far), jnp.where(odd, far, near)

    above, below = beside(0, HALO)
    for visit in range(1, visits):
        more = beside(visit * HALO, HALO)
        above, below = above + more[0], below + more[1]
    rim = jnp.zeros((BLOCK - HALO, col_count), F32)
    template = split(jnp.concatenate([rim, above, below, rim], axis=0) * (1.0 / visits))
    for tap in range(TAP_COUNT):
        for ref, own, part in zip((high_ref, low_ref), (own_high, own_low), filter_columns(template, tap, held_ref)):
            ref[tap, :BLOCK] = part[:BLOCK]
            ref[tap, BLOCK : BLOCK + row_count] = own[tap]
            ref[tap, BLOCK + row_count :] = part[BLOCK:]
    for visit in range(visits):
        first = visit * HALO
        wide_ref[visit, :EDGE] = beside(first + HALO - EDGE, EDGE)[0]
        wide_ref[visit, EDGE : EDGE + row_count] = sci_ref[visit]
        wide_ref[visit, EDGE + row_count :] = beside(first, EDGE)[1]
    copies = start_copies(((high_ref, high_out), (low_ref, low_out), (wide_ref, wide_out)), sems)
    for block in range(row_count // BLOCK):
        start = EDGE + block * BLOCK
        for tile, (group, columns) in enumerate(TILES):
            depth = tile_depth(tile, visits)
            rows = [held_ref[TAP_COUNT + tile, half, :, :depth] for half in range(2)]
            taps = [TAP_FIRST[group] + column for column in columns]
            high = [high_ref[tap, start : start + WINDOW] for tap in taps]
            low = [low_ref[tap, start : start + WINDOW] for tap in taps]
            if tile == len(TILES) - 1:
                for visit in range(visits):
                    pair = split(sci_ref[visit, block * BLOCK : (block + 1) * BLOCK])
                    high.append(pair[0])
                    low.append(pair[1])
                high.append(jnp.ones((16, col_count), BF16))
                low.append(jnp.zeros((16, col_count), BF16))
            both = mul(jnp.concatenate(rows, axis=0), jnp.concatenate(high, axis=0))
            part = both[: 8 * BLOCK] + both[8 * BLOCK :] + mul(rows[0], jnp.concatenate(low, axis=0))
            design_ref[block * BLOCK : (block + 1) * BLOCK, 8 * tile : 8 * tile + 8] = part.reshape(
                BLOCK, 8, col_count
            )
    first = visits * HALO
    hits = hits_ref[...]
    for stamps, shift in zip(beside(first, 8, slice(LANES)), (-row_count, row_count)):
        hits = hits + near_mask(stamps, float(shift), row_count, col_count)
    mask_ref[...] = jnp.minimum(hits, 1.0)
    for copy in copies:
        copy.wait()


def gram_kernel(cfg, warp_ref, cells_ref, mask_ref, design_ref, *refs):
    patches, capacity, visits, row_count, col_count, block_count, step = cfg
    blocks = refs[:block_count]
    var_ref, near_ref, far_ref, gram_ref, total_ref, weight_ref, sum_ref = refs[block_count:]
    me = lax.axis_index("patch")
    odd = lax.axis_index("sub") % 2 == 1
    assemble((patches, capacity), blocks, cells_ref, total_ref, me)
    shared = jnp.full((row_count, col_count), SKY_VAR, F32)
    for visit in range(visits):
        plane = warped(total_ref, visit, warp_ref, row_count, col_count)
        var_ref[visit] = plane
        shared = shared + plane * (1.0 / (visits * visits))
    mask = mask_ref[...]
    for visit in range(visits):
        weight_ref[visit] = mask / (var_ref[visit] + shared)
    sum_ref[...] = jnp.zeros(sum_ref.shape, F32)

    body_rows, tail = 8 * (len(TILES) - 1), ONE_SLOT % 8 + 1
    rows = visits * body_rows + visits // 2 * 8
    kept = 2 * LANES - 2 * SLOTS - 16
    at_first = lax.broadcasted_iota(jnp.int32, (8, col_count), 0) < tail

    def body(number, carry):
        left, right = [], []
        for extra in range(step):
            row = number * step + extra
            design = design_ref[row]
            high, low = split(design)
            weights = [weight_ref[visit, pl.ds(row, 1), :] for visit in range(visits)]
            scaled = [design[:body_rows] * weight for weight in weights]
            last = design[body_rows:]
            moved = pltpu.roll(last, tail, 0)
            for pair in range(visits // 2):
                scaled.append(jnp.where(at_first, last * weights[2 * pair], moved * weights[2 * pair + 1]))
            scaled_high, scaled_low = split(jnp.concatenate(scaled, axis=0))
            blank = jnp.zeros((16, col_count), BF16)
            right.append(jnp.concatenate([high, low, scaled_low[:kept], blank], axis=0))
            left.append(jnp.concatenate([scaled_high, high, scaled_low[kept:]], axis=0))
        sum_ref[...] += mul_nt(jnp.concatenate(left, axis=1), jnp.concatenate(right, axis=1))
        return carry

    lax.fori_loop(0, row_count // step, body, 0)
    depth = sum_ref.shape[0]
    main = sum_ref[:rows, :LANES]
    turned = jnp.transpose(sum_ref[depth - LANES :, :])[2 * SLOTS : 2 * SLOTS + kept]
    turned = pltpu.roll(turned, depth - rows, 1)
    main = main + pltpu.roll(main, LANES - SLOTS, 1)
    main = main + jnp.concatenate([turned, sum_ref[rows + SLOTS :, :LANES]], axis=0)
    lane = lax.broadcasted_iota(jnp.int32, (SLOTS, 2 * HALF), 1)
    for pair in range(visits // 2):
        ends = main[visits * body_rows + 8 * pair :][:8]
        both = []
        for visit, end in ((2 * pair, ends), (2 * pair + 1, pltpu.roll(ends, 8 - tail, 0))):
            both.append(jnp.concatenate([main[visit * body_rows : (visit + 1) * body_rows], end], axis=0))
        value = jnp.where(lane < HALF, both[0], pltpu.roll(both[1], HALF, 1))
        for ref in (gram_ref, near_ref, far_ref):
            ref[pair * SLOTS : (pair + 1) * SLOTS] = value
    first = visits // 2 * SLOTS
    for visit in range(visits):
        for part in range(col_count // LANES):
            place = first + (visit * (col_count // LANES) + part) * PR
            lanes = slice(part * LANES, (part + 1) * LANES)
            top, bottom = var_ref[visit, :PR, lanes], var_ref[visit, row_count - PR :, lanes]
            near_ref[place : place + PR] = jnp.where(odd, top, bottom)
            far_ref[place : place + PR] = jnp.where(odd, bottom, top)


def solve_kernel(cfg, var_ref, *refs):
    visits, row_count, col_count, subtiles, normalizer, gram_count = cfg
    grams = refs[:gram_count]
    fixed = refs[gram_count : gram_count + 6]
    diff_ref, sig_ref, spread_ref, *held, sems = refs[gram_count + 6 :]
    copies = start_copies(zip(fixed, held), sems)
    filter_ref, edge_ref, doubled_ref, wide_ref, high_ref, low_ref = held
    sub = lax.axis_index("sub")
    high_rows = row_count + 2 * EDGE
    parts = col_count // LANES
    first = visits // 2 * SLOTS

    from_far, from_near = grams[1], grams[3]
    odd = sub % 2 == 1
    for visit in range(visits):
        spread_ref[visit, :EDGE] = jnp.zeros((EDGE, col_count), F32)
        spread_ref[visit, EDGE + row_count :] = jnp.zeros((EDGE, col_count), F32)
        spread_ref[visit, EDGE : EDGE + row_count] = var_ref[visit]
        for part in range(parts):
            place = first + (visit * parts + part) * PR
            lanes = slice(part * LANES, (part + 1) * LANES)
            near, far = from_near[place : place + PR], from_far[place : place + PR]
            spread_ref[visit, EDGE - PR : EDGE, lanes] = jnp.where(odd, near, far)
            spread_ref[visit, EDGE + row_count : EDGE + row_count + PR, lanes] = jnp.where(odd, far, near)
    row_at = lax.broadcasted_iota(jnp.int32, (high_rows, col_count), 0) + sub * row_count - EDGE
    inside = (row_at >= 0) & (row_at < subtiles * row_count)
    spread = [spread_ref[visit] for visit in range(visits)]
    shared = jnp.full((high_rows, col_count), SKY_VAR, F32)
    for visit in range(visits):
        shared = shared + spread[visit] * (1.0 / (visits * visits))
    inverse = [jnp.where(inside, 1.0 / (spread[visit] + shared), 0.0) for visit in range(visits)]

    def detected(images, kind):
        filtered = mul3(split(jnp.concatenate(images, axis=0)), (filter_ref[kind], filter_ref[kind + 1]))
        pair = split(filtered)
        rows = (edge_ref[kind, :, :high_rows], edge_ref[kind + 1, :, :high_rows])
        return [
            mul3(rows, (pair[0][v * high_rows : (v + 1) * high_rows], pair[1][v * high_rows : (v + 1) * high_rows]))
            for v in range(visits)
        ]

    lane = lax.broadcasted_iota(jnp.int32, (SLOTS, 2 * HALF), 1)
    line = lax.broadcasted_iota(jnp.int32, (SLOTS, 2 * HALF), 0)
    systems = []
    for pair in range(visits // 2):
        total = grams[0][pair * SLOTS : (pair + 1) * SLOTS]
        for ref in grams[1:]:
            total = total + ref[pair * SLOTS : (pair + 1) * SLOTS]
        diagonal = (lane == line) | (lane == line + HALF)
        systems.append(total + jnp.where(diagonal, RIDGE * total + RIDGE * EPS * normalizer, 0.0))
    pairs = range(visits // 2)
    tiles = [[matrix[8 * part : 8 * part + 8] for part in range(len(TILES))] for matrix in systems]
    line, lane = line[:8], lane[:8]
    for panel in range(len(TILES)):
        if panel == len(TILES) // 2:
            for copy in copies[:3]:
                copy.wait()
            noise = detected(inverse, 2)
        slots = [slot for slot in LIVE_SLOTS if slot // 8 == panel]
        place = {slot: jnp.where(lane < HALF, slot, HALF + slot) for slot in slots}
        columns = [
            {slot: [jnp.take_along_axis(tile, place[slot], axis=1) for tile in tiles[pair]] for slot in slots}
            for pair in pairs
        ]
        for number, slot in enumerate(slots):
            row = slot % 8
            at_row = line == row
            for pair in pairs:
                column = columns[pair][slot]
                scale = 1.0 / column[panel][row : row + 1]

                def eliminate(parts):
                    factor = parts[panel][row : row + 1] * scale
                    done = [part - column[index] * factor for index, part in enumerate(parts)]
                    done[panel] = jnp.where(at_row, factor, done[panel])
                    return done

                for later in slots[number + 1 :]:
                    columns[pair][later] = eliminate(columns[pair][later])
                tiles[pair] = eliminate(tiles[pair])
    for copy in copies[3:]:
        copy.wait()
    left = []
    offsets = []
    half_lane = lax.broadcasted_iota(jnp.int32, (BLOCK, 2 * HALF), 1) < HALF
    for pair in range(visits // 2):
        wanted = SCI_SLOT + 2 * pair
        place = jnp.where(lane < HALF, wanted, HALF + wanted + 1)
        solved = jnp.concatenate([jnp.take_along_axis(tile, place, axis=1) for tile in tiles[pair]], axis=0)
        mixes = [None] * TAP_COUNT
        for slot, (row_tap, col_tap) in SLOT_TAPS.items():
            term = solved[slot : slot + 1] * doubled_ref[row_tap]
            mixes[col_tap] = term if mixes[col_tap] is None else mixes[col_tap] + term
        own, other = [], []
        for tap in range(0, TAP_COUNT, 2):
            own.append(jnp.where(half_lane, mixes[tap], pltpu.roll(mixes[tap + 1], HALF, 1)))
            other.append(jnp.where(half_lane, pltpu.roll(mixes[tap], HALF, 1), mixes[tap + 1]))
        left += [jnp.concatenate(own, axis=1), jnp.concatenate(other, axis=1)]
        tail = solved[ONE_SLOT // 8 * 8 : ONE_SLOT // 8 * 8 + 8]
        for begin in (0, HALF):
            flat = jnp.take_along_axis(tail, jnp.full((8, LANES), begin, jnp.int32), axis=1)
            flat = flat[ONE_SLOT % 8 : ONE_SLOT % 8 + 1]
            offsets.append(jnp.concatenate([flat] * parts, axis=1))
    left = split(jnp.concatenate(left, axis=0))
    models = []
    for block in range(high_rows // BLOCK):
        start = block * BLOCK
        stack = tuple(
            jnp.concatenate([ref[tap, start : start + WINDOW] for tap in range(TAP_COUNT)], axis=0)
            for ref in (high_ref, low_ref)
        )
        models.append(mul3(left, stack))
    weighted = []
    for visit in range(visits):
        model = jnp.concatenate([part[visit * BLOCK : (visit + 1) * BLOCK] for part in models], axis=0)
        difference = wide_ref[visit] - model - offsets[visit]
        diff_ref[visit, 0] = difference[EDGE : EDGE + row_count]
        weighted.append(difference * inverse[visit])
    signal = detected(weighted, 0)
    for visit in range(visits):
        sig_ref[visit, 0] = signal[visit] * lax.rsqrt(noise[visit])


def vmem():
    return pl.BlockSpec(memory_space=pltpu.VMEM)


def smem():
    return pl.BlockSpec(memory_space=pltpu.SMEM)


def far():
    return pl.BlockSpec(memory_space=pltpu.HBM)


def in_hbm(array):
    return pltpu.with_memory_space_constraint(jnp.asarray(array), pltpu.HBM)


def call(kernel, outs, out_specs, in_specs, scratch):
    return pl.pallas_call(
        kernel,
        out_shape=outs,
        in_specs=in_specs,
        out_specs=out_specs,
        scratch_shapes=scratch,
        compiler_params=pltpu.CompilerParams(vmem_limit_bytes=VMEM_BYTES),
    )


def after(array, others):
    return pl.pallas_call(
        lambda *refs: None,
        out_shape=[jax.ShapeDtypeStruct(array.shape, array.dtype)],
        in_specs=[far()] * (1 + len(others)),
        out_specs=[far()],
        input_output_aliases={0: 0},
        compiler_params=pltpu.CompilerParams(vmem_limit_bytes=1024 * 1024),
    )(array, *others)


def local(
    pieces_image,
    pieces_variance,
    piece_patch,
    piece_cell,
    stamp_row,
    stamp_col,
    stamp_count,
    warp_offsets,
):
    patches = lax.axis_size("patch")
    subtiles = lax.axis_size("sub")
    _, pieces, cell_rows, col_count = pieces_image.shape
    visits = warp_offsets.shape[0]
    row_count = cell_rows * NCELL
    slots = stamp_row.shape[1]
    capacity = max(2, 2 * pieces // patches)
    direct = patches <= 8
    units = 2 * capacity
    sds = jax.ShapeDtypeStruct
    design_fixed, filters, edges, doubled = constants(visits, row_count, col_count)

    image_blocks = patches if direct else 1
    var_blocks = 1

    def sent(blocks, depth):
        return [sds((1 if blocks > 1 else patches, depth, 8, LANES), F32)] * blocks

    *images, stamps, warps, chosen = call(
        functools.partial(pack_kernel, (patches, capacity, pieces, image_blocks, slots)),
        sent(image_blocks, units + 1)
        + [sds((8, LANES), F32), sds((visits,), jnp.int32), sds((patches * capacity,), jnp.int32)],
        [vmem()] * (image_blocks + 1) + [smem()] * 2,
        [far()] * 7,
        [
            pltpu.VMEM((-(-patches // 8) * 8, LANES), F32),
            pltpu.SMEM((patches,), jnp.int32),
            pltpu.SMEM((1, pieces), jnp.int32),
            pltpu.SMEM((1, pieces), jnp.int32),
            pltpu.VMEM((1, slots), jnp.int32),
            pltpu.VMEM((1, slots), jnp.int32),
            pltpu.SMEM((1, 1), jnp.int32),
            pltpu.VMEM(pieces_image.shape, F32),
            pltpu.SemaphoreType.DMA((7,)),
        ],
    )(
        in_hbm(piece_patch[:, :, 0]),
        in_hbm(piece_cell),
        in_hbm(stamp_row),
        in_hbm(stamp_col),
        stamp_count,
        in_hbm(pieces_image),
        in_hbm(warp_offsets),
    )

    def route(blocks):
        if len(blocks) == 1:
            return [lax.all_to_all(blocks[0], "patch", split_axis=0, concat_axis=0, tiled=True)]
        result = list(blocks[:1])
        for away, block in zip(turn(patches)[1:], blocks[1:]):
            result.append(lax.ppermute(block, "patch", [(i, i ^ away) for i in range(patches)]))
        return result

    got = route(images)
    variances = call(
        functools.partial(pack_more_kernel, (patches, capacity, var_blocks)),
        sent(var_blocks, units),
        [vmem()] * var_blocks,
        [smem(), far()],
        [pltpu.VMEM(pieces_image.shape, F32), pltpu.SemaphoreType.DMA((1,))],
    )(chosen, in_hbm(pieces_variance))
    if direct:
        variances = after(variances[0], got[1:])
    got_var = route(variances)

    side = sds((visits * HALO + 8, col_count), F32)
    science, to_near, to_far, cells = call(
        functools.partial(image_kernel, (patches, capacity, visits, row_count, col_count, image_blocks)),
        [sds((visits, row_count, col_count), F32), side, side, sds((patches * capacity,), jnp.int32)],
        [vmem(), vmem(), vmem(), smem()],
        [smem()] + [vmem()] * (1 + image_blocks),
        [
            pltpu.VMEM((visits * NCELL + 1, 2, 8, LANES), F32),
            pltpu.SMEM((patches, LANES), F32),
            pltpu.SemaphoreType.DMA((patches,)),
        ],
    )(warps, stamps, *got)
    beside = [(i, i ^ 3) for i in range(subtiles) if abs(i - (i ^ 3)) == 1]
    from_far = lax.ppermute(to_far, "sub", beside)
    from_near = lax.ppermute(to_near, "sub", [(i, i ^ 1) for i in range(subtiles)])

    field = sds((TAP_COUNT, row_count + 2 * BLOCK, col_count), BF16)
    own_field = sds((TAP_COUNT, row_count, col_count), BF16)
    plane = sds((row_count, col_count), F32)
    wide = sds((visits, row_count + 2 * EDGE, col_count), F32)
    held, own_high, own_low, hits = call(
        functools.partial(own_kernel, (visits, row_count, col_count)),
        [sds(design_fixed.shape, BF16), own_field, own_field, plane],
        [vmem()] * 4,
        [vmem(), vmem(), far()],
        [pltpu.SemaphoreType.DMA((design_fixed.shape[0],))],
    )(science, stamps, in_hbm(design_fixed))
    design, mask, high, low, wide_science = call(
        functools.partial(design_kernel, (visits, row_count, col_count)),
        [sds((row_count, SLOTS, col_count), F32), plane] + [pltpu.HBM(part.shape, part.dtype) for part in (field, field, wide)],
        [vmem()] * 2 + [far()] * 3,
        [vmem()] * 7,
        [pltpu.VMEM(part.shape, part.dtype) for part in (field, field, wide)] + [pltpu.SemaphoreType.DMA((3,))],
    )(science, from_far, from_near, held, own_high, own_low, hits)

    gram_rows = visits // 2 * SLOTS
    tail_rows = visits * PR * (col_count // LANES)
    step = 32
    gram_depth = 2 * visits * (8 * len(TILES) - 4) + 3 * SLOTS + 16 - 2 * LANES
    variance, to_near, to_far, gram = call(
        functools.partial(gram_kernel, (patches, capacity, visits, row_count, col_count, var_blocks, step)),
        [
            sds((visits, row_count, col_count), F32),
            sds((gram_rows + tail_rows, LANES), F32),
            sds((gram_rows + tail_rows, LANES), F32),
            sds((gram_rows, LANES), F32),
        ],
        [vmem()] * 4,
        [smem(), smem(), vmem(), vmem()] + [vmem()] * var_blocks,
        [
            pltpu.VMEM((visits * NCELL + 1, 2, 8, LANES), F32),
            pltpu.VMEM((visits, row_count, col_count), F32),
            pltpu.VMEM((gram_depth, 2 * LANES), F32),
        ],
    )(warps, cells, mask, design, *got_var)
    grams = [gram]
    for away, part in ((3, to_far), (2, gram), (1, to_near)):
        grams.append(lax.ppermute(part, "sub", [(i, i ^ away) for i in range(subtiles)]))

    normalizer = subtiles * slots * (2 * SH + 1) ** 2
    result = sds((visits, 1, row_count, col_count), F32)
    kept = [filters, edges, doubled, wide_science, high, low]
    return call(
        functools.partial(solve_kernel, (visits, row_count, col_count, subtiles, float(normalizer), len(grams))),
        [result, result],
        [vmem(), vmem()],
        [vmem()] * (1 + len(grams)) + [far()] * len(kept),
        [pltpu.VMEM(wide.shape, F32)] + [pltpu.VMEM(part.shape, part.dtype) for part in kept] + [pltpu.SemaphoreType.DMA((len(kept),))],
    )(variance, *grams, *[in_hbm(part) for part in kept])


def solution(mesh):
    in_specs = (
        P("sub", "patch", None, None),
        P("sub", "patch", None, None),
        P("sub", "patch", None),
        P("sub", "patch"),
        P("patch", "sub"),
        P("patch", "sub"),
        P("patch", "sub"),
        P(),
    )
    out_specs = (P(None, "patch", "sub", None), P(None, "patch", "sub", None))
    return jax.shard_map(local, mesh=mesh, in_specs=in_specs, out_specs=out_specs, check_vma=False)
```

```python
import functools

import jax
import jax.numpy as jnp
import ml_dtypes
import numpy as np
from jax import lax
from jax.experimental import pallas as pl
from jax.experimental.pallas import tpu as pltpu
from jax.sharding import PartitionSpec as P

NCELL = 8
KR = 10
PR = 10
SH = 15
WARP = 4

SIGMAS = (0.75, 1.5, 3.0)
DEGREES = (4, 4, 3)
PSF_SIGMA = 2.0
SKY_VAR = 0.1
RIDGE = 0.5
EPS = 1e-05

F32 = jnp.float32
BF16 = jnp.bfloat16
LANES = 128
HALO = 24
EDGE = 16
BLOCK = 32
WINDOW = 64
VMEM_BYTES = 20 * 1024 * 1024

TILES = ((0, (0, 2)), (0, (1, 3, 4)), (1, (0, 2)), (1, (1, 3, 4)), (2, (0, 1, 3)), (2, (2,)))
SLOTS = 8 * len(TILES)
HALF = 64
TAP_FIRST = (0, DEGREES[0] + 1, DEGREES[0] + DEGREES[1] + 2)
TAP_COUNT = sum(DEGREES) + len(DEGREES)


def slot_table():
    result = {}
    for tile, (group, columns) in enumerate(TILES):
        slot = 8 * tile
        for column in columns:
            for row in range(DEGREES[group] + 1 - column):
                result[slot] = (TAP_FIRST[group] + row, TAP_FIRST[group] + column)
                slot += 1
    return result


SLOT_TAPS = slot_table()
ONE_SLOT = 8 * (len(TILES) - 1) + 2
SCI_SLOT = ONE_SLOT + 1
LIVE_SLOTS = sorted(SLOT_TAPS) + [ONE_SLOT]


def basis_taps():
    offset = np.arange(-KR, KR + 1, dtype=np.float64)
    rows = []
    for spread, degree in zip(SIGMAS, DEGREES):
        scaled = offset / spread
        envelope = np.exp(-0.5 * scaled * scaled)
        previous, current = np.zeros_like(scaled), np.ones_like(scaled)
        for term_no in range(degree + 1):
            rows.append(current * envelope)
            previous, current = current, scaled * current - term_no * previous
    taps = np.stack(rows)
    return taps / np.sqrt(np.sum(taps * taps, axis=1, keepdims=True))


def psf_taps():
    offset = np.arange(-PR, PR + 1, dtype=np.float64)
    values = np.exp(-0.5 * (offset / PSF_SIGMA) ** 2)
    return values / values.sum()


def band(taps, rows, columns, shift):
    radius = (taps.shape[-1] - 1) // 2
    offset = np.arange(columns)[None, :] - shift - np.arange(rows)[:, None]
    inside = np.abs(offset) <= radius
    return np.where(inside, taps[..., np.clip(offset + radius, 0, 2 * radius)], 0.0)


def halves(values):
    values = np.asarray(values, np.float32)
    high = values.astype(ml_dtypes.bfloat16)
    low = (values - high.astype(np.float32)).astype(ml_dtypes.bfloat16)
    return high, low


def tile_depth(tile, visits):
    depth = len(TILES[tile][1]) * WINDOW
    return depth + visits * BLOCK + 16 if tile == len(TILES) - 1 else depth


@functools.lru_cache(maxsize=None)
def constants(visits, row_count, col_count):
    taps = basis_taps()
    column_bands = np.stack([band(taps[t], col_count, col_count, 0).T for t in range(TAP_COUNT)])
    toeplitz = np.stack([band(taps[t], BLOCK, WINDOW, EDGE) for t in range(TAP_COUNT)])
    row_parts = []
    for tile, (group, columns) in enumerate(TILES):
        matrix = np.zeros((BLOCK, 8, tile_depth(tile, visits)))
        slot = 0
        for place, column in enumerate(columns):
            for row in range(DEGREES[group] + 1 - column):
                matrix[:, slot, place * WINDOW : (place + 1) * WINDOW] = toeplitz[TAP_FIRST[group] + row]
                slot += 1
        if tile == len(TILES) - 1:
            base = len(columns) * WINDOW
            for visit in range(visits):
                first = base + visit * BLOCK
                matrix[np.arange(BLOCK), slot + 1 + visit, first + np.arange(BLOCK)] = 1.0
            matrix[:, slot, base + visits * BLOCK] = 1.0
        row_parts.append(matrix.reshape(BLOCK * 8, -1))
    depth = col_count
    for tile, part in enumerate(row_parts):
        row_parts[tile] = np.pad(part, ((0, 0), (0, depth - part.shape[1])))
    design = np.stack(halves(np.concatenate([column_bands, np.stack(row_parts)])), axis=1)
    psf = psf_taps()
    filters = np.stack([half for power in (1, 2) for half in halves(band(psf**power, col_count, col_count, 0).T)])
    edges = np.stack(
        [half for power in (1, 2) for half in halves(band(psf**power, row_count, row_count + 2 * EDGE, EDGE))]
    )
    edges = np.pad(edges, ((0, 0), (0, 0), (0, -edges.shape[2] % LANES)))
    doubled = np.concatenate([toeplitz, toeplitz], axis=2).astype(np.float32)
    return design, filters, edges, doubled


def split(values):
    high = values.astype(BF16)
    return high, (values - high.astype(F32)).astype(BF16)


def mul(left, right):
    return jnp.dot(left, right, preferred_element_type=F32)


def mul3(left, right):
    return mul(left[0], right[0]) + mul(left[0], right[1]) + mul(left[1], right[0])


def mul_nt(left, right):
    return lax.dot_general(left, right, (((1,), (1,)), ((), ())), preferred_element_type=F32)


def turn(patches):
    half = patches // 2
    return [0, *(away for step in range(half) for away in (half + step, step + 1))][:patches]


def fill(cfg, outs, source, chosen_ref, table_ref):
    patches, capacity = cfg
    me = lax.axis_index("patch")
    for block in range(patches):
        if len(outs) == 1:
            out, place, away = outs[0], block, block ^ me
        else:
            out, place, away = outs[block], 0, turn(patches)[block]
        for rank in range(capacity):
            piece = chosen_ref[away * capacity + rank]
            out[place, 2 * rank] = source[0, piece, :, :LANES]
            out[place, 2 * rank + 1] = source[0, piece, :, LANES:]
        if table_ref is not None:
            out[place, 2 * capacity] = jnp.broadcast_to(table_ref[pl.ds(away, 1), :], (8, LANES))


def start_copies(pairs, sems):
    copies = [pltpu.make_async_copy(source, place, sems.at[number]) for number, (source, place) in enumerate(pairs)]
    for copy in copies:
        copy.start()
    return copies


def pack_kernel(cfg, *refs):
    patches, capacity, pieces, blocks, slots = cfg
    sources, refs = refs[:7], refs[7:]
    outs, refs = refs[:blocks], refs[blocks:]
    stamp_out, warp_out, chosen_ref, table_ref, count_ref, *held = refs
    held, sems = held[:-1], held[-1]
    target_ref, cell_ref, row_ref, col_ref, live_ref, image_ref = held
    copies = start_copies(
        zip(sources, (target_ref, cell_ref, row_ref, col_ref, live_ref, image_ref, warp_out)), sems
    )
    me = lax.axis_index("patch")
    for entry in range(patches * capacity):
        chosen_ref[entry] = 0
    for entry in range(patches):
        count_ref[entry] = 0
    line = lax.broadcasted_iota(jnp.int32, table_ref.shape, 0)
    lane = lax.broadcasted_iota(jnp.int32, table_ref.shape, 1)
    copies[0].wait()
    copies[1].wait()
    table = jnp.full(table_ref.shape, -1.0, F32)
    for piece in range(pieces):
        away = target_ref[0, piece] ^ me
        rank = count_ref[away]
        count_ref[away] = rank + 1
        chosen_ref[away * capacity + rank] = piece
        value = cell_ref[0, piece].astype(F32)
        table = jnp.where((line == away) & (lane == rank), value, table)
    table_ref[...] = table
    for copy in copies[2:5]:
        copy.wait()
    live = lax.broadcasted_iota(jnp.int32, (1, slots), 1) < live_ref[0, 0]
    stamp_out[...] = jnp.zeros(stamp_out.shape, F32)
    stamp_out[0:1, :slots] = row_ref[...].astype(F32)
    stamp_out[1:2, :slots] = col_ref[...].astype(F32)
    stamp_out[2:3, :slots] = jnp.where(live, 1.0, 0.0)
    copies[5].wait()
    fill((patches, capacity), outs, image_ref, chosen_ref, table_ref)
    copies[6].wait()


def pack_more_kernel(cfg, chosen_ref, var_hbm, *refs):
    patches, capacity, blocks = cfg
    outs, (var_ref, sems) = refs[:blocks], refs[blocks:]
    (copy,) = start_copies([(var_hbm, var_ref)], sems)
    copy.wait()
    fill((patches, capacity), outs, var_ref, chosen_ref, None)


def assemble(cfg, blocks, cells_ref, total_ref, me):
    patches, capacity = cfg
    total_ref[...] = jnp.zeros(total_ref.shape, F32)
    for block in range(patches):
        if len(blocks) == 1:
            ref, place, away = blocks[0], block, block ^ me
        else:
            ref, place, away = blocks[block], 0, turn(patches)[block]
        for rank in range(capacity):
            cell = cells_ref[away * capacity + rank]
            total_ref[cell, 0] += ref[place, 2 * rank]
            total_ref[cell, 1] += ref[place, 2 * rank + 1]


def warped(total_ref, visit, warp_ref, row_count, col_count):
    first = visit * NCELL
    left = total_ref[first : first + NCELL, 0].reshape(row_count, LANES)
    right = total_ref[first : first + NCELL, 1].reshape(row_count, LANES)
    plane = jnp.concatenate([left, right], axis=1)
    offset = warp_ref[visit] - WARP
    moved = pltpu.roll(plane, lax.rem(col_count - offset, col_count), 1)
    source = lax.broadcasted_iota(jnp.int32, plane.shape, 1) + offset
    return jnp.where((source >= 0) & (source < col_count), moved, 0.0)


def image_kernel(cfg, warp_ref, stamp_ref, *refs):
    patches, capacity, visits, row_count, col_count, block_count = cfg
    blocks = refs[:block_count]
    sci_ref, near_out, far_out, cells_ref, total_ref, near_ref, sems = refs[block_count:]
    me = lax.axis_index("patch")
    odd = lax.axis_index("sub") % 2 == 1
    copies = []
    for block in range(patches):
        ref, place = (blocks[0], block) if block_count == 1 else (blocks[block], 0)
        copies.append(
            pltpu.make_async_copy(
                ref.at[place, 2 * capacity, pl.ds(0, 1), :], near_ref.at[pl.ds(block, 1), :], sems.at[block]
            )
        )
    for copy in copies:
        copy.start()
    for copy in copies:
        copy.wait()
    for block in range(patches):
        away = block ^ me if block_count == 1 else turn(patches)[block]
        for rank in range(capacity):
            cell = near_ref[block, rank].astype(jnp.int32)
            cells_ref[away * capacity + rank] = jnp.where(cell < 0, visits * NCELL, cell)
    assemble((patches, capacity), blocks, cells_ref, total_ref, me)
    for visit in range(visits):
        plane = warped(total_ref, visit, warp_ref, row_count, col_count)
        sci_ref[visit] = plane
        top, bottom = plane[:HALO], plane[row_count - HALO :]
        near_out[visit * HALO : (visit + 1) * HALO] = jnp.where(odd, top, bottom)
        far_out[visit * HALO : (visit + 1) * HALO] = jnp.where(odd, bottom, top)
    first = visits * HALO
    for ref in (near_out, far_out):
        ref[first : first + 8, :LANES] = stamp_ref[...]
        ref[first : first + 8, LANES:] = jnp.zeros((8, col_count - LANES), F32)


def near_mask(stamps, shift, row_count, col_count):
    row_at = lax.broadcasted_iota(jnp.int32, (row_count, LANES), 0).astype(F32)
    col_at = lax.broadcasted_iota(jnp.int32, (col_count, LANES), 0).astype(F32)
    row_in = (jnp.abs(row_at - (stamps[0:1] + shift)) <= SH) & (stamps[2:3] > 0.5)
    col_in = jnp.abs(col_at - stamps[1:2]) <= SH
    return mul_nt(jnp.where(row_in, 1.0, 0.0).astype(BF16), jnp.where(col_in, 1.0, 0.0).astype(BF16))


def filter_columns(image, tap, held_ref):
    rows = image[0].shape[0]
    both = mul(jnp.concatenate(image, axis=0), held_ref[tap, 0])
    return split(both[:rows] + both[rows:] + mul(image[0], held_ref[tap, 1]))


def fetch_kernel(cfg, stamp_ref, fixed_ref, held_ref, hits_ref, sems):
    row_count, col_count = cfg
    copies = start_copies([(fixed_ref.at[n], held_ref.at[n]) for n in range(TAP_COUNT + len(TILES))], sems)
    hits_ref[...] = near_mask(stamp_ref[...], 0.0, row_count, col_count)
    for copy in copies:
        copy.wait()


def design_kernel(cfg, sci_ref, far_ref, near_ref, held_ref, hits_ref, *refs):
    visits, row_count, col_count = cfg
    design_ref, mask_ref, high_out, low_out, wide_out, high_ref, low_ref, wide_ref, sems = refs
    odd = lax.axis_index("sub") % 2 == 1

    def beside(first, count, lanes=slice(None)):
        near, far = near_ref[first : first + count, lanes], far_ref[first : first + count, lanes]
        return jnp.where(odd, near, far), jnp.where(odd, far, near)

    above, below = beside(0, HALO)
    own = sci_ref[0]
    for visit in range(1, visits):
        more = beside(visit * HALO, HALO)
        above, own, below = above + more[0], own + sci_ref[visit], below + more[1]
    rim = jnp.zeros((BLOCK - HALO, col_count), F32)
    template = split(jnp.concatenate([rim, above, own, below, rim], axis=0) * (1.0 / visits))
    for tap in range(TAP_COUNT):
        high_ref[tap], low_ref[tap] = filter_columns(template, tap, held_ref)
    for visit in range(visits):
        first = visit * HALO
        wide_ref[visit, :EDGE] = beside(first + HALO - EDGE, EDGE)[0]
        wide_ref[visit, EDGE : EDGE + row_count] = sci_ref[visit]
        wide_ref[visit, EDGE + row_count :] = beside(first, EDGE)[1]
    copies = start_copies(((high_ref, high_out), (low_ref, low_out), (wide_ref, wide_out)), sems)
    for block in range(row_count // BLOCK):
        start = EDGE + block * BLOCK
        for tile, (group, columns) in enumerate(TILES):
            depth = tile_depth(tile, visits)
            rows = [held_ref[TAP_COUNT + tile, half, :, :depth] for half in range(2)]
            taps = [TAP_FIRST[group] + column for column in columns]
            high = [high_ref[tap, start : start + WINDOW] for tap in taps]
            low = [low_ref[tap, start : start + WINDOW] for tap in taps]
            if tile == len(TILES) - 1:
                for visit in range(visits):
                    pair = split(sci_ref[visit, block * BLOCK : (block + 1) * BLOCK])
                    high.append(pair[0])
                    low.append(pair[1])
                high.append(jnp.ones((16, col_count), BF16))
                low.append(jnp.zeros((16, col_count), BF16))
            both = mul(jnp.concatenate(rows, axis=0), jnp.concatenate(high, axis=0))
            part = both[: 8 * BLOCK] + both[8 * BLOCK :] + mul(rows[0], jnp.concatenate(low, axis=0))
            design_ref[block * BLOCK : (block + 1) * BLOCK, 8 * tile : 8 * tile + 8] = part.reshape(
                BLOCK, 8, col_count
            )
    first = visits * HALO
    hits = hits_ref[...]
    for stamps, shift in zip(beside(first, 8, slice(LANES)), (-row_count, row_count)):
        hits = hits + near_mask(stamps, float(shift), row_count, col_count)
    mask_ref[...] = jnp.minimum(hits, 1.0)
    for copy in copies:
        copy.wait()


def gram_kernel(cfg, warp_ref, cells_ref, mask_ref, design_ref, *refs):
    patches, capacity, visits, row_count, col_count, block_count, step = cfg
    blocks = refs[:block_count]
    var_ref, near_ref, far_ref, gram_ref, total_ref, weight_ref, sum_ref = refs[block_count:]
    me = lax.axis_index("patch")
    odd = lax.axis_index("sub") % 2 == 1
    assemble((patches, capacity), blocks, cells_ref, total_ref, me)
    shared = jnp.full((row_count, col_count), SKY_VAR, F32)
    for visit in range(visits):
        plane = warped(total_ref, visit, warp_ref, row_count, col_count)
        var_ref[visit] = plane
        shared = shared + plane * (1.0 / (visits * visits))
    mask = mask_ref[...]
    for visit in range(visits):
        weight_ref[visit] = mask / (var_ref[visit] + shared)
    sum_ref[...] = jnp.zeros(sum_ref.shape, F32)

    body_rows, tail = 8 * (len(TILES) - 1), ONE_SLOT % 8 + 1
    rows = visits * body_rows + visits // 2 * 8
    kept = 2 * LANES - 2 * SLOTS - 16
    at_first = lax.broadcasted_iota(jnp.int32, (8, col_count), 0) < tail

    def body(number, carry):
        left, right = [], []
        for extra in range(step):
            row = number * step + extra
            design = design_ref[row]
            high, low = split(design)
            weights = [weight_ref[visit, pl.ds(row, 1), :] for visit in range(visits)]
            scaled = [design[:body_rows] * weight for weight in weights]
            last = design[body_rows:]
            moved = pltpu.roll(last, tail, 0)
            for pair in range(visits // 2):
                scaled.append(jnp.where(at_first, last * weights[2 * pair], moved * weights[2 * pair + 1]))
            scaled_high, scaled_low = split(jnp.concatenate(scaled, axis=0))
            blank = jnp.zeros((16, col_count), BF16)
            right.append(jnp.concatenate([high, low, scaled_low[:kept], blank], axis=0))
            left.append(jnp.concatenate([scaled_high, high, scaled_low[kept:]], axis=0))
        sum_ref[...] += mul_nt(jnp.concatenate(left, axis=1), jnp.concatenate(right, axis=1))
        return carry

    lax.fori_loop(0, row_count // step, body, 0)
    depth = sum_ref.shape[0]
    main = sum_ref[:rows, :LANES]
    turned = jnp.transpose(sum_ref[depth - LANES :, :])[2 * SLOTS : 2 * SLOTS + kept]
    turned = pltpu.roll(turned, depth - rows, 1)
    main = main + pltpu.roll(main, LANES - SLOTS, 1)
    main = main + jnp.concatenate([turned, sum_ref[rows + SLOTS :, :LANES]], axis=0)
    lane = lax.broadcasted_iota(jnp.int32, (SLOTS, 2 * HALF), 1)
    for pair in range(visits // 2):
        ends = main[visits * body_rows + 8 * pair :][:8]
        both = []
        for visit, end in ((2 * pair, ends), (2 * pair + 1, pltpu.roll(ends, 8 - tail, 0))):
            both.append(jnp.concatenate([main[visit * body_rows : (visit + 1) * body_rows], end], axis=0))
        value = jnp.where(lane < HALF, both[0], pltpu.roll(both[1], HALF, 1))
        for ref in (gram_ref, near_ref, far_ref):
            ref[pair * SLOTS : (pair + 1) * SLOTS] = value
    first = visits // 2 * SLOTS
    for visit in range(visits):
        for part in range(col_count // LANES):
            place = first + (visit * (col_count // LANES) + part) * PR
            lanes = slice(part * LANES, (part + 1) * LANES)
            top, bottom = var_ref[visit, :PR, lanes], var_ref[visit, row_count - PR :, lanes]
            near_ref[place : place + PR] = jnp.where(odd, top, bottom)
            far_ref[place : place + PR] = jnp.where(odd, bottom, top)


def solve_kernel(cfg, var_ref, *refs):
    visits, row_count, col_count, subtiles, normalizer, gram_count = cfg
    grams = refs[:gram_count]
    fixed = refs[gram_count : gram_count + 6]
    diff_out, sig_out, spread_ref, diff_ref, sig_ref, *held, sems, out_sems = refs[gram_count + 6 :]
    copies = start_copies(zip(fixed, held), sems)
    results = []
    filter_ref, edge_ref, doubled_ref, wide_ref, high_ref, low_ref = held
    sub = lax.axis_index("sub")
    high_rows = row_count + 2 * EDGE
    parts = col_count // LANES
    first = visits // 2 * SLOTS

    from_far, from_near = grams[1], grams[3]
    odd = sub % 2 == 1
    for visit in range(visits):
        spread_ref[visit, :EDGE] = jnp.zeros((EDGE, col_count), F32)
        spread_ref[visit, EDGE + row_count :] = jnp.zeros((EDGE, col_count), F32)
        spread_ref[visit, EDGE : EDGE + row_count] = var_ref[visit]
        for part in range(parts):
            place = first + (visit * parts + part) * PR
            lanes = slice(part * LANES, (part + 1) * LANES)
            near, far = from_near[place : place + PR], from_far[place : place + PR]
            spread_ref[visit, EDGE - PR : EDGE, lanes] = jnp.where(odd, near, far)
            spread_ref[visit, EDGE + row_count : EDGE + row_count + PR, lanes] = jnp.where(odd, far, near)
    row_at = lax.broadcasted_iota(jnp.int32, (high_rows, col_count), 0) + sub * row_count - EDGE
    inside = (row_at >= 0) & (row_at < subtiles * row_count)
    spread = [spread_ref[visit] for visit in range(visits)]
    shared = jnp.full((high_rows, col_count), SKY_VAR, F32)
    for visit in range(visits):
        shared = shared + spread[visit] * (1.0 / (visits * visits))
    inverse = [jnp.where(inside, 1.0 / (spread[visit] + shared), 0.0) for visit in range(visits)]

    def detected(images, kind):
        filtered = mul3(split(jnp.concatenate(images, axis=0)), (filter_ref[kind], filter_ref[kind + 1]))
        pair = split(filtered)
        rows = (edge_ref[kind, :, :high_rows], edge_ref[kind + 1, :, :high_rows])
        return [
            mul3(rows, (pair[0][v * high_rows : (v + 1) * high_rows], pair[1][v * high_rows : (v + 1) * high_rows]))
            for v in range(visits)
        ]

    lane = lax.broadcasted_iota(jnp.int32, (SLOTS, 2 * HALF), 1)
    line = lax.broadcasted_iota(jnp.int32, (SLOTS, 2 * HALF), 0)
    systems = []
    for pair in range(visits // 2):
        total = grams[0][pair * SLOTS : (pair + 1) * SLOTS]
        for ref in grams[1:]:
            total = total + ref[pair * SLOTS : (pair + 1) * SLOTS]
        diagonal = (lane == line) | (lane == line + HALF)
        systems.append(total + jnp.where(diagonal, RIDGE * total + RIDGE * EPS * normalizer, 0.0))
    pairs = range(visits // 2)
    tiles = [[matrix[8 * part : 8 * part + 8] for part in range(len(TILES))] for matrix in systems]
    line, lane = line[:8], lane[:8]
    for panel in range(len(TILES)):
        if panel == len(TILES) // 2:
            for copy in copies[:3]:
                copy.wait()
            noise = detected(inverse, 2)
        slots = [slot for slot in LIVE_SLOTS if slot // 8 == panel]
        place = {slot: jnp.where(lane < HALF, slot, HALF + slot) for slot in slots}
        columns = [
            {slot: [jnp.take_along_axis(tile, place[slot], axis=1) for tile in tiles[pair]] for slot in slots}
            for pair in pairs
        ]
        for number, slot in enumerate(slots):
            row = slot % 8
            at_row = line == row
            for pair in pairs:
                column = columns[pair][slot]
                scale = 1.0 / column[panel][row : row + 1]

                def eliminate(parts):
                    factor = parts[panel][row : row + 1] * scale
                    done = [part - column[index] * factor for index, part in enumerate(parts)]
                    done[panel] = jnp.where(at_row, factor, done[panel])
                    return done

                for later in slots[number + 1 :]:
                    columns[pair][later] = eliminate(columns[pair][later])
                tiles[pair] = eliminate(tiles[pair])
    for copy in copies[3:]:
        copy.wait()
    left = []
    offsets = []
    half_lane = lax.broadcasted_iota(jnp.int32, (BLOCK, 2 * HALF), 1) < HALF
    for pair in range(visits // 2):
        wanted = SCI_SLOT + 2 * pair
        place = jnp.where(lane < HALF, wanted, HALF + wanted + 1)
        solved = jnp.concatenate([jnp.take_along_axis(tile, place, axis=1) for tile in tiles[pair]], axis=0)
        mixes = [None] * TAP_COUNT
        for slot, (row_tap, col_tap) in SLOT_TAPS.items():
            term = solved[slot : slot + 1] * doubled_ref[row_tap]
            mixes[col_tap] = term if mixes[col_tap] is None else mixes[col_tap] + term
        own, other = [], []
        for tap in range(0, TAP_COUNT, 2):
            own.append(jnp.where(half_lane, mixes[tap], pltpu.roll(mixes[tap + 1], HALF, 1)))
            other.append(jnp.where(half_lane, pltpu.roll(mixes[tap], HALF, 1), mixes[tap + 1]))
        left += [jnp.concatenate(own, axis=1), jnp.concatenate(other, axis=1)]
        tail = solved[ONE_SLOT // 8 * 8 : ONE_SLOT // 8 * 8 + 8]
        for begin in (0, HALF):
            flat = jnp.take_along_axis(tail, jnp.full((8, LANES), begin, jnp.int32), axis=1)
            flat = flat[ONE_SLOT % 8 : ONE_SLOT % 8 + 1]
            offsets.append(jnp.concatenate([flat] * parts, axis=1))
    left = split(jnp.concatenate(left, axis=0))
    models = []
    for block in range(high_rows // BLOCK):
        start = block * BLOCK
        stack = tuple(
            jnp.concatenate([ref[tap, start : start + WINDOW] for tap in range(TAP_COUNT)], axis=0)
            for ref in (high_ref, low_ref)
        )
        models.append(mul3(left, stack))
    weighted = []
    for visit in range(visits):
        model = jnp.concatenate([part[visit * BLOCK : (visit + 1) * BLOCK] for part in models], axis=0)
        difference = wide_ref[visit] - model - offsets[visit]
        diff_ref[visit] = difference[EDGE : EDGE + row_count]
        results.append(pltpu.make_async_copy(diff_ref.at[visit], diff_out.at[visit, 0], out_sems.at[visit]))
        results[-1].start()
        weighted.append(difference * inverse[visit])
    signal = detected(weighted, 0)
    for visit in range(visits):
        sig_ref[visit] = signal[visit] * lax.rsqrt(noise[visit])
        results.append(pltpu.make_async_copy(sig_ref.at[visit], sig_out.at[visit, 0], out_sems.at[visits + visit]))
        results[-1].start()
    for copy in results:
        copy.wait()


def vmem():
    return pl.BlockSpec(memory_space=pltpu.VMEM)


def smem():
    return pl.BlockSpec(memory_space=pltpu.SMEM)


def far():
    return pl.BlockSpec(memory_space=pltpu.HBM)


def in_hbm(array):
    return pltpu.with_memory_space_constraint(jnp.asarray(array), pltpu.HBM)


def call(kernel, outs, out_specs, in_specs, scratch):
    return pl.pallas_call(
        kernel,
        out_shape=outs,
        in_specs=in_specs,
        out_specs=out_specs,
        scratch_shapes=scratch,
        compiler_params=pltpu.CompilerParams(vmem_limit_bytes=VMEM_BYTES),
    )


def after(array, others):
    return pl.pallas_call(
        lambda *refs: None,
        out_shape=[jax.ShapeDtypeStruct(array.shape, array.dtype)],
        in_specs=[far()] * (1 + len(others)),
        out_specs=[far()],
        input_output_aliases={0: 0},
        compiler_params=pltpu.CompilerParams(vmem_limit_bytes=1024 * 1024),
    )(array, *others)


def local(
    pieces_image,
    pieces_variance,
    piece_patch,
    piece_cell,
    stamp_row,
    stamp_col,
    stamp_count,
    warp_offsets,
):
    patches = lax.axis_size("patch")
    subtiles = lax.axis_size("sub")
    _, pieces, cell_rows, col_count = pieces_image.shape
    visits = warp_offsets.shape[0]
    row_count = cell_rows * NCELL
    slots = stamp_row.shape[1]
    capacity = max(2, 2 * pieces // patches)
    direct = patches <= 8
    units = 2 * capacity
    sds = jax.ShapeDtypeStruct
    design_fixed, filters, edges, doubled = constants(visits, row_count, col_count)

    image_blocks = patches if direct else 1
    var_blocks = 1

    def sent(blocks, depth):
        return [sds((1 if blocks > 1 else patches, depth, 8, LANES), F32)] * blocks

    *images, stamps, warps, chosen = call(
        functools.partial(pack_kernel, (patches, capacity, pieces, image_blocks, slots)),
        sent(image_blocks, units + 1)
        + [sds((8, LANES), F32), sds((visits,), jnp.int32), sds((patches * capacity,), jnp.int32)],
        [vmem()] * (image_blocks + 1) + [smem()] * 2,
        [far()] * 7,
        [
            pltpu.VMEM((-(-patches // 8) * 8, LANES), F32),
            pltpu.SMEM((patches,), jnp.int32),
            pltpu.SMEM((1, pieces), jnp.int32),
            pltpu.SMEM((1, pieces), jnp.int32),
            pltpu.VMEM((1, slots), jnp.int32),
            pltpu.VMEM((1, slots), jnp.int32),
            pltpu.SMEM((1, 1), jnp.int32),
            pltpu.VMEM(pieces_image.shape, F32),
            pltpu.SemaphoreType.DMA((7,)),
        ],
    )(
        in_hbm(piece_patch[:, :, 0]),
        in_hbm(piece_cell),
        in_hbm(stamp_row),
        in_hbm(stamp_col),
        stamp_count,
        in_hbm(pieces_image),
        in_hbm(warp_offsets),
    )

    def route(blocks):
        if len(blocks) == 1:
            return [lax.all_to_all(blocks[0], "patch", split_axis=0, concat_axis=0, tiled=True)]
        result = list(blocks[:1])
        for away, block in zip(turn(patches)[1:], blocks[1:]):
            result.append(lax.ppermute(block, "patch", [(i, i ^ away) for i in range(patches)]))
        return result

    got = route(images)
    variances = call(
        functools.partial(pack_more_kernel, (patches, capacity, var_blocks)),
        sent(var_blocks, units),
        [vmem()] * var_blocks,
        [smem(), far()],
        [pltpu.VMEM(pieces_image.shape, F32), pltpu.SemaphoreType.DMA((1,))],
    )(chosen, in_hbm(pieces_variance))
    if direct:
        variances = after(variances[0], got[1:])
    got_var = route(variances)

    side = sds((visits * HALO + 8, col_count), F32)
    science, to_near, to_far, cells = call(
        functools.partial(image_kernel, (patches, capacity, visits, row_count, col_count, image_blocks)),
        [sds((visits, row_count, col_count), F32), side, side, sds((patches * capacity,), jnp.int32)],
        [vmem(), vmem(), vmem(), smem()],
        [smem()] + [vmem()] * (1 + image_blocks),
        [
            pltpu.VMEM((visits * NCELL + 1, 2, 8, LANES), F32),
            pltpu.SMEM((patches, LANES), F32),
            pltpu.SemaphoreType.DMA((patches,)),
        ],
    )(warps, stamps, *got)
    beside = [(i, i ^ 3) for i in range(subtiles) if abs(i - (i ^ 3)) == 1]
    from_far = lax.ppermute(to_far, "sub", beside)
    from_near = lax.ppermute(to_near, "sub", [(i, i ^ 1) for i in range(subtiles)])

    field = sds((TAP_COUNT, row_count + 2 * BLOCK, col_count), BF16)
    plane = sds((row_count, col_count), F32)
    wide = sds((visits, row_count + 2 * EDGE, col_count), F32)
    held, hits = call(
        functools.partial(fetch_kernel, (row_count, col_count)),
        [sds(design_fixed.shape, BF16), plane],
        [vmem()] * 2,
        [vmem(), far()],
        [pltpu.SemaphoreType.DMA((design_fixed.shape[0],))],
    )(stamps, in_hbm(design_fixed))
    design, mask, high, low, wide_science = call(
        functools.partial(design_kernel, (visits, row_count, col_count)),
        [sds((row_count, SLOTS, col_count), F32), plane] + [pltpu.HBM(part.shape, part.dtype) for part in (field, field, wide)],
        [vmem()] * 2 + [far()] * 3,
        [vmem()] * 5,
        [pltpu.VMEM(part.shape, part.dtype) for part in (field, field, wide)] + [pltpu.SemaphoreType.DMA((3,))],
    )(science, from_far, from_near, held, hits)

    gram_rows = visits // 2 * SLOTS
    tail_rows = visits * PR * (col_count // LANES)
    step = 32
    gram_depth = 2 * visits * (8 * len(TILES) - 4) + 3 * SLOTS + 16 - 2 * LANES
    variance, to_near, to_far, gram = call(
        functools.partial(gram_kernel, (patches, capacity, visits, row_count, col_count, var_blocks, step)),
        [
            sds((visits, row_count, col_count), F32),
            sds((gram_rows + tail_rows, LANES), F32),
            sds((gram_rows + tail_rows, LANES), F32),
            sds((gram_rows, LANES), F32),
        ],
        [vmem()] * 4,
        [smem(), smem(), vmem(), vmem()] + [vmem()] * var_blocks,
        [
            pltpu.VMEM((visits * NCELL + 1, 2, 8, LANES), F32),
            pltpu.VMEM((visits, row_count, col_count), F32),
            pltpu.VMEM((gram_depth, 2 * LANES), F32),
        ],
    )(warps, cells, mask, design, *got_var)
    grams = [gram]
    for away, part in ((3, to_far), (2, gram), (1, to_near)):
        grams.append(lax.ppermute(part, "sub", [(i, i ^ away) for i in range(subtiles)]))

    normalizer = subtiles * slots * (2 * SH + 1) ** 2
    result = sds((visits, 1, row_count, col_count), F32)
    kept = [filters, edges, doubled, wide_science, high, low]
    return call(
        functools.partial(solve_kernel, (visits, row_count, col_count, subtiles, float(normalizer), len(grams))),
        [result, result],
        [far(), far()],
        [vmem()] * (1 + len(grams)) + [far()] * len(kept),
        [pltpu.VMEM(wide.shape, F32)]
        + [pltpu.VMEM((visits, row_count, col_count), F32)] * 2
        + [pltpu.VMEM(part.shape, part.dtype) for part in kept]
        + [pltpu.SemaphoreType.DMA((len(kept),)), pltpu.SemaphoreType.DMA((2 * visits,))],
    )(variance, *grams, *[in_hbm(part) for part in kept])


def solution(mesh):
    in_specs = (
        P("sub", "patch", None, None),
        P("sub", "patch", None, None),
        P("sub", "patch", None),
        P("sub", "patch"),
        P("patch", "sub"),
        P("patch", "sub"),
        P("patch", "sub"),
        P(),
    )
    out_specs = (P(None, "patch", "sub", None), P(None, "patch", "sub", None))
    return jax.shard_map(local, mesh=mesh, in_specs=in_specs, out_specs=out_specs, check_vma=False)
```

```python
import functools

import jax
import jax.numpy as jnp
import ml_dtypes
import numpy as np
from jax import lax
from jax.experimental import pallas as pl
from jax.experimental.pallas import tpu as pltpu
from jax.sharding import PartitionSpec as P

NCELL = 8
KR = 10
PR = 10
SH = 15
WARP = 4

SIGMAS = (0.75, 1.5, 3.0)
DEGREES = (4, 4, 3)
PSF_SIGMA = 2.0
SKY_VAR = 0.1
RIDGE = 0.5
EPS = 1e-05

F32 = jnp.float32
BF16 = jnp.bfloat16
LANES = 128
HALO = 24
EDGE = 16
BLOCK = 32
WINDOW = 64
VMEM_BYTES = 20 * 1024 * 1024

TILES = (
    ((0, 0, range(5)), (0, 2, range(3))),
    ((0, 1, range(4)), (0, 3, range(2)), (0, 4, range(1)), (2, 2, range(1))),
    ((1, 0, range(5)), (1, 2, range(3))),
    ((1, 1, range(4)), (1, 3, range(2)), (1, 4, range(1)), (2, 2, range(1, 2))),
    ((2, 0, range(4)), (2, 1, range(3)), (2, 3, range(1))),
)
BASIS = 8 * len(TILES)
SLOTS = BASIS + 8
HALF = 64
TAP_FIRST = (0, DEGREES[0] + 1, DEGREES[0] + DEGREES[1] + 2)
TAP_COUNT = sum(DEGREES) + len(DEGREES)


def slot_table():
    result = {}
    for tile, entries in enumerate(TILES):
        taps = [(TAP_FIRST[group] + row, TAP_FIRST[group] + column) for group, column, rows in entries for row in rows]
        result.update({8 * tile + place: pair for place, pair in enumerate(taps)})
    return result


SLOT_TAPS = slot_table()
ONE_SLOT = BASIS
SCI_SLOT = ONE_SLOT + 1
LIVE_SLOTS = sorted(SLOT_TAPS) + [ONE_SLOT]


def basis_taps():
    offset = np.arange(-KR, KR + 1, dtype=np.float64)
    rows = []
    for spread, degree in zip(SIGMAS, DEGREES):
        scaled = offset / spread
        envelope = np.exp(-0.5 * scaled * scaled)
        previous, current = np.zeros_like(scaled), np.ones_like(scaled)
        for term_no in range(degree + 1):
            rows.append(current * envelope)
            previous, current = current, scaled * current - term_no * previous
    taps = np.stack(rows)
    return taps / np.sqrt(np.sum(taps * taps, axis=1, keepdims=True))


def psf_taps():
    offset = np.arange(-PR, PR + 1, dtype=np.float64)
    values = np.exp(-0.5 * (offset / PSF_SIGMA) ** 2)
    return values / values.sum()


def band(taps, rows, columns, shift):
    radius = (taps.shape[-1] - 1) // 2
    offset = np.arange(columns)[None, :] - shift - np.arange(rows)[:, None]
    inside = np.abs(offset) <= radius
    return np.where(inside, taps[..., np.clip(offset + radius, 0, 2 * radius)], 0.0)


def halves(values):
    values = np.asarray(values, np.float32)
    high = values.astype(ml_dtypes.bfloat16)
    low = (values - high.astype(np.float32)).astype(ml_dtypes.bfloat16)
    return high, low


@functools.lru_cache(maxsize=None)
def constants(visits, row_count, col_count):
    taps = basis_taps()
    column_bands = np.stack([band(taps[t], col_count, col_count, 0).T for t in range(TAP_COUNT)])
    toeplitz = np.stack([band(taps[t], BLOCK, WINDOW, EDGE) for t in range(TAP_COUNT)])
    row_parts = []
    for entries in TILES:
        matrix = np.zeros((BLOCK, 8, len(entries) * WINDOW))
        slot = 0
        for place, (group, _, rows) in enumerate(entries):
            for row in rows:
                matrix[:, slot, place * WINDOW : (place + 1) * WINDOW] = toeplitz[TAP_FIRST[group] + row]
                slot += 1
        row_parts.append(matrix.reshape(BLOCK * 8, -1))
    depth = col_count
    for tile, part in enumerate(row_parts):
        row_parts[tile] = np.pad(part, ((0, 0), (0, depth - part.shape[1])))
    design = np.stack(halves(np.concatenate([column_bands, np.stack(row_parts)])), axis=1)
    psf = psf_taps()
    filters = np.stack([half for power in (1, 2) for half in halves(band(psf**power, col_count, col_count, 0).T)])
    edges = np.stack(
        [half for power in (1, 2) for half in halves(band(psf**power, row_count, row_count + 2 * EDGE, EDGE))]
    )
    edges = np.pad(edges, ((0, 0), (0, 0), (0, -edges.shape[2] % LANES)))
    doubled = np.concatenate([toeplitz, toeplitz], axis=2).astype(np.float32)
    return design, filters, edges, doubled


def split(values):
    high = values.astype(BF16)
    return high, (values - high.astype(F32)).astype(BF16)


def mul(left, right):
    return jnp.dot(left, right, preferred_element_type=F32)


def mul3(left, right):
    return mul(left[0], right[0]) + mul(left[0], right[1]) + mul(left[1], right[0])


def mul_nt(left, right):
    return lax.dot_general(left, right, (((1,), (1,)), ((), ())), preferred_element_type=F32)


def turn(patches):
    half = patches // 2
    return [0, *(away for step in range(half) for away in (half + step, step + 1))][:patches]


def fill(cfg, outs, source, chosen_ref, table_ref):
    patches, capacity = cfg
    me = lax.axis_index("patch")
    for block in range(patches):
        if len(outs) == 1:
            out, place, away = outs[0], block, block ^ me
        else:
            out, place, away = outs[block], 0, turn(patches)[block]
        for rank in range(capacity):
            piece = chosen_ref[away * capacity + rank]
            out[place, 2 * rank] = source[0, piece, :, :LANES]
            out[place, 2 * rank + 1] = source[0, piece, :, LANES:]
        if table_ref is not None:
            out[place, 2 * capacity] = jnp.broadcast_to(table_ref[pl.ds(away, 1), :], (8, LANES))


def start_copies(pairs, sems):
    copies = [pltpu.make_async_copy(source, place, sems.at[number]) for number, (source, place) in enumerate(pairs)]
    for copy in copies:
        copy.start()
    return copies


def pack_kernel(cfg, *refs):
    patches, capacity, pieces, blocks, slots = cfg
    sources, refs = refs[:7], refs[7:]
    outs, refs = refs[:blocks], refs[blocks:]
    stamp_out, warp_out, chosen_ref, table_ref, count_ref, *held = refs
    held, sems = held[:-1], held[-1]
    target_ref, cell_ref, row_ref, col_ref, live_ref, image_ref = held
    copies = start_copies(
        zip(sources, (target_ref, cell_ref, row_ref, col_ref, live_ref, image_ref, warp_out)), sems
    )
    me = lax.axis_index("patch")
    for entry in range(patches * capacity):
        chosen_ref[entry] = 0
    for entry in range(patches):
        count_ref[entry] = 0
    line = lax.broadcasted_iota(jnp.int32, table_ref.shape, 0)
    lane = lax.broadcasted_iota(jnp.int32, table_ref.shape, 1)
    copies[0].wait()
    copies[1].wait()
    table = jnp.full(table_ref.shape, -1.0, F32)
    for piece in range(pieces):
        away = target_ref[0, piece] ^ me
        rank = count_ref[away]
        count_ref[away] = rank + 1
        chosen_ref[away * capacity + rank] = piece
        value = cell_ref[0, piece].astype(F32)
        table = jnp.where((line == away) & (lane == rank), value, table)
    table_ref[...] = table
    for copy in copies[2:5]:
        copy.wait()
    live = lax.broadcasted_iota(jnp.int32, (1, slots), 1) < live_ref[0, 0]
    stamp_out[...] = jnp.zeros(stamp_out.shape, F32)
    stamp_out[0:1, :slots] = row_ref[...].astype(F32)
    stamp_out[1:2, :slots] = col_ref[...].astype(F32)
    stamp_out[2:3, :slots] = jnp.where(live, 1.0, 0.0)
    copies[5].wait()
    fill((patches, capacity), outs, image_ref, chosen_ref, table_ref)
    copies[6].wait()


def pack_more_kernel(cfg, chosen_ref, var_hbm, *refs):
    patches, capacity, blocks = cfg
    outs, (var_ref, sems) = refs[:blocks], refs[blocks:]
    (copy,) = start_copies([(var_hbm, var_ref)], sems)
    copy.wait()
    fill((patches, capacity), outs, var_ref, chosen_ref, None)


def assemble(cfg, blocks, cells_ref, total_ref, me):
    patches, capacity = cfg
    total_ref[...] = jnp.zeros(total_ref.shape, F32)
    for block in range(patches):
        if len(blocks) == 1:
            ref, place, away = blocks[0], block, block ^ me
        else:
            ref, place, away = blocks[block], 0, turn(patches)[block]
        for rank in range(capacity):
            cell = cells_ref[away * capacity + rank]
            total_ref[cell, 0] += ref[place, 2 * rank]
            total_ref[cell, 1] += ref[place, 2 * rank + 1]


def warped(total_ref, visit, warp_ref, row_count, col_count):
    first = visit * NCELL
    left = total_ref[first : first + NCELL, 0].reshape(row_count, LANES)
    right = total_ref[first : first + NCELL, 1].reshape(row_count, LANES)
    plane = jnp.concatenate([left, right], axis=1)
    offset = warp_ref[visit] - WARP
    moved = pltpu.roll(plane, lax.rem(col_count - offset, col_count), 1)
    source = lax.broadcasted_iota(jnp.int32, plane.shape, 1) + offset
    return jnp.where((source >= 0) & (source < col_count), moved, 0.0)


def image_kernel(cfg, warp_ref, stamp_ref, *refs):
    patches, capacity, visits, row_count, col_count, block_count = cfg
    blocks = refs[:block_count]
    sci_ref, near_out, far_out, cells_ref, total_ref, near_ref, sems = refs[block_count:]
    me = lax.axis_index("patch")
    odd = lax.axis_index("sub") % 2 == 1
    copies = []
    for block in range(patches):
        ref, place = (blocks[0], block) if block_count == 1 else (blocks[block], 0)
        copies.append(
            pltpu.make_async_copy(
                ref.at[place, 2 * capacity, pl.ds(0, 1), :], near_ref.at[pl.ds(block, 1), :], sems.at[block]
            )
        )
    for copy in copies:
        copy.start()
    for copy in copies:
        copy.wait()
    for block in range(patches):
        away = block ^ me if block_count == 1 else turn(patches)[block]
        for rank in range(capacity):
            cell = near_ref[block, rank].astype(jnp.int32)
            cells_ref[away * capacity + rank] = jnp.where(cell < 0, visits * NCELL, cell)
    assemble((patches, capacity), blocks, cells_ref, total_ref, me)
    for visit in range(visits):
        plane = warped(total_ref, visit, warp_ref, row_count, col_count)
        sci_ref[visit] = plane
        top, bottom = plane[:HALO], plane[row_count - HALO :]
        near_out[visit * HALO : (visit + 1) * HALO] = jnp.where(odd, top, bottom)
        far_out[visit * HALO : (visit + 1) * HALO] = jnp.where(odd, bottom, top)
    first = visits * HALO
    for ref in (near_out, far_out):
        ref[first : first + 8, :LANES] = stamp_ref[...]
        ref[first : first + 8, LANES:] = jnp.zeros((8, col_count - LANES), F32)


def near_mask(stamps, shift, row_count, col_count):
    row_at = lax.broadcasted_iota(jnp.int32, (row_count, LANES), 0).astype(F32)
    col_at = lax.broadcasted_iota(jnp.int32, (col_count, LANES), 0).astype(F32)
    row_in = (jnp.abs(row_at - (stamps[0:1] + shift)) <= SH) & (stamps[2:3] > 0.5)
    col_in = jnp.abs(col_at - stamps[1:2]) <= SH
    return mul_nt(jnp.where(row_in, 1.0, 0.0).astype(BF16), jnp.where(col_in, 1.0, 0.0).astype(BF16))


def filter_columns(image, tap, held_ref):
    rows = image[0].shape[0]
    both = mul(jnp.concatenate(image, axis=0), held_ref[tap, 0])
    return split(both[:rows] + both[rows:] + mul(image[0], held_ref[tap, 1]))


def fetch_kernel(cfg, stamp_ref, fixed_ref, held_ref, hits_ref, sems):
    row_count, col_count = cfg
    copies = start_copies([(fixed_ref.at[n], held_ref.at[n]) for n in range(TAP_COUNT + len(TILES))], sems)
    hits_ref[...] = near_mask(stamp_ref[...], 0.0, row_count, col_count)
    for copy in copies:
        copy.wait()


def design_kernel(cfg, sci_ref, far_ref, near_ref, held_ref, hits_ref, *refs):
    visits, row_count, col_count = cfg
    design_ref, mask_ref, high_out, low_out, wide_out, high_ref, low_ref, wide_ref, sems = refs
    odd = lax.axis_index("sub") % 2 == 1

    def beside(first, count, lanes=slice(None)):
        near, far = near_ref[first : first + count, lanes], far_ref[first : first + count, lanes]
        return jnp.where(odd, near, far), jnp.where(odd, far, near)

    above, below = beside(0, HALO)
    own = sci_ref[0]
    for visit in range(1, visits):
        more = beside(visit * HALO, HALO)
        above, own, below = above + more[0], own + sci_ref[visit], below + more[1]
    rim = jnp.zeros((BLOCK - HALO, col_count), F32)
    template = split(jnp.concatenate([rim, above, own, below, rim], axis=0) * (1.0 / visits))
    for tap in range(TAP_COUNT):
        high_ref[tap], low_ref[tap] = filter_columns(template, tap, held_ref)
    for visit in range(visits):
        first = visit * HALO
        wide_ref[visit, :EDGE] = beside(first + HALO - EDGE, EDGE)[0]
        wide_ref[visit, EDGE : EDGE + row_count] = sci_ref[visit]
        wide_ref[visit, EDGE + row_count :] = beside(first, EDGE)[1]
    copies = start_copies(((high_ref, high_out), (low_ref, low_out), (wide_ref, wide_out)), sems)
    for block in range(row_count // BLOCK):
        start = EDGE + block * BLOCK
        for tile, entries in enumerate(TILES):
            rows = [held_ref[TAP_COUNT + tile, half, :, : len(entries) * WINDOW] for half in range(2)]
            taps = [TAP_FIRST[group] + column for group, column, _ in entries]
            high = [high_ref[tap, start : start + WINDOW] for tap in taps]
            low = [low_ref[tap, start : start + WINDOW] for tap in taps]
            both = mul(jnp.concatenate(rows, axis=0), jnp.concatenate(high, axis=0))
            part = both[: 8 * BLOCK] + both[8 * BLOCK :] + mul(rows[0], jnp.concatenate(low, axis=0))
            design_ref[block * BLOCK : (block + 1) * BLOCK, 8 * tile : 8 * tile + 8] = part.reshape(
                BLOCK, 8, col_count
            )
    first = visits * HALO
    hits = hits_ref[...]
    for stamps, shift in zip(beside(first, 8, slice(LANES)), (-row_count, row_count)):
        hits = hits + near_mask(stamps, float(shift), row_count, col_count)
    mask_ref[...] = jnp.minimum(hits, 1.0)
    for copy in copies:
        copy.wait()


def gram_kernel(cfg, warp_ref, cells_ref, mask_ref, sci_ref, design_ref, *refs):
    patches, capacity, visits, row_count, col_count, block_count, step = cfg
    blocks = refs[:block_count]
    var_ref, near_ref, far_ref, gram_ref, total_ref, weight_ref, sum_ref = refs[block_count:]
    me = lax.axis_index("patch")
    odd = lax.axis_index("sub") % 2 == 1
    assemble((patches, capacity), blocks, cells_ref, total_ref, me)
    shared = jnp.full((row_count, col_count), SKY_VAR, F32)
    for visit in range(visits):
        plane = warped(total_ref, visit, warp_ref, row_count, col_count)
        var_ref[visit] = plane
        shared = shared + plane * (1.0 / (visits * visits))
    mask = mask_ref[...]
    for visit in range(visits):
        weight_ref[visit] = mask / (var_ref[visit] + shared)
    sum_ref[...] = jnp.zeros(sum_ref.shape, F32)

    rows = visits * BASIS + visits // 2 * 8
    kept = 2 * LANES - 2 * SLOTS - 16
    line = lax.broadcasted_iota(jnp.int32, (8, col_count), 0)

    def body(number, carry):
        left, right = [], []
        for extra in range(step):
            row = number * step + extra
            design = design_ref[row]
            last = jnp.ones((8, col_count), F32)
            for visit in range(visits):
                last = jnp.where(line == SCI_SLOT - BASIS + visit, sci_ref[visit, pl.ds(row, 1), :], last)
            high, low = split(jnp.concatenate([design, last], axis=0))
            weights = [weight_ref[visit, pl.ds(row, 1), :] for visit in range(visits)]
            scaled = [design * weight for weight in weights]
            for pair in range(visits // 2):
                scaled.append(jnp.where(line == 0, weights[2 * pair], weights[2 * pair + 1]))
            scaled_high, scaled_low = split(jnp.concatenate(scaled, axis=0))
            blank = jnp.zeros((16, col_count), BF16)
            right.append(jnp.concatenate([high, low, scaled_low[:kept], blank], axis=0))
            left.append(jnp.concatenate([scaled_high, high, scaled_low[kept:]], axis=0))
        sum_ref[...] += mul_nt(jnp.concatenate(left, axis=1), jnp.concatenate(right, axis=1))
        return carry

    lax.fori_loop(0, row_count // step, body, 0)
    depth = sum_ref.shape[0]
    main = sum_ref[:rows, :LANES]
    turned = jnp.transpose(sum_ref[depth - LANES :, :])[2 * SLOTS : 2 * SLOTS + kept]
    turned = pltpu.roll(turned, depth - rows, 1)
    main = main + pltpu.roll(main, LANES - SLOTS, 1)
    main = main + jnp.concatenate([turned, sum_ref[rows + SLOTS :, :LANES]], axis=0)
    lane = lax.broadcasted_iota(jnp.int32, (SLOTS, 2 * HALF), 1)
    for pair in range(visits // 2):
        ends = main[visits * BASIS + 8 * pair :][:8]
        both = []
        for visit, end in ((2 * pair, ends), (2 * pair + 1, pltpu.roll(ends, 7, 0))):
            both.append(jnp.concatenate([main[visit * BASIS : (visit + 1) * BASIS], end], axis=0))
        value = jnp.where(lane < HALF, both[0], pltpu.roll(both[1], HALF, 1))
        for ref in (gram_ref, near_ref, far_ref):
            ref[pair * SLOTS : (pair + 1) * SLOTS] = value
    first = visits // 2 * SLOTS
    for visit in range(visits):
        for part in range(col_count // LANES):
            place = first + (visit * (col_count // LANES) + part) * PR
            lanes = slice(part * LANES, (part + 1) * LANES)
            top, bottom = var_ref[visit, :PR, lanes], var_ref[visit, row_count - PR :, lanes]
            near_ref[place : place + PR] = jnp.where(odd, top, bottom)
            far_ref[place : place + PR] = jnp.where(odd, bottom, top)


def solve_kernel(cfg, var_ref, *refs):
    visits, row_count, col_count, subtiles, normalizer, gram_count = cfg
    grams = refs[:gram_count]
    fixed = refs[gram_count : gram_count + 6]
    diff_out, sig_out, spread_ref, diff_ref, sig_ref, *held, sems, out_sems = refs[gram_count + 6 :]
    copies = start_copies(zip(fixed, held), sems)
    results = []
    filter_ref, edge_ref, doubled_ref, wide_ref, high_ref, low_ref = held
    sub = lax.axis_index("sub")
    high_rows = row_count + 2 * EDGE
    parts = col_count // LANES
    first = visits // 2 * SLOTS

    from_far, from_near = grams[1], grams[3]
    odd = sub % 2 == 1
    for visit in range(visits):
        spread_ref[visit, :EDGE] = jnp.zeros((EDGE, col_count), F32)
        spread_ref[visit, EDGE + row_count :] = jnp.zeros((EDGE, col_count), F32)
        spread_ref[visit, EDGE : EDGE + row_count] = var_ref[visit]
        for part in range(parts):
            place = first + (visit * parts + part) * PR
            lanes = slice(part * LANES, (part + 1) * LANES)
            near, far = from_near[place : place + PR], from_far[place : place + PR]
            spread_ref[visit, EDGE - PR : EDGE, lanes] = jnp.where(odd, near, far)
            spread_ref[visit, EDGE + row_count : EDGE + row_count + PR, lanes] = jnp.where(odd, far, near)
    row_at = lax.broadcasted_iota(jnp.int32, (high_rows, col_count), 0) + sub * row_count - EDGE
    inside = (row_at >= 0) & (row_at < subtiles * row_count)
    spread = [spread_ref[visit] for visit in range(visits)]
    shared = jnp.full((high_rows, col_count), SKY_VAR, F32)
    for visit in range(visits):
        shared = shared + spread[visit] * (1.0 / (visits * visits))
    inverse = [jnp.where(inside, 1.0 / (spread[visit] + shared), 0.0) for visit in range(visits)]

    def detected(images, kind):
        filtered = mul3(split(jnp.concatenate(images, axis=0)), (filter_ref[kind], filter_ref[kind + 1]))
        pair = split(filtered)
        rows = (edge_ref[kind, :, :high_rows], edge_ref[kind + 1, :, :high_rows])
        return [
            mul3(rows, (pair[0][v * high_rows : (v + 1) * high_rows], pair[1][v * high_rows : (v + 1) * high_rows]))
            for v in range(visits)
        ]

    lane = lax.broadcasted_iota(jnp.int32, (SLOTS, 2 * HALF), 1)
    line = lax.broadcasted_iota(jnp.int32, (SLOTS, 2 * HALF), 0)
    systems = []
    for pair in range(visits // 2):
        total = grams[0][pair * SLOTS : (pair + 1) * SLOTS]
        for ref in grams[1:]:
            total = total + ref[pair * SLOTS : (pair + 1) * SLOTS]
        diagonal = (lane == line) | (lane == line + HALF)
        systems.append(total + jnp.where(diagonal, RIDGE * total + RIDGE * EPS * normalizer, 0.0))
    pairs = range(visits // 2)
    tiles = [[matrix[8 * part : 8 * part + 8] for part in range(SLOTS // 8)] for matrix in systems]
    line, lane = line[:8], lane[:8]
    for panel in range(SLOTS // 8):
        if panel == 3:
            for copy in copies[:3]:
                copy.wait()
            noise = detected(inverse, 2)
        slots = [slot for slot in LIVE_SLOTS if slot // 8 == panel]
        place = {slot: jnp.where(lane < HALF, slot, HALF + slot) for slot in slots}
        columns = [
            {slot: [jnp.take_along_axis(tile, place[slot], axis=1) for tile in tiles[pair]] for slot in slots}
            for pair in pairs
        ]
        for number, slot in enumerate(slots):
            row = slot % 8
            at_row = line == row
            for pair in pairs:
                column = columns[pair][slot]
                scale = 1.0 / column[panel][row : row + 1]

                def eliminate(parts):
                    factor = parts[panel][row : row + 1] * scale
                    done = [part - column[index] * factor for index, part in enumerate(parts)]
                    done[panel] = jnp.where(at_row, factor, done[panel])
                    return done

                for later in slots[number + 1 :]:
                    columns[pair][later] = eliminate(columns[pair][later])
                tiles[pair] = eliminate(tiles[pair])
    for copy in copies[3:]:
        copy.wait()
    left = []
    offsets = []
    half_lane = lax.broadcasted_iota(jnp.int32, (BLOCK, 2 * HALF), 1) < HALF
    for pair in range(visits // 2):
        wanted = SCI_SLOT + 2 * pair
        place = jnp.where(lane < HALF, wanted, HALF + wanted + 1)
        solved = jnp.concatenate([jnp.take_along_axis(tile, place, axis=1) for tile in tiles[pair]], axis=0)
        mixes = [None] * TAP_COUNT
        for slot, (row_tap, col_tap) in SLOT_TAPS.items():
            term = solved[slot : slot + 1] * doubled_ref[row_tap]
            mixes[col_tap] = term if mixes[col_tap] is None else mixes[col_tap] + term
        own, other = [], []
        for tap in range(0, TAP_COUNT, 2):
            own.append(jnp.where(half_lane, mixes[tap], pltpu.roll(mixes[tap + 1], HALF, 1)))
            other.append(jnp.where(half_lane, pltpu.roll(mixes[tap], HALF, 1), mixes[tap + 1]))
        left += [jnp.concatenate(own, axis=1), jnp.concatenate(other, axis=1)]
        tail = solved[ONE_SLOT // 8 * 8 : ONE_SLOT // 8 * 8 + 8]
        for begin in (0, HALF):
            flat = jnp.take_along_axis(tail, jnp.full((8, LANES), begin, jnp.int32), axis=1)
            flat = flat[ONE_SLOT % 8 : ONE_SLOT % 8 + 1]
            offsets.append(jnp.concatenate([flat] * parts, axis=1))
    left = split(jnp.concatenate(left, axis=0))
    models = []
    for block in range(high_rows // BLOCK):
        start = block * BLOCK
        stack = tuple(
            jnp.concatenate([ref[tap, start : start + WINDOW] for tap in range(TAP_COUNT)], axis=0)
            for ref in (high_ref, low_ref)
        )
        models.append(mul3(left, stack))
    weighted = []
    for visit in range(visits):
        model = jnp.concatenate([part[visit * BLOCK : (visit + 1) * BLOCK] for part in models], axis=0)
        difference = wide_ref[visit] - model - offsets[visit]
        diff_ref[visit] = difference[EDGE : EDGE + row_count]
        results.append(pltpu.make_async_copy(diff_ref.at[visit], diff_out.at[visit, 0], out_sems.at[visit]))
        results[-1].start()
        weighted.append(difference * inverse[visit])
    signal = detected(weighted, 0)
    for visit in range(visits):
        sig_ref[visit] = signal[visit] * lax.rsqrt(noise[visit])
        results.append(pltpu.make_async_copy(sig_ref.at[visit], sig_out.at[visit, 0], out_sems.at[visits + visit]))
        results[-1].start()
    for copy in results:
        copy.wait()


def vmem():
    return pl.BlockSpec(memory_space=pltpu.VMEM)


def smem():
    return pl.BlockSpec(memory_space=pltpu.SMEM)


def far():
    return pl.BlockSpec(memory_space=pltpu.HBM)


def in_hbm(array):
    return pltpu.with_memory_space_constraint(jnp.asarray(array), pltpu.HBM)


def call(kernel, outs, out_specs, in_specs, scratch):
    return pl.pallas_call(
        kernel,
        out_shape=outs,
        in_specs=in_specs,
        out_specs=out_specs,
        scratch_shapes=scratch,
        compiler_params=pltpu.CompilerParams(vmem_limit_bytes=VMEM_BYTES),
    )


def after(array, others):
    return pl.pallas_call(
        lambda *refs: None,
        out_shape=[jax.ShapeDtypeStruct(array.shape, array.dtype)],
        in_specs=[far()] * (1 + len(others)),
        out_specs=[far()],
        input_output_aliases={0: 0},
        compiler_params=pltpu.CompilerParams(vmem_limit_bytes=1024 * 1024),
    )(array, *others)


def local(
    pieces_image,
    pieces_variance,
    piece_patch,
    piece_cell,
    stamp_row,
    stamp_col,
    stamp_count,
    warp_offsets,
):
    patches = lax.axis_size("patch")
    subtiles = lax.axis_size("sub")
    _, pieces, cell_rows, col_count = pieces_image.shape
    visits = warp_offsets.shape[0]
    row_count = cell_rows * NCELL
    slots = stamp_row.shape[1]
    capacity = max(2, 2 * pieces // patches)
    direct = patches <= 8
    units = 2 * capacity
    sds = jax.ShapeDtypeStruct
    design_fixed, filters, edges, doubled = constants(visits, row_count, col_count)

    image_blocks = patches if direct else 1
    var_blocks = 1

    def sent(blocks, depth):
        return [sds((1 if blocks > 1 else patches, depth, 8, LANES), F32)] * blocks

    *images, stamps, warps, chosen = call(
        functools.partial(pack_kernel, (patches, capacity, pieces, image_blocks, slots)),
        sent(image_blocks, units + 1)
        + [sds((8, LANES), F32), sds((visits,), jnp.int32), sds((patches * capacity,), jnp.int32)],
        [vmem()] * (image_blocks + 1) + [smem()] * 2,
        [far()] * 7,
        [
            pltpu.VMEM((-(-patches // 8) * 8, LANES), F32),
            pltpu.SMEM((patches,), jnp.int32),
            pltpu.SMEM((1, pieces), jnp.int32),
            pltpu.SMEM((1, pieces), jnp.int32),
            pltpu.VMEM((1, slots), jnp.int32),
            pltpu.VMEM((1, slots), jnp.int32),
            pltpu.SMEM((1, 1), jnp.int32),
            pltpu.VMEM(pieces_image.shape, F32),
            pltpu.SemaphoreType.DMA((7,)),
        ],
    )(
        in_hbm(piece_patch[:, :, 0]),
        in_hbm(piece_cell),
        in_hbm(stamp_row),
        in_hbm(stamp_col),
        stamp_count,
        in_hbm(pieces_image),
        in_hbm(warp_offsets),
    )

    def route(blocks):
        if len(blocks) == 1:
            return [lax.all_to_all(blocks[0], "patch", split_axis=0, concat_axis=0, tiled=True)]
        result = list(blocks[:1])
        for away, block in zip(turn(patches)[1:], blocks[1:]):
            result.append(lax.ppermute(block, "patch", [(i, i ^ away) for i in range(patches)]))
        return result

    got = route(images)
    variances = call(
        functools.partial(pack_more_kernel, (patches, capacity, var_blocks)),
        sent(var_blocks, units),
        [vmem()] * var_blocks,
        [smem(), far()],
        [pltpu.VMEM(pieces_image.shape, F32), pltpu.SemaphoreType.DMA((1,))],
    )(chosen, in_hbm(pieces_variance))
    if direct:
        variances = after(variances[0], got[1:])
    got_var = route(variances)

    side = sds((visits * HALO + 8, col_count), F32)
    science, to_near, to_far, cells = call(
        functools.partial(image_kernel, (patches, capacity, visits, row_count, col_count, image_blocks)),
        [sds((visits, row_count, col_count), F32), side, side, sds((patches * capacity,), jnp.int32)],
        [vmem(), vmem(), vmem(), smem()],
        [smem()] + [vmem()] * (1 + image_blocks),
        [
            pltpu.VMEM((visits * NCELL + 1, 2, 8, LANES), F32),
            pltpu.SMEM((patches, LANES), F32),
            pltpu.SemaphoreType.DMA((patches,)),
        ],
    )(warps, stamps, *got)
    beside = [(i, i ^ 3) for i in range(subtiles) if abs(i - (i ^ 3)) == 1]
    from_far = lax.ppermute(to_far, "sub", beside)
    from_near = lax.ppermute(to_near, "sub", [(i, i ^ 1) for i in range(subtiles)])

    field = sds((TAP_COUNT, row_count + 2 * BLOCK, col_count), BF16)
    plane = sds((row_count, col_count), F32)
    wide = sds((visits, row_count + 2 * EDGE, col_count), F32)
    held, hits = call(
        functools.partial(fetch_kernel, (row_count, col_count)),
        [sds(design_fixed.shape, BF16), plane],
        [vmem()] * 2,
        [vmem(), far()],
        [pltpu.SemaphoreType.DMA((design_fixed.shape[0],))],
    )(stamps, in_hbm(design_fixed))
    design, mask, high, low, wide_science = call(
        functools.partial(design_kernel, (visits, row_count, col_count)),
        [sds((row_count, BASIS, col_count), F32), plane] + [pltpu.HBM(part.shape, part.dtype) for part in (field, field, wide)],
        [vmem()] * 2 + [far()] * 3,
        [vmem()] * 5,
        [pltpu.VMEM(part.shape, part.dtype) for part in (field, field, wide)] + [pltpu.SemaphoreType.DMA((3,))],
    )(science, from_far, from_near, held, hits)

    gram_rows = visits // 2 * SLOTS
    tail_rows = visits * PR * (col_count // LANES)
    step = 32
    gram_depth = 2 * visits * (BASIS + 4) + 3 * SLOTS + 16 - 2 * LANES
    variance, to_near, to_far, gram = call(
        functools.partial(gram_kernel, (patches, capacity, visits, row_count, col_count, var_blocks, step)),
        [
            sds((visits, row_count, col_count), F32),
            sds((gram_rows + tail_rows, LANES), F32),
            sds((gram_rows + tail_rows, LANES), F32),
            sds((gram_rows, LANES), F32),
        ],
        [vmem()] * 4,
        [smem(), smem()] + [vmem()] * (3 + var_blocks),
        [
            pltpu.VMEM((visits * NCELL + 1, 2, 8, LANES), F32),
            pltpu.VMEM((visits, row_count, col_count), F32),
            pltpu.VMEM((gram_depth, 2 * LANES), F32),
        ],
    )(warps, cells, mask, science, design, *got_var)
    grams = [gram]
    for away, part in ((3, to_far), (2, gram), (1, to_near)):
        grams.append(lax.ppermute(part, "sub", [(i, i ^ away) for i in range(subtiles)]))

    normalizer = subtiles * slots * (2 * SH + 1) ** 2
    result = sds((visits, 1, row_count, col_count), F32)
    kept = [filters, edges, doubled, wide_science, high, low]
    return call(
        functools.partial(solve_kernel, (visits, row_count, col_count, subtiles, float(normalizer), len(grams))),
        [result, result],
        [far(), far()],
        [vmem()] * (1 + len(grams)) + [far()] * len(kept),
        [pltpu.VMEM(wide.shape, F32)]
        + [pltpu.VMEM((visits, row_count, col_count), F32)] * 2
        + [pltpu.VMEM(part.shape, part.dtype) for part in kept]
        + [pltpu.SemaphoreType.DMA((len(kept),)), pltpu.SemaphoreType.DMA((2 * visits,))],
    )(variance, *grams, *[in_hbm(part) for part in kept])


def solution(mesh):
    in_specs = (
        P("sub", "patch", None, None),
        P("sub", "patch", None, None),
        P("sub", "patch", None),
        P("sub", "patch"),
        P("patch", "sub"),
        P("patch", "sub"),
        P("patch", "sub"),
        P(),
    )
    out_specs = (P(None, "patch", "sub", None), P(None, "patch", "sub", None))
    return jax.shard_map(local, mesh=mesh, in_specs=in_specs, out_specs=out_specs, check_vma=False)
```

```python
import functools

import jax
import jax.numpy as jnp
import ml_dtypes
import numpy as np
from jax import lax
from jax.experimental import pallas as pl
from jax.experimental.pallas import tpu as pltpu
from jax.sharding import PartitionSpec as P

NCELL = 8
KR = 10
PR = 10
SH = 15
WARP = 4

SIGMAS = (0.75, 1.5, 3.0)
DEGREES = (4, 4, 3)
PSF_SIGMA = 2.0
SKY_VAR = 0.1
RIDGE = 0.5
EPS = 1e-05

F32 = jnp.float32
BF16 = jnp.bfloat16
LANES = 128
HALO = 24
EDGE = 16
BLOCK = 32
WINDOW = 64
VMEM_BYTES = 20 * 1024 * 1024

TILES = (
    ((0, 0, range(5)), (0, 2, range(3))),
    ((0, 1, range(4)), (0, 3, range(2)), (0, 4, range(1)), (2, 2, range(1))),
    ((1, 0, range(5)), (1, 2, range(3))),
    ((1, 1, range(4)), (1, 3, range(2)), (1, 4, range(1)), (2, 2, range(1, 2))),
    ((2, 0, range(4)), (2, 1, range(3)), (2, 3, range(1))),
)
BASIS = 8 * len(TILES)
SLOTS = BASIS + 8
HALF = 64
TAP_FIRST = (0, DEGREES[0] + 1, DEGREES[0] + DEGREES[1] + 2)
TAP_COUNT = sum(DEGREES) + len(DEGREES)


def slot_table():
    result = {}
    for tile, entries in enumerate(TILES):
        taps = [(TAP_FIRST[group] + row, TAP_FIRST[group] + column) for group, column, rows in entries for row in rows]
        result.update({8 * tile + place: pair for place, pair in enumerate(taps)})
    return result


SLOT_TAPS = slot_table()
ONE_SLOT = BASIS
SCI_SLOT = ONE_SLOT + 1
LIVE_SLOTS = sorted(SLOT_TAPS) + [ONE_SLOT]


def basis_taps():
    offset = np.arange(-KR, KR + 1, dtype=np.float64)
    rows = []
    for spread, degree in zip(SIGMAS, DEGREES):
        scaled = offset / spread
        envelope = np.exp(-0.5 * scaled * scaled)
        previous, current = np.zeros_like(scaled), np.ones_like(scaled)
        for term_no in range(degree + 1):
            rows.append(current * envelope)
            previous, current = current, scaled * current - term_no * previous
    taps = np.stack(rows)
    return taps / np.sqrt(np.sum(taps * taps, axis=1, keepdims=True))


def psf_taps():
    offset = np.arange(-PR, PR + 1, dtype=np.float64)
    values = np.exp(-0.5 * (offset / PSF_SIGMA) ** 2)
    return values / values.sum()


def band(taps, rows, columns, shift):
    radius = (taps.shape[-1] - 1) // 2
    offset = np.arange(columns)[None, :] - shift - np.arange(rows)[:, None]
    inside = np.abs(offset) <= radius
    return np.where(inside, taps[..., np.clip(offset + radius, 0, 2 * radius)], 0.0)


def halves(values):
    values = np.asarray(values, np.float32)
    high = values.astype(ml_dtypes.bfloat16)
    low = (values - high.astype(np.float32)).astype(ml_dtypes.bfloat16)
    return high, low


@functools.lru_cache(maxsize=None)
def constants(visits, row_count, col_count):
    taps = basis_taps()
    column_bands = np.stack([band(taps[t], col_count, col_count, 0).T for t in range(TAP_COUNT)])
    toeplitz = np.stack([band(taps[t], BLOCK, WINDOW, EDGE) for t in range(TAP_COUNT)])
    row_parts = []
    for entries in TILES:
        matrix = np.zeros((BLOCK, 8, len(entries) * WINDOW))
        slot = 0
        for place, (group, _, rows) in enumerate(entries):
            for row in rows:
                matrix[:, slot, place * WINDOW : (place + 1) * WINDOW] = toeplitz[TAP_FIRST[group] + row]
                slot += 1
        row_parts.append(matrix.reshape(BLOCK * 8, -1))
    depth = col_count
    for tile, part in enumerate(row_parts):
        row_parts[tile] = np.pad(part, ((0, 0), (0, depth - part.shape[1])))
    design = np.stack(halves(np.concatenate([column_bands, np.stack(row_parts)])), axis=1)
    psf = psf_taps()
    filters = np.stack([half for power in (1, 2) for half in halves(band(psf**power, col_count, col_count, 0).T)])
    edges = np.stack(
        [half for power in (1, 2) for half in halves(band(psf**power, row_count, row_count + 2 * EDGE, EDGE))]
    )
    edges = np.pad(edges, ((0, 0), (0, 0), (0, -edges.shape[2] % LANES)))
    doubled = np.concatenate([toeplitz, toeplitz], axis=2).astype(np.float32)
    return design, filters, edges, doubled


def split(values):
    high = values.astype(BF16)
    return high, (values - high.astype(F32)).astype(BF16)


def mul(left, right):
    return jnp.dot(left, right, preferred_element_type=F32)


def mul3(left, right):
    return mul(left[0], right[0]) + mul(left[0], right[1]) + mul(left[1], right[0])


def mul_nt(left, right):
    return lax.dot_general(left, right, (((1,), (1,)), ((), ())), preferred_element_type=F32)


def turn(patches):
    half = patches // 2
    return [0, *(away for step in range(half) for away in (half + step, step + 1))][:patches]


def fill(cfg, outs, source, chosen_ref, table_ref):
    patches, capacity = cfg
    me = lax.axis_index("patch")
    for block in range(patches):
        if len(outs) == 1:
            out, place, away = outs[0], block, block ^ me
        else:
            out, place, away = outs[block], 0, turn(patches)[block]
        for rank in range(capacity):
            piece = chosen_ref[away * capacity + rank]
            out[place, 2 * rank] = source[0, piece, :, :LANES]
            out[place, 2 * rank + 1] = source[0, piece, :, LANES:]
        if table_ref is not None:
            out[place, 2 * capacity] = jnp.broadcast_to(table_ref[pl.ds(away, 1), :], (8, LANES))


def start_copies(pairs, sems):
    copies = [pltpu.make_async_copy(source, place, sems.at[number]) for number, (source, place) in enumerate(pairs)]
    for copy in copies:
        copy.start()
    return copies


def pack_kernel(cfg, *refs):
    patches, capacity, pieces, blocks, slots = cfg
    sources, refs = refs[:7], refs[7:]
    outs, refs = refs[:blocks], refs[blocks:]
    stamp_out, warp_out, chosen_ref, table_ref, count_ref, *held = refs
    held, sems = held[:-1], held[-1]
    target_ref, cell_ref, row_ref, col_ref, live_ref, image_ref = held
    copies = start_copies(
        zip(sources, (target_ref, cell_ref, row_ref, col_ref, live_ref, image_ref, warp_out)), sems
    )
    me = lax.axis_index("patch")
    for entry in range(patches * capacity):
        chosen_ref[entry] = 0
    for entry in range(patches):
        count_ref[entry] = 0
    line = lax.broadcasted_iota(jnp.int32, table_ref.shape, 0)
    lane = lax.broadcasted_iota(jnp.int32, table_ref.shape, 1)
    copies[0].wait()
    copies[1].wait()
    table = jnp.full(table_ref.shape, -1.0, F32)
    for piece in range(pieces):
        away = target_ref[0, piece] ^ me
        rank = count_ref[away]
        count_ref[away] = rank + 1
        chosen_ref[away * capacity + rank] = piece
        value = cell_ref[0, piece].astype(F32)
        table = jnp.where((line == away) & (lane == rank), value, table)
    table_ref[...] = table
    for copy in copies[2:5]:
        copy.wait()
    live = lax.broadcasted_iota(jnp.int32, (1, slots), 1) < live_ref[0, 0]
    stamp_out[...] = jnp.zeros(stamp_out.shape, F32)
    stamp_out[0:1, :slots] = row_ref[...].astype(F32)
    stamp_out[1:2, :slots] = col_ref[...].astype(F32)
    stamp_out[2:3, :slots] = jnp.where(live, 1.0, 0.0)
    copies[5].wait()
    fill((patches, capacity), outs, image_ref, chosen_ref, table_ref)
    copies[6].wait()


def pack_more_kernel(cfg, chosen_ref, var_hbm, *refs):
    patches, capacity, blocks = cfg
    outs, (var_ref, sems) = refs[:blocks], refs[blocks:]
    (copy,) = start_copies([(var_hbm, var_ref)], sems)
    copy.wait()
    fill((patches, capacity), outs, var_ref, chosen_ref, None)


def assemble(cfg, blocks, cells_ref, total_ref, me):
    patches, capacity = cfg
    total_ref[...] = jnp.zeros(total_ref.shape, F32)
    for block in range(patches):
        if len(blocks) == 1:
            ref, place, away = blocks[0], block, block ^ me
        else:
            ref, place, away = blocks[block], 0, turn(patches)[block]
        for rank in range(capacity):
            cell = cells_ref[away * capacity + rank]
            total_ref[cell, 0] += ref[place, 2 * rank]
            total_ref[cell, 1] += ref[place, 2 * rank + 1]


def warped(total_ref, visit, warp_ref, row_count, col_count):
    first = visit * NCELL
    left = total_ref[first : first + NCELL, 0].reshape(row_count, LANES)
    right = total_ref[first : first + NCELL, 1].reshape(row_count, LANES)
    plane = jnp.concatenate([left, right], axis=1)
    offset = warp_ref[visit] - WARP
    moved = pltpu.roll(plane, lax.rem(col_count - offset, col_count), 1)
    source = lax.broadcasted_iota(jnp.int32, plane.shape, 1) + offset
    return jnp.where((source >= 0) & (source < col_count), moved, 0.0)


def image_kernel(cfg, warp_ref, stamp_ref, *refs):
    patches, capacity, visits, row_count, col_count, block_count = cfg
    blocks = refs[:block_count]
    sci_ref, near_out, far_out, cells_ref, total_ref, near_ref, sems = refs[block_count:]
    me = lax.axis_index("patch")
    odd = lax.axis_index("sub") % 2 == 1
    copies = []
    for block in range(patches):
        ref, place = (blocks[0], block) if block_count == 1 else (blocks[block], 0)
        copies.append(
            pltpu.make_async_copy(
                ref.at[place, 2 * capacity, pl.ds(0, 1), :], near_ref.at[pl.ds(block, 1), :], sems.at[block]
            )
        )
    for copy in copies:
        copy.start()
    for copy in copies:
        copy.wait()
    for block in range(patches):
        away = block ^ me if block_count == 1 else turn(patches)[block]
        for rank in range(capacity):
            cell = near_ref[block, rank].astype(jnp.int32)
            cells_ref[away * capacity + rank] = jnp.where(cell < 0, visits * NCELL, cell)
    assemble((patches, capacity), blocks, cells_ref, total_ref, me)
    for visit in range(visits):
        plane = warped(total_ref, visit, warp_ref, row_count, col_count)
        sci_ref[visit] = plane
        top, bottom = plane[:HALO], plane[row_count - HALO :]
        near_out[visit * HALO : (visit + 1) * HALO] = jnp.where(odd, top, bottom)
        far_out[visit * HALO : (visit + 1) * HALO] = jnp.where(odd, bottom, top)
    first = visits * HALO
    for ref in (near_out, far_out):
        ref[first : first + 8, :LANES] = stamp_ref[...]
        ref[first : first + 8, LANES:] = jnp.zeros((8, col_count - LANES), F32)


def near_mask(stamps, shift, row_count, col_count):
    row_at = lax.broadcasted_iota(jnp.int32, (row_count, LANES), 0).astype(F32)
    col_at = lax.broadcasted_iota(jnp.int32, (col_count, LANES), 0).astype(F32)
    row_in = (jnp.abs(row_at - (stamps[0:1] + shift)) <= SH) & (stamps[2:3] > 0.5)
    col_in = jnp.abs(col_at - stamps[1:2]) <= SH
    return mul_nt(jnp.where(row_in, 1.0, 0.0).astype(BF16), jnp.where(col_in, 1.0, 0.0).astype(BF16))


def filter_columns(image, tap, held_ref):
    rows = image[0].shape[0]
    both = mul(jnp.concatenate(image, axis=0), held_ref[tap, 0])
    return split(both[:rows] + both[rows:] + mul(image[0], held_ref[tap, 1]))


def fetch_kernel(cfg, stamp_ref, fixed_ref, held_ref, hits_ref, sems):
    row_count, col_count = cfg
    copies = start_copies([(fixed_ref.at[n], held_ref.at[n]) for n in range(TAP_COUNT + len(TILES))], sems)
    hits_ref[...] = near_mask(stamp_ref[...], 0.0, row_count, col_count)
    for copy in copies:
        copy.wait()


def design_kernel(cfg, sci_ref, far_ref, near_ref, held_ref, hits_ref, *refs):
    visits, row_count, col_count = cfg
    design_ref, mask_ref, high_out, low_out, wide_out, high_ref, low_ref, wide_ref, sems = refs
    odd = lax.axis_index("sub") % 2 == 1

    def beside(first, count, lanes=slice(None)):
        near, far = near_ref[first : first + count, lanes], far_ref[first : first + count, lanes]
        return jnp.where(odd, near, far), jnp.where(odd, far, near)

    above, below = beside(0, HALO)
    own = sci_ref[0]
    for visit in range(1, visits):
        more = beside(visit * HALO, HALO)
        above, own, below = above + more[0], own + sci_ref[visit], below + more[1]
    rim = jnp.zeros((BLOCK - HALO, col_count), F32)
    template = split(jnp.concatenate([rim, above, own, below, rim], axis=0) * (1.0 / visits))
    for tap in range(TAP_COUNT):
        high_ref[tap], low_ref[tap] = filter_columns(template, tap, held_ref)
    for visit in range(visits):
        first = visit * HALO
        wide_ref[visit, :EDGE] = beside(first + HALO - EDGE, EDGE)[0]
        wide_ref[visit, EDGE : EDGE + row_count] = sci_ref[visit]
        wide_ref[visit, EDGE + row_count :] = beside(first, EDGE)[1]
    copies = start_copies(((high_ref, high_out), (low_ref, low_out), (wide_ref, wide_out)), sems)
    for block in range(row_count // BLOCK):
        start = EDGE + block * BLOCK
        for tile, entries in enumerate(TILES):
            rows = [held_ref[TAP_COUNT + tile, half, :, : len(entries) * WINDOW] for half in range(2)]
            taps = [TAP_FIRST[group] + column for group, column, _ in entries]
            high = [high_ref[tap, start : start + WINDOW] for tap in taps]
            low = [low_ref[tap, start : start + WINDOW] for tap in taps]
            both = mul(jnp.concatenate(rows, axis=0), jnp.concatenate(high, axis=0))
            part = both[: 8 * BLOCK] + both[8 * BLOCK :] + mul(rows[0], jnp.concatenate(low, axis=0))
            design_ref[block * BLOCK : (block + 1) * BLOCK, 8 * tile : 8 * tile + 8] = part.reshape(
                BLOCK, 8, col_count
            )
    first = visits * HALO
    hits = hits_ref[...]
    for stamps, shift in zip(beside(first, 8, slice(LANES)), (-row_count, row_count)):
        hits = hits + near_mask(stamps, float(shift), row_count, col_count)
    mask_ref[...] = jnp.minimum(hits, 1.0)
    for copy in copies:
        copy.wait()


def gram_kernel(cfg, warp_ref, cells_ref, mask_ref, sci_ref, design_ref, *refs):
    patches, capacity, visits, row_count, col_count, block_count, step = cfg
    blocks = refs[:block_count]
    var_ref, near_ref, far_ref, gram_ref, total_ref, weight_ref, sum_ref = refs[block_count:]
    me = lax.axis_index("patch")
    odd = lax.axis_index("sub") % 2 == 1
    assemble((patches, capacity), blocks, cells_ref, total_ref, me)
    shared = jnp.full((row_count, col_count), SKY_VAR, F32)
    for visit in range(visits):
        plane = warped(total_ref, visit, warp_ref, row_count, col_count)
        var_ref[visit] = plane
        shared = shared + plane * (1.0 / (visits * visits))
    mask = mask_ref[...]
    for visit in range(visits):
        weight_ref[visit] = mask / (var_ref[visit] + shared)
    sum_ref[...] = jnp.zeros(sum_ref.shape, F32)

    rows = visits * BASIS + visits // 2 * 8
    kept = 2 * LANES - 2 * SLOTS - 16
    line = lax.broadcasted_iota(jnp.int32, (8, col_count), 0)

    def body(number, carry):
        left, right = [], []
        for extra in range(step):
            row = number * step + extra
            design = design_ref[row]
            last = jnp.ones((8, col_count), F32)
            for visit in range(visits):
                last = jnp.where(line == SCI_SLOT - BASIS + visit, sci_ref[visit, pl.ds(row, 1), :], last)
            high, low = split(jnp.concatenate([design, last], axis=0))
            weights = [weight_ref[visit, pl.ds(row, 1), :] for visit in range(visits)]
            scaled = [design * weight for weight in weights]
            for pair in range(visits // 2):
                scaled.append(jnp.where(line == 0, weights[2 * pair], weights[2 * pair + 1]))
            scaled_high, scaled_low = split(jnp.concatenate(scaled, axis=0))
            blank = jnp.zeros((16, col_count), BF16)
            right.append(jnp.concatenate([high, low, scaled_low[:kept], blank], axis=0))
            left.append(jnp.concatenate([scaled_high, high, scaled_low[kept:]], axis=0))
        sum_ref[...] += mul_nt(jnp.concatenate(left, axis=1), jnp.concatenate(right, axis=1))
        return carry

    lax.fori_loop(0, row_count // step, body, 0)
    depth = sum_ref.shape[0]
    main = sum_ref[:rows, :LANES]
    turned = jnp.transpose(sum_ref[depth - LANES :, :])[2 * SLOTS : 2 * SLOTS + kept]
    turned = pltpu.roll(turned, depth - rows, 1)
    main = main + pltpu.roll(main, LANES - SLOTS, 1)
    main = main + jnp.concatenate([turned, sum_ref[rows + SLOTS :, :LANES]], axis=0)
    lane = lax.broadcasted_iota(jnp.int32, (SLOTS, 2 * HALF), 1)
    for pair in range(visits // 2):
        ends = main[visits * BASIS + 8 * pair :][:8]
        both = []
        for visit, end in ((2 * pair, ends), (2 * pair + 1, pltpu.roll(ends, 7, 0))):
            both.append(jnp.concatenate([main[visit * BASIS : (visit + 1) * BASIS], end], axis=0))
        value = jnp.where(lane < HALF, both[0], pltpu.roll(both[1], HALF, 1))
        for ref in (gram_ref, near_ref, far_ref):
            ref[pair * SLOTS : (pair + 1) * SLOTS] = value
    first = visits // 2 * SLOTS
    for visit in range(visits):
        for part in range(col_count // LANES):
            place = first + (visit * (col_count // LANES) + part) * PR
            lanes = slice(part * LANES, (part + 1) * LANES)
            top, bottom = var_ref[visit, :PR, lanes], var_ref[visit, row_count - PR :, lanes]
            near_ref[place : place + PR] = jnp.where(odd, top, bottom)
            far_ref[place : place + PR] = jnp.where(odd, bottom, top)


def solve_kernel(cfg, var_ref, *refs):
    visits, row_count, col_count, subtiles, normalizer, gram_count = cfg
    grams = refs[:gram_count]
    fixed = refs[gram_count : gram_count + 6]
    diff_out, sig_out, spread_ref, diff_ref, sig_ref, *held, sems, out_sems = refs[gram_count + 6 :]
    copies = start_copies(zip(fixed, held), sems)
    results = []
    filter_ref, edge_ref, doubled_ref, wide_ref, high_ref, low_ref = held
    sub = lax.axis_index("sub")
    high_rows = row_count + 2 * EDGE
    parts = col_count // LANES
    first = visits // 2 * SLOTS

    from_far, from_near = grams[1], grams[3]
    odd = sub % 2 == 1
    for visit in range(visits):
        spread_ref[visit, :EDGE] = jnp.zeros((EDGE, col_count), F32)
        spread_ref[visit, EDGE + row_count :] = jnp.zeros((EDGE, col_count), F32)
        spread_ref[visit, EDGE : EDGE + row_count] = var_ref[visit]
        for part in range(parts):
            place = first + (visit * parts + part) * PR
            lanes = slice(part * LANES, (part + 1) * LANES)
            near, far = from_near[place : place + PR], from_far[place : place + PR]
            spread_ref[visit, EDGE - PR : EDGE, lanes] = jnp.where(odd, near, far)
            spread_ref[visit, EDGE + row_count : EDGE + row_count + PR, lanes] = jnp.where(odd, far, near)
    row_at = lax.broadcasted_iota(jnp.int32, (high_rows, col_count), 0) + sub * row_count - EDGE
    inside = (row_at >= 0) & (row_at < subtiles * row_count)
    spread = [spread_ref[visit] for visit in range(visits)]
    shared = jnp.full((high_rows, col_count), SKY_VAR, F32)
    for visit in range(visits):
        shared = shared + spread[visit] * (1.0 / (visits * visits))
    inverse = [jnp.where(inside, 1.0 / (spread[visit] + shared), 0.0) for visit in range(visits)]

    def detected(images, kind):
        filtered = mul3(split(jnp.concatenate(images, axis=0)), (filter_ref[kind], filter_ref[kind + 1]))
        pair = split(filtered)
        rows = (edge_ref[kind, :, :high_rows], edge_ref[kind + 1, :, :high_rows])
        return [
            mul3(rows, (pair[0][v * high_rows : (v + 1) * high_rows], pair[1][v * high_rows : (v + 1) * high_rows]))
            for v in range(visits)
        ]

    lane = lax.broadcasted_iota(jnp.int32, (SLOTS, 2 * HALF), 1)
    line = lax.broadcasted_iota(jnp.int32, (SLOTS, 2 * HALF), 0)
    systems = []
    for pair in range(visits // 2):
        total = grams[0][pair * SLOTS : (pair + 1) * SLOTS]
        for ref in grams[1:]:
            total = total + ref[pair * SLOTS : (pair + 1) * SLOTS]
        diagonal = (lane == line) | (lane == line + HALF)
        systems.append(total + jnp.where(diagonal, RIDGE * total + RIDGE * EPS * normalizer, 0.0))
    pairs = range(visits // 2)
    tiles = [[matrix[8 * part : 8 * part + 8] for part in range(SLOTS // 8)] for matrix in systems]
    line, lane = line[:8], lane[:8]
    for panel in range(SLOTS // 8):
        if panel == 3:
            for copy in copies[:3]:
                copy.wait()
            noise = detected(inverse, 2)
        slots = [slot for slot in LIVE_SLOTS if slot // 8 == panel]
        place = {slot: jnp.where(lane < HALF, slot, HALF + slot) for slot in slots}
        columns = [
            {slot: [jnp.take_along_axis(tile, place[slot], axis=1) for tile in tiles[pair]] for slot in slots}
            for pair in pairs
        ]
        for number, slot in enumerate(slots):
            row = slot % 8
            at_row = line == row
            for pair in pairs:
                column = columns[pair][slot]
                scale = 1.0 / column[panel][row : row + 1]

                def eliminate(parts):
                    factor = parts[panel][row : row + 1] * scale
                    done = [part - column[index] * factor for index, part in enumerate(parts)]
                    done[panel] = jnp.where(at_row, factor, done[panel])
                    return done

                for later in slots[number + 1 :]:
                    columns[pair][later] = eliminate(columns[pair][later])
                tiles[pair] = eliminate(tiles[pair])
    for copy in copies[3:]:
        copy.wait()
    left = []
    offsets = []
    half_lane = lax.broadcasted_iota(jnp.int32, (BLOCK, 2 * HALF), 1) < HALF
    for pair in range(visits // 2):
        wanted = SCI_SLOT + 2 * pair
        place = jnp.where(lane < HALF, wanted, HALF + wanted + 1)
        solved = jnp.concatenate([jnp.take_along_axis(tile, place, axis=1) for tile in tiles[pair]], axis=0)
        mixes = [None] * TAP_COUNT
        for slot, (row_tap, col_tap) in SLOT_TAPS.items():
            term = solved[slot : slot + 1] * doubled_ref[row_tap]
            mixes[col_tap] = term if mixes[col_tap] is None else mixes[col_tap] + term
        own, other = [], []
        for tap in range(0, TAP_COUNT, 2):
            own.append(jnp.where(half_lane, mixes[tap], pltpu.roll(mixes[tap + 1], HALF, 1)))
            other.append(jnp.where(half_lane, pltpu.roll(mixes[tap], HALF, 1), mixes[tap + 1]))
        left += [jnp.concatenate(own, axis=1), jnp.concatenate(other, axis=1)]
        tail = solved[ONE_SLOT // 8 * 8 : ONE_SLOT // 8 * 8 + 8]
        for begin in (0, HALF):
            flat = jnp.take_along_axis(tail, jnp.full((8, LANES), begin, jnp.int32), axis=1)
            flat = flat[ONE_SLOT % 8 : ONE_SLOT % 8 + 1]
            offsets.append(jnp.concatenate([flat] * parts, axis=1))
    left = split(jnp.concatenate(left, axis=0))
    models = []
    for block in range(high_rows // BLOCK):
        start = block * BLOCK
        stack = tuple(
            jnp.concatenate([ref[tap, start : start + WINDOW] for tap in range(TAP_COUNT)], axis=0)
            for ref in (high_ref, low_ref)
        )
        models.append(mul3(left, stack))
    weighted = []
    for visit in range(visits):
        model = jnp.concatenate([part[visit * BLOCK : (visit + 1) * BLOCK] for part in models], axis=0)
        difference = wide_ref[visit] - model - offsets[visit]
        diff_ref[visit] = difference[EDGE : EDGE + row_count]
        results.append(pltpu.make_async_copy(diff_ref.at[visit], diff_out.at[visit, 0], out_sems.at[visit]))
        results[-1].start()
        weighted.append(difference * inverse[visit])
    signal = detected(weighted, 0)
    for visit in range(visits):
        sig_ref[visit] = signal[visit] * lax.rsqrt(noise[visit])
        results.append(pltpu.make_async_copy(sig_ref.at[visit], sig_out.at[visit, 0], out_sems.at[visits + visit]))
        results[-1].start()
    for copy in results:
        copy.wait()


def vmem():
    return pl.BlockSpec(memory_space=pltpu.VMEM)


def smem():
    return pl.BlockSpec(memory_space=pltpu.SMEM)


def far():
    return pl.BlockSpec(memory_space=pltpu.HBM)


def in_hbm(array):
    return pltpu.with_memory_space_constraint(jnp.asarray(array), pltpu.HBM)


def call(kernel, outs, out_specs, in_specs, scratch):
    return pl.pallas_call(
        kernel,
        out_shape=outs,
        in_specs=in_specs,
        out_specs=out_specs,
        scratch_shapes=scratch,
        compiler_params=pltpu.CompilerParams(vmem_limit_bytes=VMEM_BYTES),
    )


def after(array, others):
    return pl.pallas_call(
        lambda *refs: None,
        out_shape=[jax.ShapeDtypeStruct(array.shape, array.dtype)],
        in_specs=[far()] * (1 + len(others)),
        out_specs=[far()],
        input_output_aliases={0: 0},
        compiler_params=pltpu.CompilerParams(vmem_limit_bytes=1024 * 1024),
    )(array, *others)


def local(
    pieces_image,
    pieces_variance,
    piece_patch,
    piece_cell,
    stamp_row,
    stamp_col,
    stamp_count,
    warp_offsets,
):
    patches = lax.axis_size("patch")
    subtiles = lax.axis_size("sub")
    _, pieces, cell_rows, col_count = pieces_image.shape
    visits = warp_offsets.shape[0]
    row_count = cell_rows * NCELL
    slots = stamp_row.shape[1]
    capacity = max(2, 2 * pieces // patches)
    direct = patches <= 8
    units = 2 * capacity
    sds = jax.ShapeDtypeStruct
    design_fixed, filters, edges, doubled = constants(visits, row_count, col_count)

    image_blocks = patches if direct else 1
    var_blocks = 1

    def sent(blocks, depth):
        return [sds((1 if blocks > 1 else patches, depth, 8, LANES), F32)] * blocks

    *images, stamps, warps, chosen = call(
        functools.partial(pack_kernel, (patches, capacity, pieces, image_blocks, slots)),
        sent(image_blocks, units + 1)
        + [sds((8, LANES), F32), sds((visits,), jnp.int32), sds((patches * capacity,), jnp.int32)],
        [vmem()] * (image_blocks + 1) + [smem()] * 2,
        [far()] * 7,
        [
            pltpu.VMEM((-(-patches // 8) * 8, LANES), F32),
            pltpu.SMEM((patches,), jnp.int32),
            pltpu.SMEM((1, pieces), jnp.int32),
            pltpu.SMEM((1, pieces), jnp.int32),
            pltpu.VMEM((1, slots), jnp.int32),
            pltpu.VMEM((1, slots), jnp.int32),
            pltpu.SMEM((1, 1), jnp.int32),
            pltpu.VMEM(pieces_image.shape, F32),
            pltpu.SemaphoreType.DMA((7,)),
        ],
    )(
        in_hbm(piece_patch[:, :, 0]),
        in_hbm(piece_cell),
        in_hbm(stamp_row),
        in_hbm(stamp_col),
        stamp_count,
        in_hbm(pieces_image),
        in_hbm(warp_offsets),
    )

    def route(blocks):
        if len(blocks) == 1:
            return [lax.all_to_all(blocks[0], "patch", split_axis=0, concat_axis=0, tiled=True)]
        result = list(blocks[:1])
        for away, block in zip(turn(patches)[1:], blocks[1:]):
            result.append(lax.ppermute(block, "patch", [(i, i ^ away) for i in range(patches)]))
        return result

    got = route(images)
    variances = call(
        functools.partial(pack_more_kernel, (patches, capacity, var_blocks)),
        sent(var_blocks, units),
        [vmem()] * var_blocks,
        [smem(), far()],
        [pltpu.VMEM(pieces_image.shape, F32), pltpu.SemaphoreType.DMA((1,))],
    )(chosen, in_hbm(pieces_variance))
    if direct:
        variances = after(variances[0], got[1:])
    got_var = route(variances)

    side = sds((visits * HALO + 8, col_count), F32)
    science, to_near, to_far, cells = call(
        functools.partial(image_kernel, (patches, capacity, visits, row_count, col_count, image_blocks)),
        [sds((visits, row_count, col_count), F32), side, side, sds((patches * capacity,), jnp.int32)],
        [vmem(), vmem(), vmem(), smem()],
        [smem()] + [vmem()] * (1 + image_blocks),
        [
            pltpu.VMEM((visits * NCELL + 1, 2, 8, LANES), F32),
            pltpu.SMEM((patches, LANES), F32),
            pltpu.SemaphoreType.DMA((patches,)),
        ],
    )(warps, stamps, *got)
    beside = [(i, i ^ 3) for i in range(subtiles) if abs(i - (i ^ 3)) == 1]
    from_far = lax.ppermute(to_far, "sub", beside)
    from_near = lax.ppermute(to_near, "sub", [(i, i ^ 1) for i in range(subtiles)])

    field = sds((TAP_COUNT, row_count + 2 * BLOCK, col_count), BF16)
    plane = sds((row_count, col_count), F32)
    wide = sds((visits, row_count + 2 * EDGE, col_count), F32)
    held, hits = call(
        functools.partial(fetch_kernel, (row_count, col_count)),
        [sds(design_fixed.shape, BF16), plane],
        [vmem()] * 2,
        [vmem(), far()],
        [pltpu.SemaphoreType.DMA((design_fixed.shape[0],))],
    )(stamps, in_hbm(design_fixed))
    design, mask, high, low, wide_science = call(
        functools.partial(design_kernel, (visits, row_count, col_count)),
        [sds((row_count, BASIS, col_count), F32), plane] + [pltpu.HBM(part.shape, part.dtype) for part in (field, field, wide)],
        [vmem()] * 2 + [far()] * 3,
        [vmem()] * 5,
        [pltpu.VMEM(part.shape, part.dtype) for part in (field, field, wide)] + [pltpu.SemaphoreType.DMA((3,))],
    )(science, from_far, from_near, held, hits)

    gram_rows = visits // 2 * SLOTS
    tail_rows = visits * PR * (col_count // LANES)
    step = row_count
    gram_depth = 2 * visits * (BASIS + 4) + 3 * SLOTS + 16 - 2 * LANES
    variance, to_near, to_far, gram = call(
        functools.partial(gram_kernel, (patches, capacity, visits, row_count, col_count, var_blocks, step)),
        [
            sds((visits, row_count, col_count), F32),
            sds((gram_rows + tail_rows, LANES), F32),
            sds((gram_rows + tail_rows, LANES), F32),
            sds((gram_rows, LANES), F32),
        ],
        [vmem()] * 4,
        [smem(), smem()] + [vmem()] * (3 + var_blocks),
        [
            pltpu.VMEM((visits * NCELL + 1, 2, 8, LANES), F32),
            pltpu.VMEM((visits, row_count, col_count), F32),
            pltpu.VMEM((gram_depth, 2 * LANES), F32),
        ],
    )(warps, cells, mask, science, design, *got_var)
    grams = [gram]
    for away, part in ((3, to_far), (2, gram), (1, to_near)):
        grams.append(lax.ppermute(part, "sub", [(i, i ^ away) for i in range(subtiles)]))

    normalizer = subtiles * slots * (2 * SH + 1) ** 2
    result = sds((visits, 1, row_count, col_count), F32)
    kept = [filters, edges, doubled, wide_science, high, low]
    return call(
        functools.partial(solve_kernel, (visits, row_count, col_count, subtiles, float(normalizer), len(grams))),
        [result, result],
        [far(), far()],
        [vmem()] * (1 + len(grams)) + [far()] * len(kept),
        [pltpu.VMEM(wide.shape, F32)]
        + [pltpu.VMEM((visits, row_count, col_count), F32)] * 2
        + [pltpu.VMEM(part.shape, part.dtype) for part in kept]
        + [pltpu.SemaphoreType.DMA((len(kept),)), pltpu.SemaphoreType.DMA((2 * visits,))],
    )(variance, *grams, *[in_hbm(part) for part in kept])


def solution(mesh):
    in_specs = (
        P("sub", "patch", None, None),
        P("sub", "patch", None, None),
        P("sub", "patch", None),
        P("sub", "patch"),
        P("patch", "sub"),
        P("patch", "sub"),
        P("patch", "sub"),
        P(),
    )
    out_specs = (P(None, "patch", "sub", None), P(None, "patch", "sub", None))
    return jax.shard_map(local, mesh=mesh, in_specs=in_specs, out_specs=out_specs, check_vma=False)
```

```python
import functools

import jax
import jax.numpy as jnp
import ml_dtypes
import numpy as np
from jax import lax
from jax.experimental import pallas as pl
from jax.experimental.pallas import tpu as pltpu
from jax.sharding import PartitionSpec as P

NCELL = 8
KR = 10
PR = 10
SH = 15
WARP = 4

SIGMAS = (0.75, 1.5, 3.0)
DEGREES = (4, 4, 3)
PSF_SIGMA = 2.0
SKY_VAR = 0.1
RIDGE = 0.5
EPS = 1e-05

F32 = jnp.float32
BF16 = jnp.bfloat16
LANES = 128
HALO = 24
EDGE = 16
BLOCK = 32
WINDOW = 64
VMEM_BYTES = 20 * 1024 * 1024

TILES = (
    ((0, 0, range(5)), (0, 2, range(3))),
    ((0, 1, range(4)), (0, 3, range(2)), (0, 4, range(1)), (2, 2, range(1))),
    ((1, 0, range(5)), (1, 2, range(3))),
    ((1, 1, range(4)), (1, 3, range(2)), (1, 4, range(1)), (2, 2, range(1, 2))),
    ((2, 0, range(4)), (2, 1, range(3)), (2, 3, range(1))),
)
BASIS = 8 * len(TILES)
SLOTS = BASIS + 8
HALF = 64
TAP_FIRST = (0, DEGREES[0] + 1, DEGREES[0] + DEGREES[1] + 2)
TAP_COUNT = sum(DEGREES) + len(DEGREES)


def slot_table():
    result = {}
    for tile, entries in enumerate(TILES):
        taps = [(TAP_FIRST[group] + row, TAP_FIRST[group] + column) for group, column, rows in entries for row in rows]
        result.update({8 * tile + place: pair for place, pair in enumerate(taps)})
    return result


SLOT_TAPS = slot_table()
ONE_SLOT = BASIS
SCI_SLOT = ONE_SLOT + 1
LIVE_SLOTS = sorted(SLOT_TAPS) + [ONE_SLOT]


def basis_taps():
    offset = np.arange(-KR, KR + 1, dtype=np.float64)
    rows = []
    for spread, degree in zip(SIGMAS, DEGREES):
        scaled = offset / spread
        envelope = np.exp(-0.5 * scaled * scaled)
        previous, current = np.zeros_like(scaled), np.ones_like(scaled)
        for term_no in range(degree + 1):
            rows.append(current * envelope)
            previous, current = current, scaled * current - term_no * previous
    taps = np.stack(rows)
    return taps / np.sqrt(np.sum(taps * taps, axis=1, keepdims=True))


def psf_taps():
    offset = np.arange(-PR, PR + 1, dtype=np.float64)
    values = np.exp(-0.5 * (offset / PSF_SIGMA) ** 2)
    return values / values.sum()


def band(taps, rows, columns, shift):
    radius = (taps.shape[-1] - 1) // 2
    offset = np.arange(columns)[None, :] - shift - np.arange(rows)[:, None]
    inside = np.abs(offset) <= radius
    return np.where(inside, taps[..., np.clip(offset + radius, 0, 2 * radius)], 0.0)


def halves(values):
    values = np.asarray(values, np.float32)
    high = values.astype(ml_dtypes.bfloat16)
    low = (values - high.astype(np.float32)).astype(ml_dtypes.bfloat16)
    return high, low


@functools.lru_cache(maxsize=None)
def constants(visits, row_count, col_count):
    taps = basis_taps()
    column_bands = np.stack([band(taps[t], col_count, col_count, 0).T for t in range(TAP_COUNT)])
    toeplitz = np.stack([band(taps[t], BLOCK, WINDOW, EDGE) for t in range(TAP_COUNT)])
    row_parts = []
    for entries in TILES:
        matrix = np.zeros((BLOCK, 8, len(entries) * WINDOW))
        slot = 0
        for place, (group, _, rows) in enumerate(entries):
            for row in rows:
                matrix[:, slot, place * WINDOW : (place + 1) * WINDOW] = toeplitz[TAP_FIRST[group] + row]
                slot += 1
        row_parts.append(matrix.reshape(BLOCK * 8, -1))
    depth = col_count
    for tile, part in enumerate(row_parts):
        row_parts[tile] = np.pad(part, ((0, 0), (0, depth - part.shape[1])))
    design = np.stack(halves(np.concatenate([column_bands, np.stack(row_parts)])), axis=1)
    psf = psf_taps()
    filters = np.stack([half for power in (1, 2) for half in halves(band(psf**power, col_count, col_count, 0).T)])
    edges = np.stack(
        [half for power in (1, 2) for half in halves(band(psf**power, row_count, row_count + 2 * EDGE, EDGE))]
    )
    edges = np.pad(edges, ((0, 0), (0, 0), (0, -edges.shape[2] % LANES)))
    doubled = np.concatenate([toeplitz, toeplitz], axis=2).astype(np.float32)
    return design, filters, edges, doubled


def split(values):
    high = values.astype(BF16)
    return high, (values - high.astype(F32)).astype(BF16)


def mul(left, right):
    return jnp.dot(left, right, preferred_element_type=F32)


def mul3(left, right):
    return mul(left[0], right[0]) + mul(left[0], right[1]) + mul(left[1], right[0])


def mul_nt(left, right):
    return lax.dot_general(left, right, (((1,), (1,)), ((), ())), preferred_element_type=F32)


def turn(patches):
    half = patches // 2
    return [0, *(away for step in range(half) for away in (half + step, step + 1))][:patches]


def fill(cfg, outs, source, chosen_ref, table_ref):
    patches, capacity = cfg
    me = lax.axis_index("patch")
    for block in range(patches):
        if len(outs) == 1:
            out, place, away = outs[0], block, block ^ me
        else:
            out, place, away = outs[block], 0, turn(patches)[block]
        for rank in range(capacity):
            piece = chosen_ref[away * capacity + rank]
            out[place, 2 * rank] = source[0, piece, :, :LANES]
            out[place, 2 * rank + 1] = source[0, piece, :, LANES:]
        if table_ref is not None:
            out[place, 2 * capacity] = jnp.broadcast_to(table_ref[pl.ds(away, 1), :], (8, LANES))


def start_copies(pairs, sems):
    copies = [pltpu.make_async_copy(source, place, sems.at[number]) for number, (source, place) in enumerate(pairs)]
    for copy in copies:
        copy.start()
    return copies


def pack_kernel(cfg, *refs):
    patches, capacity, pieces, blocks, slots = cfg
    sources, refs = refs[:7], refs[7:]
    outs, refs = refs[:blocks], refs[blocks:]
    stamp_out, warp_out, chosen_ref, table_ref, count_ref, *held = refs
    held, sems = held[:-1], held[-1]
    target_ref, cell_ref, row_ref, col_ref, live_ref, image_ref = held
    copies = start_copies(
        zip(sources, (target_ref, cell_ref, row_ref, col_ref, live_ref, image_ref, warp_out)), sems
    )
    me = lax.axis_index("patch")
    for entry in range(patches * capacity):
        chosen_ref[entry] = 0
    for entry in range(patches):
        count_ref[entry] = 0
    line = lax.broadcasted_iota(jnp.int32, table_ref.shape, 0)
    lane = lax.broadcasted_iota(jnp.int32, table_ref.shape, 1)
    copies[0].wait()
    copies[1].wait()
    table = jnp.full(table_ref.shape, -1.0, F32)
    for piece in range(pieces):
        away = target_ref[0, piece] ^ me
        rank = count_ref[away]
        count_ref[away] = rank + 1
        chosen_ref[away * capacity + rank] = piece
        value = cell_ref[0, piece].astype(F32)
        table = jnp.where((line == away) & (lane == rank), value, table)
    table_ref[...] = table
    for copy in copies[2:5]:
        copy.wait()
    live = lax.broadcasted_iota(jnp.int32, (1, slots), 1) < live_ref[0, 0]
    stamp_out[...] = jnp.zeros(stamp_out.shape, F32)
    stamp_out[0:1, :slots] = row_ref[...].astype(F32)
    stamp_out[1:2, :slots] = col_ref[...].astype(F32)
    stamp_out[2:3, :slots] = jnp.where(live, 1.0, 0.0)
    copies[5].wait()
    fill((patches, capacity), outs, image_ref, chosen_ref, table_ref)
    copies[6].wait()


def pack_more_kernel(cfg, chosen_ref, var_hbm, *refs):
    patches, capacity, blocks = cfg
    outs, (var_ref, sems) = refs[:blocks], refs[blocks:]
    (copy,) = start_copies([(var_hbm, var_ref)], sems)
    copy.wait()
    fill((patches, capacity), outs, var_ref, chosen_ref, None)


def assemble(cfg, blocks, cells_ref, total_ref, me):
    patches, capacity = cfg
    total_ref[...] = jnp.zeros(total_ref.shape, F32)
    for block in range(patches):
        if len(blocks) == 1:
            ref, place, away = blocks[0], block, block ^ me
        else:
            ref, place, away = blocks[block], 0, turn(patches)[block]
        for rank in range(capacity):
            cell = cells_ref[away * capacity + rank]
            total_ref[cell, 0] += ref[place, 2 * rank]
            total_ref[cell, 1] += ref[place, 2 * rank + 1]


def warped(total_ref, visit, warp_ref, row_count, col_count):
    first = visit * NCELL
    left = total_ref[first : first + NCELL, 0].reshape(row_count, LANES)
    right = total_ref[first : first + NCELL, 1].reshape(row_count, LANES)
    plane = jnp.concatenate([left, right], axis=1)
    offset = warp_ref[visit] - WARP
    moved = pltpu.roll(plane, lax.rem(col_count - offset, col_count), 1)
    source = lax.broadcasted_iota(jnp.int32, plane.shape, 1) + offset
    return jnp.where((source >= 0) & (source < col_count), moved, 0.0)


def image_kernel(cfg, warp_ref, stamp_ref, *refs):
    patches, capacity, visits, row_count, col_count, block_count = cfg
    blocks = refs[:block_count]
    sci_ref, near_out, far_out, cells_ref, total_ref, near_ref, sems = refs[block_count:]
    me = lax.axis_index("patch")
    odd = lax.axis_index("sub") % 2 == 1
    copies = []
    for block in range(patches):
        ref, place = (blocks[0], block) if block_count == 1 else (blocks[block], 0)
        copies.append(
            pltpu.make_async_copy(
                ref.at[place, 2 * capacity, pl.ds(0, 1), :], near_ref.at[pl.ds(block, 1), :], sems.at[block]
            )
        )
    for copy in copies:
        copy.start()
    for copy in copies:
        copy.wait()
    for block in range(patches):
        away = block ^ me if block_count == 1 else turn(patches)[block]
        for rank in range(capacity):
            cell = near_ref[block, rank].astype(jnp.int32)
            cells_ref[away * capacity + rank] = jnp.where(cell < 0, visits * NCELL, cell)
    assemble((patches, capacity), blocks, cells_ref, total_ref, me)
    for visit in range(visits):
        plane = warped(total_ref, visit, warp_ref, row_count, col_count)
        sci_ref[visit] = plane
        top, bottom = plane[:HALO], plane[row_count - HALO :]
        near_out[visit * HALO : (visit + 1) * HALO] = jnp.where(odd, top, bottom)
        far_out[visit * HALO : (visit + 1) * HALO] = jnp.where(odd, bottom, top)
    first = visits * HALO
    for ref in (near_out, far_out):
        ref[first : first + 8, :LANES] = stamp_ref[...]
        ref[first : first + 8, LANES:] = jnp.zeros((8, col_count - LANES), F32)


def near_mask(stamps, shift, row_count, col_count):
    row_at = lax.broadcasted_iota(jnp.int32, (row_count, LANES), 0).astype(F32)
    col_at = lax.broadcasted_iota(jnp.int32, (col_count, LANES), 0).astype(F32)
    row_in = (jnp.abs(row_at - (stamps[0:1] + shift)) <= SH) & (stamps[2:3] > 0.5)
    col_in = jnp.abs(col_at - stamps[1:2]) <= SH
    return mul_nt(jnp.where(row_in, 1.0, 0.0).astype(BF16), jnp.where(col_in, 1.0, 0.0).astype(BF16))


def filter_columns(image, tap, held_ref):
    rows = image[0].shape[0]
    both = mul(jnp.concatenate(image, axis=0), held_ref[tap, 0])
    return split(both[:rows] + both[rows:] + mul(image[0], held_ref[tap, 1]))


def fetch_kernel(cfg, stamp_ref, fixed_ref, held_ref, hits_ref, sems):
    row_count, col_count = cfg
    copies = start_copies([(fixed_ref.at[n], held_ref.at[n]) for n in range(TAP_COUNT + len(TILES))], sems)
    hits_ref[...] = near_mask(stamp_ref[...], 0.0, row_count, col_count)
    for copy in copies:
        copy.wait()


def design_kernel(cfg, sci_ref, far_ref, near_ref, held_ref, hits_ref, *refs):
    visits, row_count, col_count = cfg
    design_ref, mask_ref, high_out, low_out, wide_out, high_ref, low_ref, wide_ref, sems = refs
    odd = lax.axis_index("sub") % 2 == 1

    def beside(first, count, lanes=slice(None)):
        near, far = near_ref[first : first + count, lanes], far_ref[first : first + count, lanes]
        return jnp.where(odd, near, far), jnp.where(odd, far, near)

    above, below = beside(0, HALO)
    own = sci_ref[0]
    for visit in range(1, visits):
        more = beside(visit * HALO, HALO)
        above, own, below = above + more[0], own + sci_ref[visit], below + more[1]
    rim = jnp.zeros((BLOCK - HALO, col_count), F32)
    template = split(jnp.concatenate([rim, above, own, below, rim], axis=0) * (1.0 / visits))
    for tap in range(TAP_COUNT):
        high_ref[tap], low_ref[tap] = filter_columns(template, tap, held_ref)
    for visit in range(visits):
        first = visit * HALO
        wide_ref[visit, :EDGE] = beside(first + HALO - EDGE, EDGE)[0]
        wide_ref[visit, EDGE : EDGE + row_count] = sci_ref[visit]
        wide_ref[visit, EDGE + row_count :] = beside(first, EDGE)[1]
    copies = start_copies(((high_ref, high_out), (low_ref, low_out), (wide_ref, wide_out)), sems)
    for block in range(row_count // BLOCK):
        start = EDGE + block * BLOCK
        for tile, entries in enumerate(TILES):
            rows = [held_ref[TAP_COUNT + tile, half, :, : len(entries) * WINDOW] for half in range(2)]
            taps = [TAP_FIRST[group] + column for group, column, _ in entries]
            high = [high_ref[tap, start : start + WINDOW] for tap in taps]
            low = [low_ref[tap, start : start + WINDOW] for tap in taps]
            both = mul(jnp.concatenate(rows, axis=0), jnp.concatenate(high, axis=0))
            part = both[: 8 * BLOCK] + both[8 * BLOCK :] + mul(rows[0], jnp.concatenate(low, axis=0))
            design_ref[block * BLOCK : (block + 1) * BLOCK, 8 * tile : 8 * tile + 8] = part.reshape(
                BLOCK, 8, col_count
            )
    first = visits * HALO
    hits = hits_ref[...]
    for stamps, shift in zip(beside(first, 8, slice(LANES)), (-row_count, row_count)):
        hits = hits + near_mask(stamps, float(shift), row_count, col_count)
    mask_ref[...] = jnp.minimum(hits, 1.0)
    for copy in copies:
        copy.wait()


def gram_kernel(cfg, warp_ref, cells_ref, mask_ref, sci_ref, design_ref, *refs):
    patches, capacity, visits, row_count, col_count, block_count = cfg
    blocks = refs[:block_count]
    var_ref, near_ref, far_ref, gram_ref, total_ref, weight_ref, sum_ref = refs[block_count:]
    me = lax.axis_index("patch")
    odd = lax.axis_index("sub") % 2 == 1
    assemble((patches, capacity), blocks, cells_ref, total_ref, me)
    shared = jnp.full((row_count, col_count), SKY_VAR, F32)
    for visit in range(visits):
        plane = warped(total_ref, visit, warp_ref, row_count, col_count)
        var_ref[visit] = plane
        shared = shared + plane * (1.0 / (visits * visits))
    mask = mask_ref[...]
    for visit in range(visits):
        weight_ref[visit] = mask / (var_ref[visit] + shared)

    rows = visits * BASIS + visits // 2 * 8
    kept = 2 * LANES - 2 * SLOTS - 16
    line = lax.broadcasted_iota(jnp.int32, (8, col_count), 0)

    left, right = [], []
    for row in range(row_count):
        design = design_ref[row]
        last = jnp.ones((8, col_count), F32)
        for visit in range(visits):
            last = jnp.where(line == SCI_SLOT - BASIS + visit, sci_ref[visit, pl.ds(row, 1), :], last)
        high, low = split(jnp.concatenate([design, last], axis=0))
        weights = [weight_ref[visit, pl.ds(row, 1), :] for visit in range(visits)]
        scaled = [design * weight for weight in weights]
        for pair in range(visits // 2):
            scaled.append(jnp.where(line == 0, weights[2 * pair], weights[2 * pair + 1]))
        scaled_high, scaled_low = split(jnp.concatenate(scaled, axis=0))
        blank = jnp.zeros((16, col_count), BF16)
        right.append(jnp.concatenate([high, low, scaled_low[:kept], blank], axis=0))
        left.append(jnp.concatenate([scaled_high, high, scaled_low[kept:]], axis=0))
    sum_ref[...] = mul_nt(jnp.concatenate(left, axis=1), jnp.concatenate(right, axis=1))
    depth = sum_ref.shape[0]
    main = sum_ref[:rows, :LANES]
    turned = jnp.transpose(sum_ref[depth - LANES :, :])[2 * SLOTS : 2 * SLOTS + kept]
    turned = pltpu.roll(turned, depth - rows, 1)
    main = main + pltpu.roll(main, LANES - SLOTS, 1)
    main = main + jnp.concatenate([turned, sum_ref[rows + SLOTS :, :LANES]], axis=0)
    lane = lax.broadcasted_iota(jnp.int32, (SLOTS, 2 * HALF), 1)
    for pair in range(visits // 2):
        ends = main[visits * BASIS + 8 * pair :][:8]
        both = []
        for visit, end in ((2 * pair, ends), (2 * pair + 1, pltpu.roll(ends, 7, 0))):
            both.append(jnp.concatenate([main[visit * BASIS : (visit + 1) * BASIS], end], axis=0))
        value = jnp.where(lane < HALF, both[0], pltpu.roll(both[1], HALF, 1))
        for ref in (gram_ref, near_ref, far_ref):
            ref[pair * SLOTS : (pair + 1) * SLOTS] = value
    first = visits // 2 * SLOTS
    for visit in range(visits):
        for part in range(col_count // LANES):
            place = first + (visit * (col_count // LANES) + part) * PR
            lanes = slice(part * LANES, (part + 1) * LANES)
            top, bottom = var_ref[visit, :PR, lanes], var_ref[visit, row_count - PR :, lanes]
            near_ref[place : place + PR] = jnp.where(odd, top, bottom)
            far_ref[place : place + PR] = jnp.where(odd, bottom, top)


def solve_kernel(cfg, var_ref, *refs):
    visits, row_count, col_count, subtiles, normalizer, gram_count = cfg
    grams = refs[:gram_count]
    fixed = refs[gram_count : gram_count + 6]
    diff_out, sig_out, spread_ref, diff_ref, sig_ref, *held, sems, out_sems = refs[gram_count + 6 :]
    copies = start_copies(zip(fixed, held), sems)
    results = []
    filter_ref, edge_ref, doubled_ref, wide_ref, high_ref, low_ref = held
    sub = lax.axis_index("sub")
    high_rows = row_count + 2 * EDGE
    parts = col_count // LANES
    first = visits // 2 * SLOTS

    from_far, from_near = grams[1], grams[3]
    odd = sub % 2 == 1
    for visit in range(visits):
        spread_ref[visit, :EDGE] = jnp.zeros((EDGE, col_count), F32)
        spread_ref[visit, EDGE + row_count :] = jnp.zeros((EDGE, col_count), F32)
        spread_ref[visit, EDGE : EDGE + row_count] = var_ref[visit]
        for part in range(parts):
            place = first + (visit * parts + part) * PR
            lanes = slice(part * LANES, (part + 1) * LANES)
            near, far = from_near[place : place + PR], from_far[place : place + PR]
            spread_ref[visit, EDGE - PR : EDGE, lanes] = jnp.where(odd, near, far)
            spread_ref[visit, EDGE + row_count : EDGE + row_count + PR, lanes] = jnp.where(odd, far, near)
    row_at = lax.broadcasted_iota(jnp.int32, (high_rows, col_count), 0) + sub * row_count - EDGE
    inside = (row_at >= 0) & (row_at < subtiles * row_count)
    spread = [spread_ref[visit] for visit in range(visits)]
    shared = jnp.full((high_rows, col_count), SKY_VAR, F32)
    for visit in range(visits):
        shared = shared + spread[visit] * (1.0 / (visits * visits))
    inverse = [jnp.where(inside, 1.0 / (spread[visit] + shared), 0.0) for visit in range(visits)]

    def detected(images, kind):
        filtered = mul3(split(jnp.concatenate(images, axis=0)), (filter_ref[kind], filter_ref[kind + 1]))
        pair = split(filtered)
        rows = (edge_ref[kind, :, :high_rows], edge_ref[kind + 1, :, :high_rows])
        return [
            mul3(rows, (pair[0][v * high_rows : (v + 1) * high_rows], pair[1][v * high_rows : (v + 1) * high_rows]))
            for v in range(visits)
        ]

    lane = lax.broadcasted_iota(jnp.int32, (SLOTS, 2 * HALF), 1)
    line = lax.broadcasted_iota(jnp.int32, (SLOTS, 2 * HALF), 0)
    systems = []
    for pair in range(visits // 2):
        total = grams[0][pair * SLOTS : (pair + 1) * SLOTS]
        for ref in grams[1:]:
            total = total + ref[pair * SLOTS : (pair + 1) * SLOTS]
        diagonal = (lane == line) | (lane == line + HALF)
        systems.append(total + jnp.where(diagonal, RIDGE * total + RIDGE * EPS * normalizer, 0.0))
    pairs = range(visits // 2)
    tiles = [[matrix[8 * part : 8 * part + 8] for part in range(SLOTS // 8)] for matrix in systems]
    line, lane = line[:8], lane[:8]
    for panel in range(SLOTS // 8):
        if panel == 3:
            for copy in copies[:3]:
                copy.wait()
            noise = detected(inverse, 2)
        slots = [slot for slot in LIVE_SLOTS if slot // 8 == panel]
        place = {slot: jnp.where(lane < HALF, slot, HALF + slot) for slot in slots}
        columns = [
            {slot: [jnp.take_along_axis(tile, place[slot], axis=1) for tile in tiles[pair]] for slot in slots}
            for pair in pairs
        ]
        for number, slot in enumerate(slots):
            row = slot % 8
            at_row = line == row
            for pair in pairs:
                column = columns[pair][slot]
                scale = 1.0 / column[panel][row : row + 1]

                def eliminate(parts):
                    factor = parts[panel][row : row + 1] * scale
                    done = [part - column[index] * factor for index, part in enumerate(parts)]
                    done[panel] = jnp.where(at_row, factor, done[panel])
                    return done

                for later in slots[number + 1 :]:
                    columns[pair][later] = eliminate(columns[pair][later])
                tiles[pair] = eliminate(tiles[pair])
    for copy in copies[3:]:
        copy.wait()
    left = []
    offsets = []
    half_lane = lax.broadcasted_iota(jnp.int32, (BLOCK, 2 * HALF), 1) < HALF
    for pair in range(visits // 2):
        wanted = SCI_SLOT + 2 * pair
        place = jnp.where(lane < HALF, wanted, HALF + wanted + 1)
        solved = jnp.concatenate([jnp.take_along_axis(tile, place, axis=1) for tile in tiles[pair]], axis=0)
        mixes = [None] * TAP_COUNT
        for slot, (row_tap, col_tap) in SLOT_TAPS.items():
            term = solved[slot : slot + 1] * doubled_ref[row_tap]
            mixes[col_tap] = term if mixes[col_tap] is None else mixes[col_tap] + term
        own, other = [], []
        for tap in range(0, TAP_COUNT, 2):
            own.append(jnp.where(half_lane, mixes[tap], pltpu.roll(mixes[tap + 1], HALF, 1)))
            other.append(jnp.where(half_lane, pltpu.roll(mixes[tap], HALF, 1), mixes[tap + 1]))
        left += [jnp.concatenate(own, axis=1), jnp.concatenate(other, axis=1)]
        tail = solved[ONE_SLOT // 8 * 8 : ONE_SLOT // 8 * 8 + 8]
        for begin in (0, HALF):
            flat = jnp.take_along_axis(tail, jnp.full((8, LANES), begin, jnp.int32), axis=1)
            flat = flat[ONE_SLOT % 8 : ONE_SLOT % 8 + 1]
            offsets.append(jnp.concatenate([flat] * parts, axis=1))
    left = split(jnp.concatenate(left, axis=0))
    models = []
    for block in range(high_rows // BLOCK):
        start = block * BLOCK
        stack = tuple(
            jnp.concatenate([ref[tap, start : start + WINDOW] for tap in range(TAP_COUNT)], axis=0)
            for ref in (high_ref, low_ref)
        )
        models.append(mul3(left, stack))
    weighted = []
    for visit in range(visits):
        model = jnp.concatenate([part[visit * BLOCK : (visit + 1) * BLOCK] for part in models], axis=0)
        difference = wide_ref[visit] - model - offsets[visit]
        diff_ref[visit] = difference[EDGE : EDGE + row_count]
        results.append(pltpu.make_async_copy(diff_ref.at[visit], diff_out.at[visit, 0], out_sems.at[visit]))
        results[-1].start()
        weighted.append(difference * inverse[visit])
    signal = detected(weighted, 0)
    for visit in range(visits):
        sig_ref[visit] = signal[visit] * lax.rsqrt(noise[visit])
        results.append(pltpu.make_async_copy(sig_ref.at[visit], sig_out.at[visit, 0], out_sems.at[visits + visit]))
        results[-1].start()
    for copy in results:
        copy.wait()


def vmem():
    return pl.BlockSpec(memory_space=pltpu.VMEM)


def smem():
    return pl.BlockSpec(memory_space=pltpu.SMEM)


def far():
    return pl.BlockSpec(memory_space=pltpu.HBM)


def in_hbm(array):
    return pltpu.with_memory_space_constraint(jnp.asarray(array), pltpu.HBM)


def call(kernel, outs, out_specs, in_specs, scratch):
    return pl.pallas_call(
        kernel,
        out_shape=outs,
        in_specs=in_specs,
        out_specs=out_specs,
        scratch_shapes=scratch,
        compiler_params=pltpu.CompilerParams(vmem_limit_bytes=VMEM_BYTES),
    )


def after(array, others):
    return pl.pallas_call(
        lambda *refs: None,
        out_shape=[jax.ShapeDtypeStruct(array.shape, array.dtype)],
        in_specs=[far()] * (1 + len(others)),
        out_specs=[far()],
        input_output_aliases={0: 0},
        compiler_params=pltpu.CompilerParams(vmem_limit_bytes=1024 * 1024),
    )(array, *others)


def local(
    pieces_image,
    pieces_variance,
    piece_patch,
    piece_cell,
    stamp_row,
    stamp_col,
    stamp_count,
    warp_offsets,
):
    patches = lax.axis_size("patch")
    subtiles = lax.axis_size("sub")
    _, pieces, cell_rows, col_count = pieces_image.shape
    visits = warp_offsets.shape[0]
    row_count = cell_rows * NCELL
    slots = stamp_row.shape[1]
    capacity = max(2, 2 * pieces // patches)
    direct = patches <= 8
    units = 2 * capacity
    sds = jax.ShapeDtypeStruct
    design_fixed, filters, edges, doubled = constants(visits, row_count, col_count)

    image_blocks = patches if direct else 1
    var_blocks = 1

    def sent(blocks, depth):
        return [sds((1 if blocks > 1 else patches, depth, 8, LANES), F32)] * blocks

    *images, stamps, warps, chosen = call(
        functools.partial(pack_kernel, (patches, capacity, pieces, image_blocks, slots)),
        sent(image_blocks, units + 1)
        + [sds((8, LANES), F32), sds((visits,), jnp.int32), sds((patches * capacity,), jnp.int32)],
        [vmem()] * (image_blocks + 1) + [smem()] * 2,
        [far()] * 7,
        [
            pltpu.VMEM((-(-patches // 8) * 8, LANES), F32),
            pltpu.SMEM((patches,), jnp.int32),
            pltpu.SMEM((1, pieces), jnp.int32),
            pltpu.SMEM((1, pieces), jnp.int32),
            pltpu.VMEM((1, slots), jnp.int32),
            pltpu.VMEM((1, slots), jnp.int32),
            pltpu.SMEM((1, 1), jnp.int32),
            pltpu.VMEM(pieces_image.shape, F32),
            pltpu.SemaphoreType.DMA((7,)),
        ],
    )(
        in_hbm(piece_patch[:, :, 0]),
        in_hbm(piece_cell),
        in_hbm(stamp_row),
        in_hbm(stamp_col),
        stamp_count,
        in_hbm(pieces_image),
        in_hbm(warp_offsets),
    )

    def route(blocks):
        if len(blocks) == 1:
            return [lax.all_to_all(blocks[0], "patch", split_axis=0, concat_axis=0, tiled=True)]
        result = list(blocks[:1])
        for away, block in zip(turn(patches)[1:], blocks[1:]):
            result.append(lax.ppermute(block, "patch", [(i, i ^ away) for i in range(patches)]))
        return result

    got = route(images)
    variances = call(
        functools.partial(pack_more_kernel, (patches, capacity, var_blocks)),
        sent(var_blocks, units),
        [vmem()] * var_blocks,
        [smem(), far()],
        [pltpu.VMEM(pieces_image.shape, F32), pltpu.SemaphoreType.DMA((1,))],
    )(chosen, in_hbm(pieces_variance))
    if direct:
        variances = after(variances[0], got[1:])
    got_var = route(variances)

    side = sds((visits * HALO + 8, col_count), F32)
    science, to_near, to_far, cells = call(
        functools.partial(image_kernel, (patches, capacity, visits, row_count, col_count, image_blocks)),
        [sds((visits, row_count, col_count), F32), side, side, sds((patches * capacity,), jnp.int32)],
        [vmem(), vmem(), vmem(), smem()],
        [smem()] + [vmem()] * (1 + image_blocks),
        [
            pltpu.VMEM((visits * NCELL + 1, 2, 8, LANES), F32),
            pltpu.SMEM((patches, LANES), F32),
            pltpu.SemaphoreType.DMA((patches,)),
        ],
    )(warps, stamps, *got)
    beside = [(i, i ^ 3) for i in range(subtiles) if abs(i - (i ^ 3)) == 1]
    from_far = lax.ppermute(to_far, "sub", beside)
    from_near = lax.ppermute(to_near, "sub", [(i, i ^ 1) for i in range(subtiles)])

    field = sds((TAP_COUNT, row_count + 2 * BLOCK, col_count), BF16)
    plane = sds((row_count, col_count), F32)
    wide = sds((visits, row_count + 2 * EDGE, col_count), F32)
    held, hits = call(
        functools.partial(fetch_kernel, (row_count, col_count)),
        [sds(design_fixed.shape, BF16), plane],
        [vmem()] * 2,
        [vmem(), far()],
        [pltpu.SemaphoreType.DMA((design_fixed.shape[0],))],
    )(stamps, in_hbm(design_fixed))
    design, mask, high, low, wide_science = call(
        functools.partial(design_kernel, (visits, row_count, col_count)),
        [sds((row_count, BASIS, col_count), F32), plane] + [pltpu.HBM(part.shape, part.dtype) for part in (field, field, wide)],
        [vmem()] * 2 + [far()] * 3,
        [vmem()] * 5,
        [pltpu.VMEM(part.shape, part.dtype) for part in (field, field, wide)] + [pltpu.SemaphoreType.DMA((3,))],
    )(science, from_far, from_near, held, hits)

    gram_rows = visits // 2 * SLOTS
    tail_rows = visits * PR * (col_count // LANES)
    gram_depth = 2 * visits * (BASIS + 4) + 3 * SLOTS + 16 - 2 * LANES
    variance, to_near, to_far, gram = call(
        functools.partial(gram_kernel, (patches, capacity, visits, row_count, col_count, var_blocks)),
        [
            sds((visits, row_count, col_count), F32),
            sds((gram_rows + tail_rows, LANES), F32),
            sds((gram_rows + tail_rows, LANES), F32),
            sds((gram_rows, LANES), F32),
        ],
        [vmem()] * 4,
        [smem(), smem()] + [vmem()] * (3 + var_blocks),
        [
            pltpu.VMEM((visits * NCELL + 1, 2, 8, LANES), F32),
            pltpu.VMEM((visits, row_count, col_count), F32),
            pltpu.VMEM((gram_depth, 2 * LANES), F32),
        ],
    )(warps, cells, mask, science, design, *got_var)
    grams = [gram]
    for away, part in ((3, to_far), (2, gram), (1, to_near)):
        grams.append(lax.ppermute(part, "sub", [(i, i ^ away) for i in range(subtiles)]))

    normalizer = subtiles * slots * (2 * SH + 1) ** 2
    result = sds((visits, 1, row_count, col_count), F32)
    kept = [filters, edges, doubled, wide_science, high, low]
    return call(
        functools.partial(solve_kernel, (visits, row_count, col_count, subtiles, float(normalizer), len(grams))),
        [result, result],
        [far(), far()],
        [vmem()] * (1 + len(grams)) + [far()] * len(kept),
        [pltpu.VMEM(wide.shape, F32)]
        + [pltpu.VMEM((visits, row_count, col_count), F32)] * 2
        + [pltpu.VMEM(part.shape, part.dtype) for part in kept]
        + [pltpu.SemaphoreType.DMA((len(kept),)), pltpu.SemaphoreType.DMA((2 * visits,))],
    )(variance, *grams, *[in_hbm(part) for part in kept])


def solution(mesh):
    in_specs = (
        P("sub", "patch", None, None),
        P("sub", "patch", None, None),
        P("sub", "patch", None),
        P("sub", "patch"),
        P("patch", "sub"),
        P("patch", "sub"),
        P("patch", "sub"),
        P(),
    )
    out_specs = (P(None, "patch", "sub", None), P(None, "patch", "sub", None))
    return jax.shard_map(local, mesh=mesh, in_specs=in_specs, out_specs=out_specs, check_vma=False)
```
